32 devices in a mesh: dp: 4 (over z), tensor: 8 (over y, x, core).
Axes of the slice: x: 2, y: 2, z: 4, core: 2. Of those that a mesh axis runs over, the one named last changes fastest.
Arguments:
- inputs: bfloat16 [8, 2048, 2048], P('dp', 'tensor'), may hold values from -6 to 6
- cotangent: bfloat16 [8, 2048, 2048], P('dp', 'tensor'), may hold values from -6 to 6
- documents: int32 [8, 2048], P('dp'), may hold values from 0 to 7, as said below
- padding: int32 [8, 2048], P('dp'), may hold values from 0 to 1, as said below
- attn_gain: float32 [2048], replicated, may hold values from 0.5 to 1.5
- attn_shift: float32 [2048], replicated, may hold values from -1.75 to 1.75
- query_matrix: bfloat16 [2048, 2048], P(None, 'tensor'), may hold values from -0.25 to 0.25
- query_bias: float32 [2048], P('tensor'), may hold values from -1.75 to 1.75
- shared_matrix: bfloat16 [2048, 256], replicated, may hold values from -0.125 to 0.125
- value_bias: float32 [128], replicated, may hold values from -1.75 to 1.75
- output_matrix: bfloat16 [2048, 2048], P('tensor'), may hold values from -0.5 to 0.5
- output_bias: float32 [2048], replicated, may hold values from -1.75 to 1.75
- mlp_gain: float32 [2048], replicated, may hold values from 0.5 to 1.5
- mlp_shift: float32 [2048], replicated, may hold values from -1.75 to 1.75
- expansion_weights: bfloat16 [2048, 8192], P(None, 'tensor'), may hold values from -0.125 to 0.125
- up_bias: float32 [8192], P('tensor'), may hold values from -1.75 to 1.75
- down_matrix: bfloat16 [8192, 2048], P('tensor'), may hold values from -0.0625 to 0.0625
- down_bias: float32 [2048], replicated, may hold values from -1.75 to 1.75
Outputs:
- block_out: bfloat16 [8, 2048, 2048], P('dp', 'tensor')
- input_grad: float32 [8, 2048, 2048], P('dp', 'tensor')
- focus_scale_derivative: float32 [2048], replicated
- focus_offset_derivative: float32 [2048], replicated
- query_weight_grad: float32 [2048, 2048], P(None, 'tensor')
- query_bias_grad: float32 [2048], P('tensor')
- shared_weight_grad: float32 [2048, 256], replicated
- value_bias_grad: float32 [128], replicated
- output_weight_grad: float32 [2048, 2048], P('tensor')
- output_bias_grad: float32 [2048], replicated
- mlp_gain_grad: float32 [2048], replicated
- mlp_shift_grad: float32 [2048], replicated
- up_weight_grad: float32 [2048, 8192], P(None, 'tensor')
- up_bias_grad: float32 [8192], P('tensor')
- down_weight_grad: float32 [8192, 2048], P('tensor')
- down_bias_grad: float32 [2048], replicated
The draws below stay inside these ranges and needn't reach their ends.
Inputs may be any that keep to these rules, and one draw needn't show every extreme that they name: Along each row the ids start at 0 and never fall, rising by at most one from a position to the next; in each group of 2 consecutive rows one row, drawn from the seed, is a single document, and every other row holds exactly 8 documents. Each row is real on a leading run of at least 1792 positions and padded after it; the single-document row of each group has no padding.
All inputs are finite; a program needn't handle non-finite values.
Results may differ from the reference program's by a relative error of at most 0.015.
Values may be sent and summed in bfloat16 or wider, within the bound.
A program may use at most 384 MiB of HBM per device.

```python
import jax
import jax.numpy as jnp
from jax import lax

D = 2048
HEADS = 16
HD = 128
FF = 8192
LEN = 2048
SEQS = 2
QW = 2048
ROWS = 8


def whole_rows(key):
    chosen = jax.random.randint(jax.random.fold_in(key, 91), (ROWS // SEQS,), 0, SEQS)
    row_index = jnp.arange(ROWS, dtype=jnp.int32)
    return row_index % SEQS == chosen[row_index // SEQS]


def draw_documents(key, part):
    single = whole_rows(key)
    key = jax.random.fold_in(key, 3)
    row_keys = jax.random.split(key, ROWS)

    def row_cuts(row_key):
        return jax.random.permutation(row_key, LEN - 1)[:7].astype(jnp.int32) + 1
    cuts = jax.vmap(row_cuts)(row_keys)
    place = jnp.arange(LEN, dtype=jnp.int32)
    marks = jnp.any(place[None, None, :] == cuts[:, :, None], axis=1)
    marks = marks & jnp.logical_not(single)[:, None]
    return jnp.cumsum(marks.astype(jnp.int32), axis=1).astype(jnp.int32)


def draw_padding(key, part):
    single = whole_rows(key)
    key = jax.random.fold_in(key, 5)
    tails = jax.random.randint(key, (ROWS,), 0, LEN // 8 + 1)
    tails = jnp.where(single, 0, tails)
    place = jnp.arange(LEN, dtype=jnp.int32)
    return (place[None, :] < (LEN - tails)[:, None]).astype(jnp.int32)


def shard_levels(own_key, dims, pieces, least, top_value):
    def one(axis_at, parts):
        steps = jax.random.uniform(jax.random.fold_in(jax.random.fold_in(own_key, 6), axis_at), (parts,), jnp.float32, least / len(pieces), top_value / len(pieces))
        return jnp.repeat(jnp.exp(steps), dims[axis_at] // parts).reshape((-1,) + (1,) * (len(dims) - axis_at - 1))

    level = one(*pieces[0])
    for cut in pieces[1:]:
        level = level * one(*cut)
    return level


def centred(own_key, shape, scale, reach, cuts=(), kind=jnp.bfloat16):
    drawn = jax.random.normal(own_key, shape, jnp.float32) * scale
    if len(cuts) > 0:
        drawn = shard_levels(own_key, shape, cuts, -0.22, 0.18) * drawn
    return jnp.clip(drawn, min=-reach, max=reach).astype(kind)


def setup_inputs(seed: int = 0) -> dict:
    splits = jax.random.split(jax.random.key(seed), 19)
    return {
        "inputs": centred(splits[0], (ROWS, LEN, D), 1.0, 6.0, ((0, 4), (1, 8))),
        "cotangent": centred(splits[1], (ROWS, LEN, D), 1.0, 6.0, ((0, 4), (1, 8))),
        "documents": draw_documents(jax.random.fold_in(splits[18], 71), 0),
        "padding": draw_padding(jax.random.fold_in(splits[18], 71), 0),
        "attn_gain": jnp.clip(1.0 + 0.1 * jax.random.normal(splits[4], (D,), jnp.float32), 0.5, 1.5),
        "attn_shift": centred(splits[5], (D,), 0.3, 1.75, (), jnp.float32),
        "query_matrix": centred(splits[6], (D, QW), (D // 4) ** -0.5, 0.25, ((1, 8),)),
        "query_bias": centred(splits[7], (QW,), 0.3, 1.75, ((0, 8),), jnp.float32),
        "shared_matrix": centred(splits[8], (D, 2 * HD), D ** -0.5, 0.125),
        "value_bias": centred(splits[9], (HD,), 0.3, 1.75, (), jnp.float32),
        "output_matrix": centred(splits[10], (QW, D), (QW // 16) ** -0.5, 0.5, ((0, 8),)),
        "output_bias": centred(splits[11], (D,), 0.3, 1.75, (), jnp.float32),
        "mlp_gain": jnp.clip(1.0 + 0.1 * jax.random.normal(splits[12], (D,), jnp.float32), 0.5, 1.5),
        "mlp_shift": centred(splits[13], (D,), 0.3, 1.75, (), jnp.float32),
        "expansion_weights": centred(splits[14], (D, FF), D ** -0.5, 0.125, ((1, 8),)),
        "up_bias": centred(splits[15], (FF,), 0.3, 1.75, ((0, 8),), jnp.float32),
        "down_matrix": centred(splits[16], (FF, D), FF ** -0.5, 0.0625, ((0, 8),)),
        "down_bias": centred(splits[17], (D,), 0.3, 1.75, (), jnp.float32),
    }


@jax.custom_vjp
def low(v):
    return lax.optimization_barrier(v.astype(jnp.bfloat16)).astype(jnp.float32)

@jax.custom_vjp
def low_back(v):
    return v

def low_keep(v):
    return (low(v), None)

def low_pass(kept, grad):
    return (grad,)

def back_keep(v):
    return (v, None)

def back_low(kept, grad):
    return (low(grad),)
low.defvjp(low_keep, low_pass)
low_back.defvjp(back_keep, back_low)
EPSILON = 1e-05
EXACT_ARITHMETIC = lax.Precision.HIGHEST

def layer_norm(values, gain, shift):
    center = values - lax.optimization_barrier(jnp.mean(values, axis=-1, keepdims=True))
    spread = lax.optimization_barrier(jnp.mean(center * center, axis=-1, keepdims=True))
    return center * lax.rsqrt(spread + EPSILON) * gain + shift

def project(left_operand, right_operand):
    return jnp.einsum('nif,ft->nit', left_operand, right_operand, precision=EXACT_ARITHMETIC)

def attend_row(query_row, keys_row, values_row, doc_row, pad_row):
    scores = low_back(jnp.einsum('qhd,kd->hqk', query_row, keys_row, precision=EXACT_ARITHMETIC) * HD ** (-0.5))
    place = jnp.arange(LEN, dtype=jnp.int32)
    causal = place[None, :] <= place[:, None]
    same_doc = doc_row[None, :] == doc_row[:, None]
    visible = (pad_row[None, :] == 1) | (place[None, :] == place[:, None])
    allowed = causal & same_doc & visible
    scores = jnp.where(allowed[None], scores, -1e+30)
    weights = low(jax.nn.softmax(scores, axis=-1))
    return jnp.einsum('hqk,kd->qhd', weights, values_row, precision=EXACT_ARITHMETIC)

def evaluate_block(inputs, attn_gain, attn_shift, query_matrix, query_bias, shared_matrix, value_bias, output_matrix, output_bias, mlp_gain, mlp_shift, expansion_weights, up_bias, down_matrix, down_bias, documents, padding):
    group_rows = inputs.shape[0]
    hidden = low(layer_norm(inputs, attn_gain, attn_shift))
    query = low_back(low(project(hidden, query_matrix) + query_bias))
    shared = project(hidden, shared_matrix)
    keys = low_back(low(shared[..., :HD]))
    values = low_back(low(shared[..., HD:] + value_bias))
    query = query.reshape(group_rows, LEN, HEADS, HD)
    checked = jax.checkpoint(attend_row)

    def per_row(pack):
        return checked(*pack)
    attended_rows = lax.map(per_row, (query, keys, values, documents, padding))
    attended_rows = low_back(low(attended_rows.reshape(group_rows, LEN, HEADS * HD)))
    mixed = inputs + low_back(project(attended_rows, output_matrix)) + output_bias
    normed = low(layer_norm(mixed, mlp_gain, mlp_shift))
    raised = low_back(project(normed, expansion_weights) + up_bias)
    active_values = low(jax.nn.gelu(raised, approximate=True))
    return mixed + low_back(project(active_values, down_matrix)) + down_bias

def reference(inputs, cotangent, documents, padding, attn_gain, attn_shift, query_matrix, query_bias, shared_matrix, value_bias, output_matrix, output_bias, mlp_gain, mlp_shift, expansion_weights, up_bias, down_matrix, down_bias):
    params = (attn_gain.astype(jnp.float32), attn_shift.astype(jnp.float32), query_matrix.astype(jnp.float32), query_bias.astype(jnp.float32), shared_matrix.astype(jnp.float32), value_bias.astype(jnp.float32), output_matrix.astype(jnp.float32), output_bias.astype(jnp.float32), mlp_gain.astype(jnp.float32), mlp_shift.astype(jnp.float32), expansion_weights.astype(jnp.float32), up_bias.astype(jnp.float32), down_matrix.astype(jnp.float32), down_bias.astype(jnp.float32))
    groups = ROWS // SEQS
    packs = (inputs.astype(jnp.float32).reshape(groups, SEQS, LEN, D), cotangent.astype(jnp.float32).reshape(groups, SEQS, LEN, D), documents.reshape(groups, SEQS, LEN), padding.reshape(groups, SEQS, LEN))

    def step(totals, pack):
        span_in, span_cot, span_doc, span_pad = pack

        def closed(values_in, *weights):
            return evaluate_block(values_in, *weights, span_doc, span_pad)
        output, pullback = jax.vjp(closed, span_in, *params)
        grads = pullback(span_cot)
        accumulated_total = tuple((before + after for before, after in zip(totals, grads[1:])))
        return (accumulated_total, (output.astype(jnp.bfloat16), grads[0]))
    zeros = tuple((jnp.zeros_like(weight) for weight in params))
    totals, (outputs, input_grads) = lax.scan(step, zeros, packs)
    block_out = outputs.reshape(ROWS, LEN, D)
    input_grad = input_grads.reshape(ROWS, LEN, D)
    return (block_out, input_grad, totals[0], totals[1], totals[2], totals[3], totals[4], totals[5], totals[6], totals[7], totals[8], totals[9], totals[10], totals[11], totals[12], totals[13])
```

```python
import functools

import jax
import jax.numpy as jnp
from jax import lax
from jax.experimental import pallas as pl
from jax.experimental.pallas import tpu as pltpu
from jax.sharding import PartitionSpec as P

EPSILON = 1e-05
LOG2E = 1.4426950408889634
LN2 = 0.6931471805599453
BF = jnp.bfloat16
F32 = jnp.float32
NEG = -1e30
MIB = 1024 * 1024


def dot(a, b):
    return lax.dot_general(a, b, (((1,), (0,)), ((), ())), preferred_element_type=F32)


def dot_nt(a, b):
    return lax.dot_general(a, b, (((1,), (1,)), ((), ())), preferred_element_type=F32)


def dot_tn(a, b):
    return lax.dot_general(a, b, (((0,), (0,)), ((), ())), preferred_element_type=F32)


def swap(x, bit, axis="tensor"):
    n = lax.axis_size(axis)
    return lax.ppermute(x, axis, [(i, i ^ (1 << bit)) for i in range(n)])


def bit_orders(n):
    bits = list(range(1, n.bit_length() - 1))
    return bits, bits[::-1]


def gather_slots(block, order):
    held = {0: block}
    for bit in list(order) + [0]:
        held.update({k | (1 << bit): swap(v, bit) for k, v in list(held.items())})
    return [held[k] for k in range(len(held))]


def scatter_slots(slots, order):
    held = dict(enumerate(slots))
    for bit in [0] + list(order)[::-1]:
        for k in sorted(held, reverse=True):
            if k & (1 << bit):
                arrived = swap(held.pop(k).astype(BF), bit)
                low = k ^ (1 << bit)
                held[low] = held[low].astype(F32) + arrived.astype(F32)
        held = {k: (v if len(held) == 1 else v.astype(BF)) for k, v in held.items()}
    return held[0].astype(F32)


def xor_order(x, me):
    n = x.shape[0]
    rest = x.shape[1:]
    for bit in range(n.bit_length() - 1):
        pairs = x.reshape((n >> (bit + 1), 2, 1 << bit) + rest)
        x = jnp.where((me >> bit) & 1 == 1, jnp.flip(pairs, 1), pairs).reshape((n,) + rest)
    return x


def stack_heads(block, heads, hd):
    return jnp.concatenate([block[:, i * hd : (i + 1) * hd] for i in range(heads)], axis=0)


def diagonal_mask(rows, cols, same):
    key_at = lax.broadcasted_iota(jnp.int32, (rows, cols), 0)
    query_at = lax.broadcasted_iota(jnp.int32, (rows, cols), 1) % rows
    return (same & (key_at < query_at)) | (key_at == query_at)


def below_blocks(low, at, step, carry):
    even = at - at % 2
    carry = lax.fori_loop(jnp.maximum(low, even), at, lambda b, c: step(b ^ at, 1, c), carry)
    return lax.fori_loop(low // 2, at // 2, lambda p, c: step((p ^ (at // 2)) * 2, 2, c), carry)


def attention_fwd_kernel(low_ref, at_ref, q_ref, k_ref, vt_ref, dock_ref, docq_ref, o_ref, lse_ref, *, heads, hd):
    row = pl.program_id(0)
    span = q_ref.shape[1]
    at = at_ref[0]
    q2 = stack_heads(q_ref[0], heads, hd)
    docq = docq_ref[0]

    def scores(slot, count):
        here = pl.ds(pl.multiple_of(slot * span, count * span), count * span)
        s = dot_nt(k_ref[0, here, :], q2)
        same = dock_ref[0, here, :] == docq
        return s, same, here

    s, same, here = scores(0, 1)
    s = jnp.where(diagonal_mask(span, heads * span, same), s, NEG)
    top = jnp.max(s, axis=0, keepdims=True)
    p = jnp.exp2(s - top)
    total = jnp.sum(p, axis=0, keepdims=True)
    acc = dot(vt_ref[0, :, here], p.astype(BF))

    def step(slot, count, carry):
        top, total, acc = carry
        s, same, here = scores(slot, count)
        s = jnp.where(same, s, NEG)
        new = jnp.maximum(top, jnp.max(s, axis=0, keepdims=True))
        shrink = jnp.exp2(top - new)
        p = jnp.exp2(s - new)
        total = total * shrink + jnp.sum(p, axis=0, keepdims=True)
        acc = acc * shrink + dot(vt_ref[0, :, here], p.astype(BF))
        return new, total, acc

    carry = below_blocks(low_ref[row], at, step, (top, total, acc))
    top, total, acc = carry
    out = (acc / total).T.astype(BF)
    for i in range(heads):
        o_ref[0, :, i * hd : (i + 1) * hd] = out[i * span : (i + 1) * span]
    lse_ref[0, 0] = top + jnp.log2(total)


def attention_bwd_kernel(
    low_ref, at_ref, q_ref, do_ref, o_ref, lse_ref, k_ref, kt_ref, v_ref, dock_ref, docq_ref,
    dq_ref, dk_ref, dv_ref, *, heads, hd, scale,
):
    row = pl.program_id(0)
    span = q_ref.shape[1]
    at = at_ref[0]

    @pl.when(pl.program_id(1) == 0)
    def _():
        dk_ref[...] = jnp.zeros_like(dk_ref)
        dv_ref[...] = jnp.zeros_like(dv_ref)

    q2 = stack_heads(q_ref[0], heads, hd)
    do2 = stack_heads(do_ref[0], heads, hd)
    o2 = stack_heads(o_ref[0], heads, hd)
    delta = jnp.sum((do2.astype(F32) * o2.astype(F32)).T, axis=0, keepdims=True)
    lse = lse_ref[0, 0]
    docq = docq_ref[0]

    def one(slot, count, dqt, diagonal=False):
        here = pl.ds(pl.multiple_of(slot * span, count * span), count * span)
        s = dot_nt(k_ref[0, here, :], q2)
        same = dock_ref[0, here, :] == docq
        if diagonal:
            same = diagonal_mask(span, heads * span, same)
        p = jnp.where(same, jnp.exp2(s - lse), 0.0)
        dp = dot_nt(v_ref[0, here, :], do2)
        ds = (p * (dp - delta)).astype(BF)
        dk_ref[0, here, :] += dot(ds, q2)
        dv_ref[0, here, :] += dot(p.astype(BF), do2)
        return dqt + dot(kt_ref[0, :, here], ds)

    dqt = one(0, 1, jnp.zeros((hd, heads * span), F32), True)
    dqt = below_blocks(low_ref[row], at, one, dqt)
    dq = (dqt * scale).T.astype(BF)
    for i in range(heads):
        dq_ref[0, :, i * hd : (i + 1) * hd] = dq[i * span : (i + 1) * span]


def attention_fwd(q, k, vt, low, at, dock, docq, heads, hd):
    rows, span, width = q.shape
    length = k.shape[1]
    groups = width // (heads * hd)
    gw = heads * hd
    return pl.pallas_call(
        functools.partial(attention_fwd_kernel, heads=heads, hd=hd),
        grid_spec=pltpu.PrefetchScalarGridSpec(
            num_scalar_prefetch=2,
            grid=(rows, groups),
            in_specs=[
                pl.BlockSpec((1, span, gw), lambda r, g, *_: (r, 0, g)),
                pl.BlockSpec((1, length, hd), lambda r, g, *_: (r, 0, 0)),
                pl.BlockSpec((1, hd, length), lambda r, g, *_: (r, 0, 0)),
                pl.BlockSpec((1, length, 1), lambda r, g, *_: (r, 0, 0)),
                pl.BlockSpec((1, 1, heads * span), lambda r, g, *_: (r, 0, 0)),
            ],
            out_specs=[
                pl.BlockSpec((1, span, gw), lambda r, g, *_: (r, 0, g)),
                pl.BlockSpec((1, 1, 1, heads * span), lambda r, g, *_: (r, g, 0, 0)),
            ],
        ),
        out_shape=[
            jax.ShapeDtypeStruct((rows, span, width), BF),
            jax.ShapeDtypeStruct((rows, groups, 1, heads * span), F32),
        ],
        compiler_params=pltpu.CompilerParams(vmem_limit_bytes=24 * MIB),
        cost_estimate=pl.CostEstimate(
            flops=2 * rows * span * width * length, bytes_accessed=8 * MIB, transcendentals=rows * span * length
        ),
    )(low, at, q, k, vt, dock, docq)


def attention_bwd(q, do, o, lse, k, kt, v, low, at, dock, docq, heads, hd, scale):
    rows, span, width = q.shape
    length = k.shape[1]
    groups = width // (heads * hd)
    gw = heads * hd
    blk = pl.BlockSpec((1, span, gw), lambda r, g, *_: (r, 0, g))
    full = pl.BlockSpec((1, length, hd), lambda r, g, *_: (r, 0, 0))
    return pl.pallas_call(
        functools.partial(attention_bwd_kernel, heads=heads, hd=hd, scale=scale),
        grid_spec=pltpu.PrefetchScalarGridSpec(
            num_scalar_prefetch=2,
            grid=(rows, groups),
            in_specs=[
                blk,
                blk,
                blk,
                pl.BlockSpec((1, 1, 1, heads * span), lambda r, g, *_: (r, g, 0, 0)),
                full,
                pl.BlockSpec((1, hd, length), lambda r, g, *_: (r, 0, 0)),
                full,
                pl.BlockSpec((1, length, 1), lambda r, g, *_: (r, 0, 0)),
                pl.BlockSpec((1, 1, heads * span), lambda r, g, *_: (r, 0, 0)),
            ],
            out_specs=[blk, full, full],
        ),
        out_shape=[
            jax.ShapeDtypeStruct((rows, span, width), BF),
            jax.ShapeDtypeStruct((rows, length, hd), F32),
            jax.ShapeDtypeStruct((rows, length, hd), F32),
        ],
        compiler_params=pltpu.CompilerParams(vmem_limit_bytes=32 * MIB),
        cost_estimate=pl.CostEstimate(
            flops=5 * rows * span * width * length, bytes_accessed=16 * MIB, transcendentals=rows * span * length
        ),
    )(low, at, q, do, o, lse, k, kt, v, dock, docq)


def fill(whole_ref, parts, axis):
    for i, slots in enumerate(parts):
        for k, part in enumerate(slots):
            rows, cols = part.shape
            if axis == 1:
                whole_ref[i * rows : (i + 1) * rows, k * cols : (k + 1) * cols] = part[...]
            else:
                whole_ref[k * rows : (k + 1) * rows, i * cols : (i + 1) * cols] = part[...]


def split_parts(refs):
    count = len(refs) // 2
    return [refs[:count], refs[count:]]


def q_kernel(x_ref, b_ref, *refs, factor):
    *parts, o_ref, w_s = refs

    @pl.when(pl.program_id(0) == 0)
    def _():
        fill(w_s, split_parts(parts), 1)

    o_ref[...] = ((dot(x_ref[...], w_s[...]) + b_ref[...]) * factor).astype(BF)


def o_kernel(a_ref, x_ref, b_ref, gain_ref, shift_ref, *refs):
    *parts, mixed_ref, normed_ref, w_s = refs

    @pl.when(pl.program_id(0) == 0)
    def _():
        fill(w_s, split_parts(parts), 0)

    mixed = x_ref[...].astype(F32) + dot(a_ref[...], w_s[...]) + b_ref[...]
    mixed_ref[...] = mixed
    unit, _ = norm_parts(mixed)
    normed_ref[...] = (unit * gain_ref[...] + shift_ref[...]).astype(BF)


def do_kernel(g_ref, *refs):
    *parts, o_ref, w_s = refs

    @pl.when(pl.program_id(0) == 0)
    def _():
        fill(w_s, split_parts(parts), 0)

    o_ref[...] = dot_nt(g_ref[...], w_s[...]).astype(BF)


def dh_kernel(g_ref, kv_ref, shared_ref, *refs):
    *parts, o_ref, w_s = refs

    @pl.when(pl.program_id(0) == 0)
    def _():
        fill(w_s, split_parts(parts), 1)

    o_ref[...] = dot_nt(g_ref[...], w_s[...]) + dot_nt(kv_ref[...], shared_ref[...])


def slot_product(kernel, tiled, fixed, parts, outs, shape):
    flat = parts[0] + parts[1]
    tokens = tiled[0].shape[0]
    tile = tokens // 2
    still = lambda a: pl.BlockSpec(a.shape, lambda i: (0, 0), pipeline_mode=pl.Buffered(1))
    flow = lambda a: pl.BlockSpec((tile, a.shape[1]), lambda i: (i, 0))
    result = pl.pallas_call(
        kernel,
        grid=(2,),
        in_specs=[flow(a) for a in tiled] + [still(a) for a in fixed] + [still(a) for a in flat],
        out_specs=[flow(o) for o in outs],
        out_shape=outs,
        scratch_shapes=[pltpu.VMEM(shape, BF)],
        compiler_params=pltpu.CompilerParams(vmem_limit_bytes=48 * MIB),
        cost_estimate=pl.CostEstimate(
            flops=2 * tokens * shape[0] * shape[1], bytes_accessed=2 * shape[0] * shape[1] + 8 * MIB, transcendentals=0
        ),
    )(*tiled, *fixed, *flat)
    return result


def weight_grad_kernel(*refs, units):
    count = sum(len(a) + len(b) for a, b in units)
    ins = refs[:count]
    o_ref, a_s, b_s, acc, sem = refs[count:]
    steps = len(units)
    wide = a_s.shape[2]
    tile = min(256, wide)

    def copies(u):
        slot, at, out = u % 2, sum(len(a) + len(b) for a, b in units[:u]), []
        for which, (buf, rows) in enumerate(((a_s, units[u][0]), (b_s, units[u][1]))):
            begin = 0
            for j, size in enumerate(rows):
                out.append(
                    pltpu.make_async_copy(ins[at], buf.at[slot, pl.ds(begin, size)], sem.at[slot, which, j])
                )
                begin += size
                at += 1
        return out

    for c in copies(0):
        c.start()
    for u in range(steps):
        if u + 1 < steps:
            for c in copies(u + 1):
                c.start()
        for c in copies(u):
            c.wait()

        @pl.loop(0, wide // tile)
        def _(i, u=u):
            here = pl.ds(pl.multiple_of(i * tile, tile), tile)
            term = dot_tn(a_s[u % 2, :, here], b_s[u % 2])
            if u == 0:
                acc[here, :] = term
            elif u + 1 < steps:
                acc[here, :] += term
            else:
                o_ref[here, :] = (acc[here, :] + term).astype(BF)


def weight_grad(a_units, b_units):
    units = [([x.shape[0] for x in a], [x.shape[0] for x in b]) for a, b in zip(a_units, b_units)]
    flat = [x for a, b in zip(a_units, b_units) for x in list(a) + list(b)]
    tokens = sum(units[0][0])
    wide, cols = a_units[0][0].shape[1], b_units[0][0].shape[1]
    most = max(max(len(a), len(b)) for a, b in units)
    return pl.pallas_call(
        functools.partial(weight_grad_kernel, units=units),
        in_specs=[pl.BlockSpec(memory_space=pl.ANY)] * len(flat),
        out_specs=pl.BlockSpec(memory_space=pltpu.VMEM),
        out_shape=jax.ShapeDtypeStruct((wide, cols), BF),
        scratch_shapes=[
            pltpu.VMEM((2, tokens, wide), BF),
            pltpu.VMEM((2, tokens, cols), BF),
            pltpu.VMEM((wide, cols), F32),
            pltpu.SemaphoreType.DMA((2, 2, most)),
        ],
        compiler_params=pltpu.CompilerParams(vmem_limit_bytes=48 * MIB),
        cost_estimate=pl.CostEstimate(
            flops=2 * tokens * len(units) * wide * cols, bytes_accessed=32 * MIB, transcendentals=0
        ),
    )(*flat)


def sum_all(x, axes):
    for axis in axes:
        for bit in range(lax.axis_size(axis).bit_length() - 1):
            x = x + swap(x, bit, axis)
    return x


def sum_line(x):
    if lax.axis_size("dp") != 4:
        return lax.psum(x, "dp")
    inner = lax.axis_index("dp") % 3 != 0
    pair = (x.astype(F32) + lax.ppermute(x, "dp", [(0, 1), (3, 2)]).astype(F32)).astype(BF)
    both = (pair.astype(F32) + lax.ppermute(pair, "dp", [(1, 2), (2, 1)]).astype(F32)).astype(BF)
    return jnp.where(inner, both, lax.ppermute(both, "dp", [(1, 0), (2, 3)]))


def mlp_kernel(xa_ref, xb_ref, ca_ref, cb_ref, up_ref, bias_ref, down_ref,
               ffa_ref, ffb_ref, gna_ref, gnb_ref, act_ref, gr_ref, gb_ref, x_s, c_s, ff_s, gn_s):
    step = pl.program_id(0)
    half = xa_ref.shape[0]

    @pl.when(step == 0)
    def _():
        x_s[:half] = xa_ref[...]
        x_s[half:] = xb_ref[...]
        c_s[:half] = ca_ref[...]
        c_s[half:] = cb_ref[...]

    raised = dot(x_s[...], up_ref[...]) + bias_ref[...]
    square = raised * raised
    th = jnp.tanh(0.7978845608028654 * raised * (1.0 + 0.044715 * square))
    act = (0.5 * raised * (1.0 + th)).astype(BF)
    act_ref[...] = act
    ff = dot(act, down_ref[...])
    slope = 0.5 * (1.0 + th) + 0.5 * raised * (1.0 - th * th) * (
        0.7978845608028654 * (1.0 + 3 * 0.044715 * square)
    )
    gr32 = dot_nt(c_s[...], down_ref[...]) * slope
    gr = gr32.astype(BF)
    gr_ref[...] = gr
    gb_ref[...] = jnp.sum(gr.astype(F32), axis=0, keepdims=True)
    gn = dot_nt(gr, up_ref[...])

    @pl.when(step == 0)
    def _():
        ff_s[...] = ff
        gn_s[...] = gn

    @pl.when(step != 0)
    def _():
        ff_s[...] += ff
        gn_s[...] += gn

    @pl.when(step == pl.num_programs(0) - 1)
    def _():
        ffa_ref[...] = ff_s[:half].astype(BF)
        ffb_ref[...] = ff_s[half:].astype(BF)
        gna_ref[...] = gn_s[:half].astype(BF)
        gnb_ref[...] = gn_s[half:].astype(BF)


def mlp_unit(xa, xb, ca, cb, up, bias, down):
    half, d = xa.shape
    ff = up.shape[1]
    tile = min(512, ff)
    tokens = 2 * half
    whole = pl.BlockSpec((half, d), lambda j: (0, 0))
    return pl.pallas_call(
        mlp_kernel,
        grid=(ff // tile,),
        in_specs=[
            whole, whole, whole, whole,
            pl.BlockSpec((d, tile), lambda j: (0, j)),
            pl.BlockSpec((1, tile), lambda j: (0, j)),
            pl.BlockSpec((tile, d), lambda j: (j, 0)),
        ],
        out_specs=[
            whole, whole, whole, whole,
            pl.BlockSpec((tokens, tile), lambda j: (0, j)),
            pl.BlockSpec((tokens, tile), lambda j: (0, j)),
            pl.BlockSpec((1, tile), lambda j: (0, j)),
        ],
        out_shape=[jax.ShapeDtypeStruct((half, d), BF)] * 4
        + [jax.ShapeDtypeStruct((tokens, ff), BF)] * 2
        + [jax.ShapeDtypeStruct((1, ff), F32)],
        scratch_shapes=[
            pltpu.VMEM((tokens, d), BF),
            pltpu.VMEM((tokens, d), BF),
            pltpu.VMEM((tokens, d), F32),
            pltpu.VMEM((tokens, d), F32),
        ],
        compiler_params=pltpu.CompilerParams(vmem_limit_bytes=56 * MIB),
        cost_estimate=pl.CostEstimate(
            flops=8 * tokens * d * ff, bytes_accessed=20 * MIB, transcendentals=tokens * ff
        ),
    )(xa, xb, ca, cb, up, bias, down)


def norm_parts(values):
    center = values - jnp.mean(values, axis=-1, keepdims=True)
    scale = lax.rsqrt(jnp.mean(center * center, axis=-1, keepdims=True) + EPSILON)
    return center * scale, scale


def norm_back(unit, scale, gain, grad):
    e = gain * grad
    back = scale * (e - jnp.mean(e, axis=-1, keepdims=True) - unit * jnp.mean(e * unit, axis=-1, keepdims=True))
    return back, jnp.sum(grad * unit, axis=(0, 1)), jnp.sum(grad, axis=(0, 1))


def body(
    inputs, cotangent, documents, padding, attn_gain, attn_shift, query_matrix, query_bias, shared_matrix,
    value_bias, output_matrix, output_bias, mlp_gain, mlp_shift, expansion_weights, up_bias, down_matrix, down_bias,
):
    n = lax.axis_size("tensor")
    me = lax.axis_index("tensor")
    hd = value_bias.shape[0]
    seqs, span, d = inputs.shape
    length = documents.shape[1]
    qw = query_matrix.shape[1]
    heads = qw // hd
    scale = hd**-0.5
    paths = bit_orders(n)
    tokens = seqs * span

    x32 = inputs.astype(F32)
    unit1, scale1 = norm_parts(x32)
    hidden = (unit1 * attn_gain + attn_shift).astype(BF)
    h2 = hidden.reshape(tokens, d)
    shared = dot(h2, shared_matrix)
    kv_own = jnp.concatenate([shared[:, :hd], shared[:, hd:] + value_bias], axis=1).astype(BF)
    kv_own = kv_own.reshape(seqs, span, 2 * hd)
    kv = jnp.concatenate(gather_slots(kv_own, paths[0]), axis=1)
    keys, values = kv[..., :hd], kv[..., hd:]
    keys_t, values_t = keys.swapaxes(1, 2), values.swapaxes(1, 2)

    half = d // 2
    wq = [gather_slots(query_matrix[i * half : (i + 1) * half], paths[i]) for i in range(2)]
    wo = [gather_slots(output_matrix[:, i * half : (i + 1) * half], paths[i]) for i in range(2)]
    bq = jnp.concatenate(gather_slots(query_bias[None], paths[0]), axis=1)

    like = lambda t, cols: jax.ShapeDtypeStruct((tokens, cols), t)
    (query,) = slot_product(
        functools.partial(q_kernel, factor=scale * LOG2E), [h2], [bq], wq, [like(BF, n * qw)], (d, n * qw)
    )
    query = query.reshape(seqs, span, n * qw)
    first = lax.dynamic_slice_in_dim(documents, me * span, 1, 1)
    low = (jnp.sum((documents < first).astype(jnp.int32), axis=1) // span).astype(jnp.int32)
    low = jnp.minimum(low, me)
    at = me.reshape(1).astype(jnp.int32)
    dock = jnp.where(padding == 1, documents, -1)
    dock = xor_order(dock.reshape(seqs, n, span).swapaxes(0, 1), me).swapaxes(0, 1).reshape(seqs, length, 1)
    docq = lax.dynamic_slice_in_dim(documents, me * span, span, 1)
    docq = jnp.concatenate([docq] * heads, axis=1)[:, None, :]
    attended, lse = attention_fwd(query, keys, values_t, low, at, dock, docq, heads, hd)
    a2 = attended.reshape(tokens, n * qw)
    mixed, normed = slot_product(
        o_kernel, [a2, inputs.reshape(tokens, d)], [output_bias[None], mlp_gain[None], mlp_shift[None]], wo,
        [like(F32, d), like(BF, d)], (n * qw, d),
    )
    mixed, normed = mixed.reshape(seqs, span, d), normed.reshape(seqs, span, d)
    unit2, scale2 = norm_parts(mixed)

    cot_slots = [gather_slots(cotangent[r], paths[r % 2]) for r in range(seqs)]
    normed_slots = [gather_slots(normed[r], paths[r % 2]) for r in range(seqs)]
    ff_slots = [[None] * n for _ in range(seqs)]
    gn_slots = [[None] * n for _ in range(seqs)]
    acts, grs, xs, cs = [], [], [], []
    up_bias_part = jnp.zeros((1, up_bias.shape[0]), F32)
    for k in range(0, n, 2):
        for r in range(seqs):
            xa, xb, ca, cb = normed_slots[r][k], normed_slots[r][k + 1], cot_slots[r][k], cot_slots[r][k + 1]
            ffa, ffb, gna, gnb, act, gr, gb = mlp_unit(
                xa, xb, ca, cb, expansion_weights, up_bias[None], down_matrix
            )
            ff_slots[r][k], ff_slots[r][k + 1] = ffa, ffb
            gn_slots[r][k], gn_slots[r][k + 1] = gna, gnb
            acts.append(act)
            grs.append(gr)
            xs.append([xa, xb])
            cs.append([ca, cb])
            up_bias_part = up_bias_part + gb
    grad_normed = jnp.stack([scatter_slots(gn_slots[r], paths[r % 2]) for r in range(seqs)])
    down_gradient = weight_grad([[a] for a in acts], cs)
    up_gradient = weight_grad(xs, [[g] for g in grs])
    mlp_branch = jnp.stack([scatter_slots(ff_slots[r], paths[r % 2]) for r in range(seqs)])
    block_out = (mixed + mlp_branch + down_bias).astype(BF)

    cot_wide = cotangent.astype(F32)
    back2, mlp_gain_part, mlp_shift_part = norm_back(unit2, scale2, mlp_gain, grad_normed)
    grad_mixed = cot_wide + back2
    gm2 = grad_mixed.astype(BF).reshape(tokens, d)
    (grad_attended,) = slot_product(do_kernel, [gm2], [], wo, [like(BF, n * qw)], (n * qw, d))
    grad_attended = grad_attended.reshape(seqs, span, n * qw)
    dq, dk, dv = attention_bwd(
        query, grad_attended, attended, lse, keys, keys_t, values, low, at, dock, docq, heads, hd, scale
    )
    dq2 = dq.reshape(tokens, n * qw)

    wo_grads = [
        scatter_slots(
            [dot_tn(a2[:, k * qw : (k + 1) * qw], gm2[:, i * half : (i + 1) * half]) for k in range(n)], paths[i]
        )
        for i in range(2)
    ]
    dkv = jnp.concatenate([dk * LN2, dv], axis=-1).astype(BF)
    dkv_own = scatter_slots([dkv[:, k * span : (k + 1) * span] for k in range(n)], paths[0]).astype(BF)
    wq_grads = [
        scatter_slots(
            [dot_tn(h2[:, i * half : (i + 1) * half], dq2[:, k * qw : (k + 1) * qw]) for k in range(n)], paths[i]
        )
        for i in range(2)
    ]
    (grad_hidden,) = slot_product(
        dh_kernel, [dq2, dkv_own.reshape(tokens, 2 * hd)], [shared_matrix], wq, [like(F32, d)], (d, n * qw)
    )
    grad_hidden = grad_hidden.reshape(seqs, span, d)
    back1, attn_gain_part, attn_shift_part = norm_back(unit1, scale1, attn_gain, grad_hidden)
    input_grad = grad_mixed + back1
    shared_part = dot_tn(h2, dkv_own.reshape(tokens, 2 * hd))
    value_bias_part = jnp.sum(dkv_own[..., hd:].astype(F32), axis=(0, 1))
    query_bias_part = xor_order(jnp.sum(dq2.astype(F32), axis=0).reshape(n, qw), me).reshape(-1)

    everywhere = ("tensor", "dp")
    down_gradient, up_gradient = lax.psum((down_gradient, up_gradient), "dp")
    output_gradient = jnp.concatenate([sum_line(g.astype(BF)) for g in wo_grads], axis=1)
    query_gradient = jnp.concatenate([sum_line(g.astype(BF)) for g in wq_grads], axis=0)
    up_bias_grad = sum_all(up_bias_part, ("dp",))[0]
    early = sum_all(
        jnp.stack([mlp_gain_part, mlp_shift_part, jnp.sum(grad_mixed, axis=(0, 1)), jnp.sum(cot_wide, axis=(0, 1))]),
        everywhere,
    )
    mlp_gain_grad, mlp_shift_grad, output_bias_grad, down_bias_grad = early
    late = sum_all(
        jnp.concatenate([attn_gain_part, attn_shift_part, query_bias_part, value_bias_part])[None], everywhere
    )[0]
    attn_gain_grad, attn_shift_grad = late[:d], late[d : 2 * d]
    query_bias_grad = lax.dynamic_slice_in_dim(late, 2 * d + me * qw, qw, 0)
    value_bias_grad = late[2 * d + n * qw :]
    piece = d // n
    shared_slots = [
        lax.dynamic_slice_in_dim(shared_part, (me ^ k) * piece, piece, 0).astype(BF) for k in range(n)
    ]
    shared_sum = sum_all(scatter_slots(shared_slots, paths[0]), ("dp",)).astype(BF)
    shared_slots = jnp.concatenate(gather_slots(shared_sum, paths[0]), axis=0)
    shared_grad = xor_order(shared_slots.reshape(n, piece, 2 * hd), me).reshape(d, 2 * hd).astype(F32)
    output_gradient, query_gradient, up_gradient, down_gradient = (
        g.astype(F32) for g in (output_gradient, query_gradient, up_gradient, down_gradient)
    )
    return (
        block_out, input_grad, attn_gain_grad, attn_shift_grad, query_gradient, query_bias_grad, shared_grad,
        value_bias_grad, output_gradient, output_bias_grad, mlp_gain_grad, mlp_shift_grad, up_gradient, up_bias_grad,
        down_gradient, down_bias_grad,
    )


def solution(mesh):
    act = P("dp", "tensor", None)
    cols, rows, vec, rep = P(None, "tensor"), P("tensor", None), P("tensor"), P()
    ids = P("dp", None)
    return jax.shard_map(
        body,
        mesh=mesh,
        in_specs=(act, act, ids, ids, rep, rep, cols, vec, rep, rep, rows, rep, rep, rep, cols, vec, rows, rep),
        out_specs=(act, act, rep, rep, cols, vec, rep, rep, rows, rep, rep, rep, cols, vec, rows, rep),
        check_vma=False,
    )
```

```python
import functools

import jax
import jax.numpy as jnp
from jax import lax
from jax.experimental import pallas as pl
from jax.experimental.pallas import tpu as pltpu
from jax.sharding import PartitionSpec as P

EPSILON = 1e-05
LOG2E = 1.4426950408889634
LN2 = 0.6931471805599453
BF = jnp.bfloat16
F32 = jnp.float32
NEG = -1e30
MIB = 1024 * 1024


def dot(a, b):
    return lax.dot_general(a, b, (((1,), (0,)), ((), ())), preferred_element_type=F32)


def dot_nt(a, b):
    return lax.dot_general(a, b, (((1,), (1,)), ((), ())), preferred_element_type=F32)


def dot_tn(a, b):
    return lax.dot_general(a, b, (((0,), (0,)), ((), ())), preferred_element_type=F32)


def swap(x, bit, axis="tensor"):
    n = lax.axis_size(axis)
    return lax.ppermute(x, axis, [(i, i ^ (1 << bit)) for i in range(n)])


def bit_orders(n):
    bits = list(range(1, n.bit_length() - 1))
    return bits, bits[::-1]


def gather_slots(block, order):
    held = {0: block}
    for bit in list(order) + [0]:
        held.update({k | (1 << bit): swap(v, bit) for k, v in list(held.items())})
    return [held[k] for k in range(len(held))]


def scatter_slots(slots, order):
    held = dict(enumerate(slots))
    for bit in [0] + list(order)[::-1]:
        for k in sorted(held, reverse=True):
            if k & (1 << bit):
                arrived = swap(held.pop(k).astype(BF), bit)
                low = k ^ (1 << bit)
                held[low] = held[low].astype(F32) + arrived.astype(F32)
        held = {k: (v if len(held) == 1 else v.astype(BF)) for k, v in held.items()}
    return held[0].astype(F32)


def xor_order(x, me):
    n = x.shape[0]
    rest = x.shape[1:]
    for bit in range(n.bit_length() - 1):
        pairs = x.reshape((n >> (bit + 1), 2, 1 << bit) + rest)
        x = jnp.where((me >> bit) & 1 == 1, jnp.flip(pairs, 1), pairs).reshape((n,) + rest)
    return x


def stack_heads(block, heads, hd):
    return jnp.concatenate([block[:, i * hd : (i + 1) * hd] for i in range(heads)], axis=0)


def diagonal_mask(rows, cols, same):
    key_at = lax.broadcasted_iota(jnp.int32, (rows, cols), 0)
    query_at = lax.broadcasted_iota(jnp.int32, (rows, cols), 1) % rows
    return (same & (key_at < query_at)) | (key_at == query_at)


def below_blocks(low, at, step, carry):
    even = at - at % 2
    carry = lax.fori_loop(jnp.maximum(low, even), at, lambda b, c: step(b ^ at, 1, c), carry)
    return lax.fori_loop(low // 2, at // 2, lambda p, c: step((p ^ (at // 2)) * 2, 2, c), carry)


def attention_fwd_kernel(low_ref, at_ref, q_ref, k_ref, vt_ref, dock_ref, docq_ref, o_ref, lse_ref, *, heads, hd):
    row = pl.program_id(0)
    span = q_ref.shape[1]
    at = at_ref[0]
    q2 = stack_heads(q_ref[0], heads, hd)
    docq = docq_ref[0]

    def scores(slot, count):
        here = pl.ds(pl.multiple_of(slot * span, count * span), count * span)
        s = dot_nt(k_ref[0, here, :], q2)
        same = dock_ref[0, here, :] == docq
        return s, same, here

    s, same, here = scores(0, 1)
    s = jnp.where(diagonal_mask(span, heads * span, same), s, NEG)
    top = jnp.max(s, axis=0, keepdims=True)
    p = jnp.exp2(s - top)
    total = jnp.sum(p, axis=0, keepdims=True)
    acc = dot(vt_ref[0, :, here], p.astype(BF))

    def step(slot, count, carry):
        top, total, acc = carry
        s, same, here = scores(slot, count)
        s = jnp.where(same, s, NEG)
        new = jnp.maximum(top, jnp.max(s, axis=0, keepdims=True))
        shrink = jnp.exp2(top - new)
        p = jnp.exp2(s - new)
        total = total * shrink + jnp.sum(p, axis=0, keepdims=True)
        acc = acc * shrink + dot(vt_ref[0, :, here], p.astype(BF))
        return new, total, acc

    carry = below_blocks(low_ref[row], at, step, (top, total, acc))
    top, total, acc = carry
    out = (acc / total).T.astype(BF)
    for i in range(heads):
        o_ref[0, :, i * hd : (i + 1) * hd] = out[i * span : (i + 1) * span]
    lse_ref[0, 0] = top + jnp.log2(total)


def attention_bwd_kernel(
    low_ref, at_ref, q_ref, do_ref, o_ref, lse_ref, k_ref, kt_ref, v_ref, dock_ref, docq_ref,
    dq_ref, dk_ref, dv_ref, *, heads, hd, scale,
):
    row = pl.program_id(0)
    span = q_ref.shape[1]
    at = at_ref[0]

    @pl.when(pl.program_id(1) == 0)
    def _():
        dk_ref[...] = jnp.zeros_like(dk_ref)
        dv_ref[...] = jnp.zeros_like(dv_ref)

    q2 = stack_heads(q_ref[0], heads, hd)
    do2 = stack_heads(do_ref[0], heads, hd)
    o2 = stack_heads(o_ref[0], heads, hd)
    delta = jnp.sum((do2.astype(F32) * o2.astype(F32)).T, axis=0, keepdims=True)
    lse = lse_ref[0, 0]
    docq = docq_ref[0]

    def one(slot, count, dqt, diagonal=False):
        here = pl.ds(pl.multiple_of(slot * span, count * span), count * span)
        s = dot_nt(k_ref[0, here, :], q2)
        same = dock_ref[0, here, :] == docq
        if diagonal:
            same = diagonal_mask(span, heads * span, same)
        p = jnp.where(same, jnp.exp2(s - lse), 0.0)
        dp = dot_nt(v_ref[0, here, :], do2)
        ds = (p * (dp - delta)).astype(BF)
        dk_ref[0, here, :] += dot(ds, q2)
        dv_ref[0, here, :] += dot(p.astype(BF), do2)
        return dqt + dot(kt_ref[0, :, here], ds)

    dqt = one(0, 1, jnp.zeros((hd, heads * span), F32), True)
    dqt = below_blocks(low_ref[row], at, one, dqt)
    dq = (dqt * scale).T.astype(BF)
    for i in range(heads):
        dq_ref[0, :, i * hd : (i + 1) * hd] = dq[i * span : (i + 1) * span]


def attention_fwd(q, k, vt, low, at, dock, docq, heads, hd):
    rows, span, width = q.shape
    length = k.shape[1]
    groups = width // (heads * hd)
    gw = heads * hd
    return pl.pallas_call(
        functools.partial(attention_fwd_kernel, heads=heads, hd=hd),
        grid_spec=pltpu.PrefetchScalarGridSpec(
            num_scalar_prefetch=2,
            grid=(rows, groups),
            in_specs=[
                pl.BlockSpec((1, span, gw), lambda r, g, *_: (r, 0, g)),
                pl.BlockSpec((1, length, hd), lambda r, g, *_: (r, 0, 0)),
                pl.BlockSpec((1, hd, length), lambda r, g, *_: (r, 0, 0)),
                pl.BlockSpec((1, length, 1), lambda r, g, *_: (r, 0, 0)),
                pl.BlockSpec((1, 1, heads * span), lambda r, g, *_: (r, 0, 0)),
            ],
            out_specs=[
                pl.BlockSpec((1, span, gw), lambda r, g, *_: (r, 0, g)),
                pl.BlockSpec((1, 1, 1, heads * span), lambda r, g, *_: (r, g, 0, 0)),
            ],
        ),
        out_shape=[
            jax.ShapeDtypeStruct((rows, span, width), BF),
            jax.ShapeDtypeStruct((rows, groups, 1, heads * span), F32),
        ],
        compiler_params=pltpu.CompilerParams(vmem_limit_bytes=24 * MIB),
        cost_estimate=pl.CostEstimate(
            flops=2 * rows * span * width * length, bytes_accessed=8 * MIB, transcendentals=rows * span * length
        ),
    )(low, at, q, k, vt, dock, docq)


def attention_bwd(q, do, o, lse, k, kt, v, low, at, dock, docq, heads, hd, scale):
    rows, span, width = q.shape
    length = k.shape[1]
    groups = width // (heads * hd)
    gw = heads * hd
    blk = pl.BlockSpec((1, span, gw), lambda r, g, *_: (r, 0, g))
    full = pl.BlockSpec((1, length, hd), lambda r, g, *_: (r, 0, 0))
    return pl.pallas_call(
        functools.partial(attention_bwd_kernel, heads=heads, hd=hd, scale=scale),
        grid_spec=pltpu.PrefetchScalarGridSpec(
            num_scalar_prefetch=2,
            grid=(rows, groups),
            in_specs=[
                blk,
                blk,
                blk,
                pl.BlockSpec((1, 1, 1, heads * span), lambda r, g, *_: (r, g, 0, 0)),
                full,
                pl.BlockSpec((1, hd, length), lambda r, g, *_: (r, 0, 0)),
                full,
                pl.BlockSpec((1, length, 1), lambda r, g, *_: (r, 0, 0)),
                pl.BlockSpec((1, 1, heads * span), lambda r, g, *_: (r, 0, 0)),
            ],
            out_specs=[blk, full, full],
        ),
        out_shape=[
            jax.ShapeDtypeStruct((rows, span, width), BF),
            jax.ShapeDtypeStruct((rows, length, hd), F32),
            jax.ShapeDtypeStruct((rows, length, hd), F32),
        ],
        compiler_params=pltpu.CompilerParams(vmem_limit_bytes=32 * MIB),
        cost_estimate=pl.CostEstimate(
            flops=5 * rows * span * width * length, bytes_accessed=16 * MIB, transcendentals=rows * span * length
        ),
    )(low, at, q, do, o, lse, k, kt, v, dock, docq)


def fill(whole_ref, parts, axis):
    for i, slots in enumerate(parts):
        for k, part in enumerate(slots):
            rows, cols = part.shape
            if axis == 1:
                whole_ref[i * rows : (i + 1) * rows, k * cols : (k + 1) * cols] = part[...]
            else:
                whole_ref[k * rows : (k + 1) * rows, i * cols : (i + 1) * cols] = part[...]


def split_parts(refs):
    count = len(refs) // 2
    return [refs[:count], refs[count:]]


def q_kernel(x_ref, b_ref, *refs, factor):
    *parts, o_ref, w_s = refs

    @pl.when(pl.program_id(0) == 0)
    def _():
        fill(w_s, split_parts(parts), 1)

    o_ref[...] = ((dot(x_ref[...], w_s[...]) + b_ref[...]) * factor).astype(BF)


def o_kernel(a_ref, x_ref, b_ref, gain_ref, shift_ref, *refs):
    *parts, mixed_ref, normed_ref, w_s = refs

    @pl.when(pl.program_id(0) == 0)
    def _():
        fill(w_s, split_parts(parts), 0)

    mixed = x_ref[...].astype(F32) + dot(a_ref[...], w_s[...]) + b_ref[...]
    mixed_ref[...] = mixed
    unit, _ = norm_parts(mixed)
    normed_ref[...] = (unit * gain_ref[...] + shift_ref[...]).astype(BF)


def do_kernel(g_ref, *refs):
    *parts, o_ref, w_s = refs

    @pl.when(pl.program_id(0) == 0)
    def _():
        fill(w_s, split_parts(parts), 0)

    o_ref[...] = dot_nt(g_ref[...], w_s[...]).astype(BF)


def dh_kernel(g_ref, kv_ref, shared_ref, *refs):
    *parts, o_ref, w_s = refs

    @pl.when(pl.program_id(0) == 0)
    def _():
        fill(w_s, split_parts(parts), 1)

    o_ref[...] = dot_nt(g_ref[...], w_s[...]) + dot_nt(kv_ref[...], shared_ref[...])


def slot_product(kernel, tiled, fixed, parts, outs, shape):
    flat = parts[0] + parts[1]
    tokens = tiled[0].shape[0]
    tile = tokens // 2
    still = lambda a: pl.BlockSpec(a.shape, lambda i: (0, 0), pipeline_mode=pl.Buffered(1))
    flow = lambda a: pl.BlockSpec((tile, a.shape[1]), lambda i: (i, 0))
    result = pl.pallas_call(
        kernel,
        grid=(2,),
        in_specs=[flow(a) for a in tiled] + [still(a) for a in fixed] + [still(a) for a in flat],
        out_specs=[flow(o) for o in outs],
        out_shape=outs,
        scratch_shapes=[pltpu.VMEM(shape, BF)],
        compiler_params=pltpu.CompilerParams(vmem_limit_bytes=48 * MIB),
        cost_estimate=pl.CostEstimate(
            flops=2 * tokens * shape[0] * shape[1], bytes_accessed=2 * shape[0] * shape[1] + 8 * MIB, transcendentals=0
        ),
    )(*tiled, *fixed, *flat)
    return result


def weight_grad_kernel(*refs, units):
    count = sum(len(a) + len(b) for a, b in units)
    ins = refs[:count]
    o_ref, a_s, b_s, acc, sem = refs[count:]
    steps = len(units)
    wide = a_s.shape[2]
    tile = min(256, wide)

    def copies(u):
        slot, at, out = u % 2, sum(len(a) + len(b) for a, b in units[:u]), []
        for which, (buf, rows) in enumerate(((a_s, units[u][0]), (b_s, units[u][1]))):
            begin = 0
            for j, size in enumerate(rows):
                out.append(
                    pltpu.make_async_copy(ins[at], buf.at[slot, pl.ds(begin, size)], sem.at[slot, which, j])
                )
                begin += size
                at += 1
        return out

    for c in copies(0):
        c.start()
    for u in range(steps):
        if u + 1 < steps:
            for c in copies(u + 1):
                c.start()
        for c in copies(u):
            c.wait()

        @pl.loop(0, wide // tile)
        def _(i, u=u):
            here = pl.ds(pl.multiple_of(i * tile, tile), tile)
            term = dot_tn(a_s[u % 2, :, here], b_s[u % 2])
            if u == 0:
                acc[here, :] = term
            elif u + 1 < steps:
                acc[here, :] += term
            else:
                o_ref[here, :] = (acc[here, :] + term).astype(BF)


def weight_grad(a_units, b_units):
    units = [([x.shape[0] for x in a], [x.shape[0] for x in b]) for a, b in zip(a_units, b_units)]
    flat = [x for a, b in zip(a_units, b_units) for x in list(a) + list(b)]
    tokens = sum(units[0][0])
    wide, cols = a_units[0][0].shape[1], b_units[0][0].shape[1]
    most = max(max(len(a), len(b)) for a, b in units)
    return pl.pallas_call(
        functools.partial(weight_grad_kernel, units=units),
        in_specs=[pl.BlockSpec(memory_space=pl.ANY)] * len(flat),
        out_specs=pl.BlockSpec(memory_space=pltpu.VMEM),
        out_shape=jax.ShapeDtypeStruct((wide, cols), BF),
        scratch_shapes=[
            pltpu.VMEM((2, tokens, wide), BF),
            pltpu.VMEM((2, tokens, cols), BF),
            pltpu.VMEM((wide, cols), F32),
            pltpu.SemaphoreType.DMA((2, 2, most)),
        ],
        compiler_params=pltpu.CompilerParams(vmem_limit_bytes=48 * MIB),
        cost_estimate=pl.CostEstimate(
            flops=2 * tokens * len(units) * wide * cols, bytes_accessed=32 * MIB, transcendentals=0
        ),
    )(*flat)


def sum_all(x, axes):
    for axis in axes:
        for bit in range(lax.axis_size(axis).bit_length() - 1):
            x = x + swap(x, bit, axis)
    return x


MESH = pl.DeviceIdType.MESH


def greet(bits, line):
    me, z = lax.axis_index("tensor"), lax.axis_index("dp")
    barrier = pltpu.get_barrier_semaphore()
    for bit in bits:
        pl.semaphore_signal(barrier, inc=1, device_id={"tensor": me ^ (1 << bit)}, device_id_type=MESH)
    count = len(bits)
    if line:
        inner = (z == 1) | (z == 2)
        pl.semaphore_signal(barrier, inc=1, device_id={"dp": z ^ 1}, device_id_type=MESH)

        @pl.when(inner)
        def _():
            pl.semaphore_signal(barrier, inc=1, device_id={"dp": 3 - z}, device_id_type=MESH)

        count = count + 1 + inner.astype(jnp.int32)
    pl.semaphore_wait(barrier, count)


class Scatter:
    def __init__(self, bits, send, recv, send_sem, recv_sem):
        self.bits, self.send, self.recv, self.send_sem, self.recv_sem = bits, send, recv, send_sem, recv_sem
        self.me = lax.axis_index("tensor")

    def stage(self, k):
        return next((i for i, b in enumerate(self.bits) if k >> b & 1), len(self.bits))

    def copy(self, k):
        bit = self.bits[self.stage(k)]
        return pltpu.make_async_remote_copy(
            src_ref=self.send.at[k],
            dst_ref=self.recv.at[k - 1],
            send_sem=self.send_sem.at[k],
            recv_sem=self.recv_sem.at[k],
            device_id={"tensor": self.me ^ (1 << bit)},
            device_id_type=MESH,
        )

    def put(self, k, value):
        self.send[k] = value.astype(BF)
        if self.stage(k) == 0:
            self.copy(k).start()

    def total(self, k):
        value = self.send[k].astype(F32)
        for bit in self.bits[: self.stage(k)]:
            self.copy(k | (1 << bit)).wait_recv()
            value = value + self.recv[(k | (1 << bit)) - 1].astype(F32)
        return value

    def forward(self, k):
        self.send[k] = self.total(k).astype(BF)
        self.copy(k).start()

    def drain(self):
        for k in range(1, 1 << len(self.bits)):
            self.copy(k).wait_send()


def scatter_order(bits):
    n = 1 << len(bits)
    rank = lambda k: next(i for i, b in enumerate(bits) if k >> b & 1)
    return sorted(range(2, n, 2), key=lambda k: (rank(k), -k))


def attention_grads_kernel(a_ref, gm_ref, dq_ref, h_ref, dkv_ref, wo_ref, wq_ref, kv_ref,
                           send, recv, ksend, krecv, zbuf, ssem, rsem, ksem, krsem, zsem, *, orders, line, qw):
    bits_of = [[0] + list(o)[::-1] for o in orders]
    count = len(bits_of[0])
    n = 1 << count
    half = gm_ref.shape[1] // 2
    greet(range(count), line)
    z = lax.axis_index("dp")

    kv = Scatter(bits_of[0], ksend, krecv, ksem, krsem)
    for k in list(range(1, n, 2)) + list(range(0, n, 2)):
        kv.put(k, dkv_ref[k])

    pairs = ((a_ref, gm_ref, wo_ref), (dq_ref, h_ref, wq_ref))
    work = [
        [Scatter(bits_of[p], send.at[m, p], recv.at[m, p], ssem.at[m, p], rsem.at[m, p]) for p in range(2)]
        for m in range(2)
    ]
    sequence = [scatter_order(b) for b in bits_of]

    def compute(m, p, k):
        x, y, _ = pairs[m]
        work[m][p].put(k, dot_tn(x[:, k * qw : (k + 1) * qw], y[:, p * half : (p + 1) * half]))

    def products(m):
        for i in range(n // 2):
            for p in range(2):
                k = (sequence[p] + [0])[i]
                compute(m, p, k + 1)
                compute(m, p, k)

    def stage(m, i):
        for at in range(n // 2 - 1):
            for p in range(2):
                k = sequence[p][at]
                if work[m][p].stage(k) == i:
                    work[m][p].forward(k)

    def z_copy(m, p, hop, to):
        return pltpu.make_async_remote_copy(
            src_ref=zbuf.at[m, p, hop % 2],
            dst_ref=zbuf.at[m, p, 2 + hop % 2],
            send_sem=zsem.at[m, p, hop],
            recv_sem=zsem.at[m, p, 3 + hop],
            device_id={"dp": to},
            device_id_type=MESH,
        )

    inner = (z == 1) | (z == 2)
    outer = jnp.logical_not(inner)

    def finish(m, p):
        value = work[m][p].total(0)
        if not line:
            pairs[m][2][:, p * half : (p + 1) * half] = value
            return
        zbuf[m, p, 0] = value.astype(BF)

        @pl.when(outer)
        def _():
            z_copy(m, p, 0, z ^ 1).start()

    def middle(m, p):
        @pl.when(inner)
        def _():
            z_copy(m, p, 0, z ^ 1).wait_recv()
            zbuf[m, p, 1] = (zbuf[m, p, 0].astype(F32) + zbuf[m, p, 2].astype(F32)).astype(BF)
            z_copy(m, p, 1, 3 - z).start()

    def back(m, p):
        here = pairs[m][2].at[:, p * half : (p + 1) * half]

        @pl.when(inner)
        def _():
            z_copy(m, p, 1, 3 - z).wait_recv()
            both = (zbuf[m, p, 1].astype(F32) + zbuf[m, p, 3].astype(F32)).astype(BF)
            zbuf[m, p, 0] = both
            z_copy(m, p, 2, z ^ 1).start()
            here[...] = both.astype(F32)

    def close(m, p):
        here = pairs[m][2].at[:, p * half : (p + 1) * half]

        @pl.when(outer)
        def _():
            z_copy(m, p, 0, z ^ 1).wait_send()
            z_copy(m, p, 2, z ^ 1).wait_recv()
            here[...] = zbuf[m, p, 2].astype(F32)

        @pl.when(inner)
        def _():
            z_copy(m, p, 1, 3 - z).wait_send()
            z_copy(m, p, 2, z ^ 1).wait_send()

    def kv_stage(i):
        for k in scatter_order(bits_of[0]):
            if kv.stage(k) == i:
                kv.forward(k)

    def both(step, m):
        for p in range(2):
            step(m, p)

    products(0)
    stage(0, 1)
    products(1)
    for i in range(1, count):
        kv_stage(i)
        if i + 1 < count:
            stage(0, i + 1)
        else:
            both(finish, 0)
        stage(1, i)
    kv_ref[...] = kv.total(0).astype(BF)
    if line:
        both(middle, 0)
    both(finish, 1)
    if line:
        both(back, 0)
        both(middle, 1)
        both(close, 0)
        both(back, 1)
        both(close, 1)
    kv.drain()
    for m in range(2):
        for p in range(2):
            work[m][p].drain()


def attention_grads(a, gm, dq, h, dkv, orders):
    n, line = lax.axis_size("tensor"), lax.axis_size("dp") == 4
    tokens, d = gm.shape
    qw = a.shape[1] // n
    slot = dkv.shape[1:]
    dma = pltpu.SemaphoreType.DMA
    vmem = pl.BlockSpec(memory_space=pltpu.VMEM)
    return pl.pallas_call(
        functools.partial(attention_grads_kernel, orders=orders, line=line, qw=qw),
        in_specs=[vmem] * 5,
        out_specs=[vmem] * 3,
        out_shape=[
            jax.ShapeDtypeStruct((qw, d), F32),
            jax.ShapeDtypeStruct((qw, d), F32),
            jax.ShapeDtypeStruct(slot, BF),
        ],
        scratch_shapes=[
            pltpu.VMEM((2, 2, n, qw, d // 2), BF),
            pltpu.VMEM((2, 2, n - 1, qw, d // 2), BF),
            pltpu.VMEM((n,) + slot, BF),
            pltpu.VMEM((n - 1,) + slot, BF),
            pltpu.VMEM((2, 2, 4, qw, d // 2), BF),
            dma((2, 2, n)), dma((2, 2, n)), dma((n,)), dma((n,)), dma((2, 2, 6)),
        ],
        compiler_params=pltpu.CompilerParams(
            collective_id=1, has_side_effects=True, vmem_limit_bytes=60 * MIB
        ),
        cost_estimate=pl.CostEstimate(
            flops=4 * tokens * n * qw * d, bytes_accessed=64 * MIB, transcendentals=0
        ),
    )(a, gm, dq, h, dkv)


def mlp_kernel(xa_ref, xb_ref, ca_ref, cb_ref, up_ref, bias_ref, down_ref,
               ffa_ref, ffb_ref, gna_ref, gnb_ref, act_ref, gr_ref, gb_ref, x_s, c_s, ff_s, gn_s):
    step = pl.program_id(0)
    half = xa_ref.shape[0]

    @pl.when(step == 0)
    def _():
        x_s[:half] = xa_ref[...]
        x_s[half:] = xb_ref[...]
        c_s[:half] = ca_ref[...]
        c_s[half:] = cb_ref[...]

    raised = dot(x_s[...], up_ref[...]) + bias_ref[...]
    square = raised * raised
    th = jnp.tanh(0.7978845608028654 * raised * (1.0 + 0.044715 * square))
    act = (0.5 * raised * (1.0 + th)).astype(BF)
    act_ref[...] = act
    ff = dot(act, down_ref[...])
    slope = 0.5 * (1.0 + th) + 0.5 * raised * (1.0 - th * th) * (
        0.7978845608028654 * (1.0 + 3 * 0.044715 * square)
    )
    gr32 = dot_nt(c_s[...], down_ref[...]) * slope
    gr = gr32.astype(BF)
    gr_ref[...] = gr
    gb_ref[...] = jnp.sum(gr.astype(F32), axis=0, keepdims=True)
    gn = dot_nt(gr, up_ref[...])

    @pl.when(step == 0)
    def _():
        ff_s[...] = ff
        gn_s[...] = gn

    @pl.when(step != 0)
    def _():
        ff_s[...] += ff
        gn_s[...] += gn

    @pl.when(step == pl.num_programs(0) - 1)
    def _():
        ffa_ref[...] = ff_s[:half].astype(BF)
        ffb_ref[...] = ff_s[half:].astype(BF)
        gna_ref[...] = gn_s[:half].astype(BF)
        gnb_ref[...] = gn_s[half:].astype(BF)


def mlp_unit(xa, xb, ca, cb, up, bias, down):
    half, d = xa.shape
    ff = up.shape[1]
    tile = min(512, ff)
    tokens = 2 * half
    whole = pl.BlockSpec((half, d), lambda j: (0, 0))
    return pl.pallas_call(
        mlp_kernel,
        grid=(ff // tile,),
        in_specs=[
            whole, whole, whole, whole,
            pl.BlockSpec((d, tile), lambda j: (0, j)),
            pl.BlockSpec((1, tile), lambda j: (0, j)),
            pl.BlockSpec((tile, d), lambda j: (j, 0)),
        ],
        out_specs=[
            whole, whole, whole, whole,
            pl.BlockSpec((tokens, tile), lambda j: (0, j)),
            pl.BlockSpec((tokens, tile), lambda j: (0, j)),
            pl.BlockSpec((1, tile), lambda j: (0, j)),
        ],
        out_shape=[jax.ShapeDtypeStruct((half, d), BF)] * 4
        + [jax.ShapeDtypeStruct((tokens, ff), BF)] * 2
        + [jax.ShapeDtypeStruct((1, ff), F32)],
        scratch_shapes=[
            pltpu.VMEM((tokens, d), BF),
            pltpu.VMEM((tokens, d), BF),
            pltpu.VMEM((tokens, d), F32),
            pltpu.VMEM((tokens, d), F32),
        ],
        compiler_params=pltpu.CompilerParams(vmem_limit_bytes=56 * MIB),
        cost_estimate=pl.CostEstimate(
            flops=8 * tokens * d * ff, bytes_accessed=20 * MIB, transcendentals=tokens * ff
        ),
    )(xa, xb, ca, cb, up, bias, down)


def norm_parts(values):
    center = values - jnp.mean(values, axis=-1, keepdims=True)
    scale = lax.rsqrt(jnp.mean(center * center, axis=-1, keepdims=True) + EPSILON)
    return center * scale, scale


def norm_back(unit, scale, gain, grad):
    e = gain * grad
    back = scale * (e - jnp.mean(e, axis=-1, keepdims=True) - unit * jnp.mean(e * unit, axis=-1, keepdims=True))
    return back, jnp.sum(grad * unit, axis=(0, 1)), jnp.sum(grad, axis=(0, 1))


def body(
    inputs, cotangent, documents, padding, attn_gain, attn_shift, query_matrix, query_bias, shared_matrix,
    value_bias, output_matrix, output_bias, mlp_gain, mlp_shift, expansion_weights, up_bias, down_matrix, down_bias,
):
    n = lax.axis_size("tensor")
    me = lax.axis_index("tensor")
    hd = value_bias.shape[0]
    seqs, span, d = inputs.shape
    length = documents.shape[1]
    qw = query_matrix.shape[1]
    heads = qw // hd
    scale = hd**-0.5
    paths = bit_orders(n)
    tokens = seqs * span

    x32 = inputs.astype(F32)
    unit1, scale1 = norm_parts(x32)
    hidden = (unit1 * attn_gain + attn_shift).astype(BF)
    h2 = hidden.reshape(tokens, d)
    shared = dot(h2, shared_matrix)
    kv_own = jnp.concatenate([shared[:, :hd], shared[:, hd:] + value_bias], axis=1).astype(BF)
    kv_own = kv_own.reshape(seqs, span, 2 * hd)
    kv = jnp.concatenate(gather_slots(kv_own, paths[0]), axis=1)
    keys, values = kv[..., :hd], kv[..., hd:]
    keys_t, values_t = keys.swapaxes(1, 2), values.swapaxes(1, 2)

    half = d // 2
    wq = [gather_slots(query_matrix[i * half : (i + 1) * half], paths[i]) for i in range(2)]
    wo = [gather_slots(output_matrix[:, i * half : (i + 1) * half], paths[i]) for i in range(2)]
    bq = jnp.concatenate(gather_slots(query_bias[None], paths[0]), axis=1)

    like = lambda t, cols: jax.ShapeDtypeStruct((tokens, cols), t)
    (query,) = slot_product(
        functools.partial(q_kernel, factor=scale * LOG2E), [h2], [bq], wq, [like(BF, n * qw)], (d, n * qw)
    )
    query = query.reshape(seqs, span, n * qw)
    first = lax.dynamic_slice_in_dim(documents, me * span, 1, 1)
    low = (jnp.sum((documents < first).astype(jnp.int32), axis=1) // span).astype(jnp.int32)
    low = jnp.minimum(low, me)
    at = me.reshape(1).astype(jnp.int32)
    dock = jnp.where(padding == 1, documents, -1)
    dock = xor_order(dock.reshape(seqs, n, span).swapaxes(0, 1), me).swapaxes(0, 1).reshape(seqs, length, 1)
    docq = lax.dynamic_slice_in_dim(documents, me * span, span, 1)
    docq = jnp.concatenate([docq] * heads, axis=1)[:, None, :]
    attended, lse = attention_fwd(query, keys, values_t, low, at, dock, docq, heads, hd)
    a2 = attended.reshape(tokens, n * qw)
    mixed, normed = slot_product(
        o_kernel, [a2, inputs.reshape(tokens, d)], [output_bias[None], mlp_gain[None], mlp_shift[None]], wo,
        [like(F32, d), like(BF, d)], (n * qw, d),
    )
    mixed, normed = mixed.reshape(seqs, span, d), normed.reshape(seqs, span, d)
    unit2, scale2 = norm_parts(mixed)

    cot_slots = [gather_slots(cotangent[r], paths[r % 2]) for r in range(seqs)]
    normed_slots = [gather_slots(normed[r], paths[r % 2]) for r in range(seqs)]
    ff_slots = [[None] * n for _ in range(seqs)]
    gn_slots = [[None] * n for _ in range(seqs)]
    acts, grs, xs, cs = [], [], [], []
    up_bias_part = jnp.zeros((1, up_bias.shape[0]), F32)
    for k in range(0, n, 2):
        for r in range(seqs):
            xa, xb, ca, cb = normed_slots[r][k], normed_slots[r][k + 1], cot_slots[r][k], cot_slots[r][k + 1]
            ffa, ffb, gna, gnb, act, gr, gb = mlp_unit(
                xa, xb, ca, cb, expansion_weights, up_bias[None], down_matrix
            )
            ff_slots[r][k], ff_slots[r][k + 1] = ffa, ffb
            gn_slots[r][k], gn_slots[r][k + 1] = gna, gnb
            acts.append(act)
            grs.append(gr)
            xs.append([xa, xb])
            cs.append([ca, cb])
            up_bias_part = up_bias_part + gb
    grad_normed = jnp.stack([scatter_slots(gn_slots[r], paths[r % 2]) for r in range(seqs)])
    down_gradient = weight_grad([[a] for a in acts], cs)
    up_gradient = weight_grad(xs, [[g] for g in grs])
    mlp_branch = jnp.stack([scatter_slots(ff_slots[r], paths[r % 2]) for r in range(seqs)])
    block_out = (mixed + mlp_branch + down_bias).astype(BF)

    cot_wide = cotangent.astype(F32)
    back2, mlp_gain_part, mlp_shift_part = norm_back(unit2, scale2, mlp_gain, grad_normed)
    grad_mixed = cot_wide + back2
    gm2 = grad_mixed.astype(BF).reshape(tokens, d)
    (grad_attended,) = slot_product(do_kernel, [gm2], [], wo, [like(BF, n * qw)], (n * qw, d))
    grad_attended = grad_attended.reshape(seqs, span, n * qw)
    dq, dk, dv = attention_bwd(
        query, grad_attended, attended, lse, keys, keys_t, values, low, at, dock, docq, heads, hd, scale
    )
    dq2 = dq.reshape(tokens, n * qw)

    dkv = jnp.concatenate([dk * LN2, dv], axis=-1).astype(BF).reshape(seqs, n, span, 2 * hd).swapaxes(0, 1)
    output_gradient, query_gradient, dkv_own = attention_grads(
        a2, gm2, dq2, h2, dkv.reshape(n, tokens, 2 * hd), paths
    )
    if lax.axis_size("dp") != 4:
        output_gradient, query_gradient = lax.psum((output_gradient.astype(BF), query_gradient.astype(BF)), "dp")
    dkv_own = dkv_own.reshape(seqs, span, 2 * hd)

    (grad_hidden,) = slot_product(
        dh_kernel, [dq2, dkv_own.reshape(tokens, 2 * hd)], [shared_matrix], wq, [like(F32, d)], (d, n * qw)
    )
    grad_hidden = grad_hidden.reshape(seqs, span, d)
    back1, attn_gain_part, attn_shift_part = norm_back(unit1, scale1, attn_gain, grad_hidden)
    input_grad = grad_mixed + back1
    shared_part = dot_tn(h2, dkv_own.reshape(tokens, 2 * hd))
    value_bias_part = jnp.sum(dkv_own[..., hd:].astype(F32), axis=(0, 1))
    query_bias_part = xor_order(jnp.sum(dq2.astype(F32), axis=0).reshape(n, qw), me).reshape(-1)

    everywhere = ("tensor", "dp")
    down_gradient, up_gradient = lax.psum((down_gradient, up_gradient), "dp")
    up_bias_grad = sum_all(up_bias_part, ("dp",))[0]
    early = sum_all(
        jnp.stack([mlp_gain_part, mlp_shift_part, jnp.sum(grad_mixed, axis=(0, 1)), jnp.sum(cot_wide, axis=(0, 1))]),
        everywhere,
    )
    mlp_gain_grad, mlp_shift_grad, output_bias_grad, down_bias_grad = early
    late = sum_all(
        jnp.concatenate([attn_gain_part, attn_shift_part, query_bias_part, value_bias_part])[None], everywhere
    )[0]
    attn_gain_grad, attn_shift_grad = late[:d], late[d : 2 * d]
    query_bias_grad = lax.dynamic_slice_in_dim(late, 2 * d + me * qw, qw, 0)
    value_bias_grad = late[2 * d + n * qw :]
    piece = d // n
    shared_slots = [
        lax.dynamic_slice_in_dim(shared_part, (me ^ k) * piece, piece, 0).astype(BF) for k in range(n)
    ]
    shared_sum = sum_all(scatter_slots(shared_slots, paths[0]), ("dp",)).astype(BF)
    shared_slots = jnp.concatenate(gather_slots(shared_sum, paths[0]), axis=0)
    shared_grad = xor_order(shared_slots.reshape(n, piece, 2 * hd), me).reshape(d, 2 * hd).astype(F32)
    output_gradient, query_gradient, up_gradient, down_gradient = (
        g.astype(F32) for g in (output_gradient, query_gradient.T, up_gradient, down_gradient)
    )
    return (
        block_out, input_grad, attn_gain_grad, attn_shift_grad, query_gradient, query_bias_grad, shared_grad,
        value_bias_grad, output_gradient, output_bias_grad, mlp_gain_grad, mlp_shift_grad, up_gradient, up_bias_grad,
        down_gradient, down_bias_grad,
    )


def solution(mesh):
    act = P("dp", "tensor", None)
    cols, rows, vec, rep = P(None, "tensor"), P("tensor", None), P("tensor"), P()
    ids = P("dp", None)
    return jax.shard_map(
        body,
        mesh=mesh,
        in_specs=(act, act, ids, ids, rep, rep, cols, vec, rep, rep, rows, rep, rep, rep, cols, vec, rows, rep),
        out_specs=(act, act, rep, rep, cols, vec, rep, rep, rows, rep, rep, rep, cols, vec, rows, rep),
        check_vma=False,
    )
```

```python
import functools

import jax
import jax.numpy as jnp
from jax import lax
from jax.experimental import pallas as pl
from jax.experimental.pallas import tpu as pltpu
from jax.sharding import PartitionSpec as P

EPSILON = 1e-05
LOG2E = 1.4426950408889634
LN2 = 0.6931471805599453
BF = jnp.bfloat16
F32 = jnp.float32
NEG = -1e30
MIB = 1024 * 1024


def dot(a, b):
    return lax.dot_general(a, b, (((1,), (0,)), ((), ())), preferred_element_type=F32)


def dot_nt(a, b):
    return lax.dot_general(a, b, (((1,), (1,)), ((), ())), preferred_element_type=F32)


def dot_tn(a, b):
    return lax.dot_general(a, b, (((0,), (0,)), ((), ())), preferred_element_type=F32)


def swap(x, bit, axis="tensor"):
    n = lax.axis_size(axis)
    return lax.ppermute(x, axis, [(i, i ^ (1 << bit)) for i in range(n)])


def bit_orders(n):
    bits = list(range(1, n.bit_length() - 1))
    return bits, bits[::-1]


def gather_slots(block, order):
    held = {0: block}
    for bit in list(order) + [0]:
        held.update({k | (1 << bit): swap(v, bit) for k, v in list(held.items())})
    return [held[k] for k in range(len(held))]


def scatter_slots(slots, order):
    held = dict(enumerate(slots))
    for bit in [0] + list(order)[::-1]:
        for k in sorted(held, reverse=True):
            if k & (1 << bit):
                arrived = swap(held.pop(k).astype(BF), bit)
                low = k ^ (1 << bit)
                held[low] = held[low].astype(F32) + arrived.astype(F32)
        held = {k: (v if len(held) == 1 else v.astype(BF)) for k, v in held.items()}
    return held[0].astype(F32)


def xor_order(x, me):
    n = x.shape[0]
    rest = x.shape[1:]
    for bit in range(n.bit_length() - 1):
        pairs = x.reshape((n >> (bit + 1), 2, 1 << bit) + rest)
        x = jnp.where((me >> bit) & 1 == 1, jnp.flip(pairs, 1), pairs).reshape((n,) + rest)
    return x


def stack_heads(block, heads, hd):
    return jnp.concatenate([block[:, i * hd : (i + 1) * hd] for i in range(heads)], axis=0)


def diagonal_mask(rows, cols, same):
    key_at = lax.broadcasted_iota(jnp.int32, (rows, cols), 0)
    query_at = lax.broadcasted_iota(jnp.int32, (rows, cols), 1) % rows
    return (same & (key_at < query_at)) | (key_at == query_at)


def below_blocks(low, at, step, carry):
    even = at - at % 2
    carry = lax.fori_loop(jnp.maximum(low, even), at, lambda b, c: step(b ^ at, 1, c), carry)
    return lax.fori_loop(low // 2, at // 2, lambda p, c: step((p ^ (at // 2)) * 2, 2, c), carry)


def attention_fwd_kernel(low_ref, at_ref, q_ref, k_ref, vt_ref, dock_ref, docq_ref, o_ref, lse_ref, *, heads, hd):
    row = pl.program_id(0)
    span = q_ref.shape[1]
    at = at_ref[0]
    q2 = stack_heads(q_ref[0], heads, hd)
    docq = docq_ref[0]

    def scores(slot, count):
        here = pl.ds(pl.multiple_of(slot * span, count * span), count * span)
        s = dot_nt(k_ref[0, here, :], q2)
        same = dock_ref[0, here, :] == docq
        return s, same, here

    s, same, here = scores(0, 1)
    s = jnp.where(diagonal_mask(span, heads * span, same), s, NEG)
    top = jnp.max(s, axis=0, keepdims=True)
    p = jnp.exp2(s - top)
    total = jnp.sum(p, axis=0, keepdims=True)
    acc = dot(vt_ref[0, :, here], p.astype(BF))

    def step(slot, count, carry):
        top, total, acc = carry
        s, same, here = scores(slot, count)
        s = jnp.where(same, s, NEG)
        new = jnp.maximum(top, jnp.max(s, axis=0, keepdims=True))
        shrink = jnp.exp2(top - new)
        p = jnp.exp2(s - new)
        total = total * shrink + jnp.sum(p, axis=0, keepdims=True)
        acc = acc * shrink + dot(vt_ref[0, :, here], p.astype(BF))
        return new, total, acc

    carry = below_blocks(low_ref[row], at, step, (top, total, acc))
    top, total, acc = carry
    out = (acc / total).T.astype(BF)
    for i in range(heads):
        o_ref[0, :, i * hd : (i + 1) * hd] = out[i * span : (i + 1) * span]
    lse_ref[0, 0] = top + jnp.log2(total)


def attention_bwd_kernel(
    low_ref, at_ref, q_ref, do_ref, o_ref, lse_ref, k_ref, kt_ref, v_ref, dock_ref, docq_ref,
    dq_ref, dk_ref, dv_ref, *, heads, hd, scale,
):
    row = pl.program_id(0)
    span = q_ref.shape[1]
    at = at_ref[0]

    @pl.when(pl.program_id(1) == 0)
    def _():
        dk_ref[...] = jnp.zeros_like(dk_ref)
        dv_ref[...] = jnp.zeros_like(dv_ref)

    q2 = stack_heads(q_ref[0], heads, hd)
    do2 = stack_heads(do_ref[0], heads, hd)
    o2 = stack_heads(o_ref[0], heads, hd)
    delta = jnp.sum((do2.astype(F32) * o2.astype(F32)).T, axis=0, keepdims=True)
    lse = lse_ref[0, 0]
    docq = docq_ref[0]

    def one(slot, count, dqt, diagonal=False):
        here = pl.ds(pl.multiple_of(slot * span, count * span), count * span)
        s = dot_nt(k_ref[0, here, :], q2)
        same = dock_ref[0, here, :] == docq
        if diagonal:
            same = diagonal_mask(span, heads * span, same)
        p = jnp.where(same, jnp.exp2(s - lse), 0.0)
        dp = dot_nt(v_ref[0, here, :], do2)
        ds = (p * (dp - delta)).astype(BF)
        dk_ref[0, here, :] += dot(ds, q2)
        dv_ref[0, here, :] += dot(p.astype(BF), do2)
        return dqt + dot(kt_ref[0, :, here], ds)

    dqt = one(0, 1, jnp.zeros((hd, heads * span), F32), True)
    dqt = below_blocks(low_ref[row], at, one, dqt)
    dq = (dqt * scale).T.astype(BF)
    for i in range(heads):
        dq_ref[0, :, i * hd : (i + 1) * hd] = dq[i * span : (i + 1) * span]


def attention_fwd(q, k, vt, low, at, dock, docq, heads, hd):
    rows, span, width = q.shape
    length = k.shape[1]
    groups = width // (heads * hd)
    gw = heads * hd
    return pl.pallas_call(
        functools.partial(attention_fwd_kernel, heads=heads, hd=hd),
        grid_spec=pltpu.PrefetchScalarGridSpec(
            num_scalar_prefetch=2,
            grid=(rows, groups),
            in_specs=[
                pl.BlockSpec((1, span, gw), lambda r, g, *_: (r, 0, g)),
                pl.BlockSpec((1, length, hd), lambda r, g, *_: (r, 0, 0)),
                pl.BlockSpec((1, hd, length), lambda r, g, *_: (r, 0, 0)),
                pl.BlockSpec((1, length, 1), lambda r, g, *_: (r, 0, 0)),
                pl.BlockSpec((1, 1, heads * span), lambda r, g, *_: (r, 0, 0)),
            ],
            out_specs=[
                pl.BlockSpec((1, span, gw), lambda r, g, *_: (r, 0, g)),
                pl.BlockSpec((1, 1, 1, heads * span), lambda r, g, *_: (r, g, 0, 0)),
            ],
        ),
        out_shape=[
            jax.ShapeDtypeStruct((rows, span, width), BF),
            jax.ShapeDtypeStruct((rows, groups, 1, heads * span), F32),
        ],
        compiler_params=pltpu.CompilerParams(vmem_limit_bytes=24 * MIB),
        cost_estimate=pl.CostEstimate(
            flops=2 * rows * span * width * length, bytes_accessed=8 * MIB, transcendentals=rows * span * length
        ),
    )(low, at, q, k, vt, dock, docq)


def attention_bwd(q, do, o, lse, k, kt, v, low, at, dock, docq, heads, hd, scale):
    rows, span, width = q.shape
    length = k.shape[1]
    groups = width // (heads * hd)
    gw = heads * hd
    blk = pl.BlockSpec((1, span, gw), lambda r, g, *_: (r, 0, g))
    full = pl.BlockSpec((1, length, hd), lambda r, g, *_: (r, 0, 0))
    return pl.pallas_call(
        functools.partial(attention_bwd_kernel, heads=heads, hd=hd, scale=scale),
        grid_spec=pltpu.PrefetchScalarGridSpec(
            num_scalar_prefetch=2,
            grid=(rows, groups),
            in_specs=[
                blk,
                blk,
                blk,
                pl.BlockSpec((1, 1, 1, heads * span), lambda r, g, *_: (r, g, 0, 0)),
                full,
                pl.BlockSpec((1, hd, length), lambda r, g, *_: (r, 0, 0)),
                full,
                pl.BlockSpec((1, length, 1), lambda r, g, *_: (r, 0, 0)),
                pl.BlockSpec((1, 1, heads * span), lambda r, g, *_: (r, 0, 0)),
            ],
            out_specs=[blk, full, full],
        ),
        out_shape=[
            jax.ShapeDtypeStruct((rows, span, width), BF),
            jax.ShapeDtypeStruct((rows, length, hd), F32),
            jax.ShapeDtypeStruct((rows, length, hd), F32),
        ],
        compiler_params=pltpu.CompilerParams(vmem_limit_bytes=32 * MIB),
        cost_estimate=pl.CostEstimate(
            flops=1000, bytes_accessed=MIB, transcendentals=0
        ),
    )(low, at, q, do, o, lse, k, kt, v, dock, docq)


def fill(whole_ref, parts, axis):
    for i, slots in enumerate(parts):
        for k, part in enumerate(slots):
            rows, cols = part.shape
            if axis == 1:
                whole_ref[i * rows : (i + 1) * rows, k * cols : (k + 1) * cols] = part[...]
            else:
                whole_ref[k * rows : (k + 1) * rows, i * cols : (i + 1) * cols] = part[...]


def split_parts(refs):
    count = len(refs) // 2
    return [refs[:count], refs[count:]]


def q_kernel(x_ref, b_ref, *refs, factor):
    *parts, o_ref, w_s = refs

    @pl.when(pl.program_id(0) == 0)
    def _():
        fill(w_s, split_parts(parts), 1)

    o_ref[...] = ((dot(x_ref[...], w_s[...]) + b_ref[...]) * factor).astype(BF)


def o_kernel(a_ref, x_ref, b_ref, gain_ref, shift_ref, *refs):
    *parts, mixed_ref, normed_ref, w_s = refs

    @pl.when(pl.program_id(0) == 0)
    def _():
        fill(w_s, split_parts(parts), 0)

    mixed = x_ref[...].astype(F32) + dot(a_ref[...], w_s[...]) + b_ref[...]
    mixed_ref[...] = mixed
    unit, _ = norm_parts(mixed)
    normed_ref[...] = (unit * gain_ref[...] + shift_ref[...]).astype(BF)


def do_kernel(g_ref, *refs):
    *parts, o_ref, w_s = refs

    @pl.when(pl.program_id(0) == 0)
    def _():
        fill(w_s, split_parts(parts), 0)

    o_ref[...] = dot_nt(g_ref[...], w_s[...]).astype(BF)


def slot_product(kernel, tiled, fixed, parts, outs, shape):
    flat = parts[0] + parts[1]
    tokens = tiled[0].shape[0]
    tile = tokens // 2
    still = lambda a: pl.BlockSpec(a.shape, lambda i: (0, 0), pipeline_mode=pl.Buffered(1))
    flow = lambda a: pl.BlockSpec((tile, a.shape[1]), lambda i: (i, 0))
    result = pl.pallas_call(
        kernel,
        grid=(2,),
        in_specs=[flow(a) for a in tiled] + [still(a) for a in fixed] + [still(a) for a in flat],
        out_specs=[flow(o) for o in outs],
        out_shape=outs,
        scratch_shapes=[pltpu.VMEM(shape, BF)],
        compiler_params=pltpu.CompilerParams(vmem_limit_bytes=48 * MIB),
        cost_estimate=pl.CostEstimate(
            flops=2 * tokens * shape[0] * shape[1], bytes_accessed=2 * shape[0] * shape[1] + 8 * MIB, transcendentals=0
        ),
    )(*tiled, *fixed, *flat)
    return result


def after_kernel(x_ref, *refs):
    refs[-1][...] = x_ref[...]


def after(x, *first):
    return pl.pallas_call(
        after_kernel,
        in_specs=[pl.BlockSpec(memory_space=pltpu.VMEM)] + [pl.BlockSpec(memory_space=pl.ANY)] * len(first),
        out_specs=pl.BlockSpec(memory_space=pltpu.VMEM),
        out_shape=jax.ShapeDtypeStruct(x.shape, x.dtype),
    )(x, *first)


MESH = pl.DeviceIdType.MESH


def greet(bits, line=False, dp_bits=()):
    me, z = lax.axis_index("tensor"), lax.axis_index("dp")
    barrier = pltpu.get_barrier_semaphore()
    for bit in bits:
        pl.semaphore_signal(barrier, inc=1, device_id={"tensor": me ^ (1 << bit)}, device_id_type=MESH)
    count = len(bits)
    flips = {1 << bit for bit in dp_bits} | ({1} if line else set())
    for flip in sorted(flips):
        pl.semaphore_signal(barrier, inc=1, device_id={"dp": z ^ flip}, device_id_type=MESH)
    count += len(flips)
    if line:
        inner = (z == 1) | (z == 2)

        @pl.when(inner)
        def _():
            pl.semaphore_signal(barrier, inc=1, device_id={"dp": 3 - z}, device_id_type=MESH)

        count = count + inner.astype(jnp.int32)
    pl.semaphore_wait(barrier, count)


class Line:
    def __init__(self, own, near, far, sem):
        self.own, self.near, self.far, self.sem = own, near, far, sem
        self.z = lax.axis_index("dp")
        self.inner = (self.z == 1) | (self.z == 2)
        self.outer = jnp.logical_not(self.inner)

    def copy(self, i, hop):
        src = (self.own, self.near, self.near)[hop].at[i]
        dst = (self.near, self.far, self.near)[hop].at[i]
        return pltpu.make_async_remote_copy(
            src_ref=src, dst_ref=dst, send_sem=self.sem.at[0, hop, i], recv_sem=self.sem.at[1, hop, i],
            device_id={"dp": 3 - self.z if hop == 1 else self.z ^ 1}, device_id_type=MESH,
        )

    def start(self, i):
        @pl.when(self.outer)
        def _():
            self.copy(i, 0).start()

    def middle(self, i, own):
        @pl.when(self.inner)
        def _():
            self.copy(i, 0).wait_recv()
            self.near[i] = (own().astype(F32) + self.near[i].astype(F32)).astype(BF)
            self.copy(i, 1).start()

    def back(self, i):
        @pl.when(self.inner)
        def _():
            self.copy(i, 1).wait()
            self.near[i] = (self.near[i].astype(F32) + self.far[i].astype(F32)).astype(BF)
            self.copy(i, 2).start()

    def close(self, i):
        @pl.when(self.outer)
        def _():
            self.copy(i, 0).wait_send()
            self.copy(i, 2).wait_recv()

        @pl.when(self.inner)
        def _():
            self.copy(i, 2).wait_send()


class Scatter:
    def __init__(self, bits, send, recv, send_sem, recv_sem, shared=0):
        self.bits, self.send, self.recv, self.send_sem, self.recv_sem = bits, send, recv, send_sem, recv_sem
        self.me = lax.axis_index("tensor")
        self.shared = shared
        self.busy = {}

    def place(self, k):
        if not self.shared:
            return k
        return k // 2 if k % 2 == 0 else (1 << len(self.bits)) // 2 + k // 2 % self.shared

    def claim(self, k):
        place = self.place(k)
        if place in self.busy:
            self.copy(self.busy.pop(place)).wait_send()
        return self.send.at[place]

    def launch(self, k):
        self.copy(k).start()
        self.busy[self.place(k)] = k

    def stage(self, k):
        return next((i for i, b in enumerate(self.bits) if k >> b & 1), len(self.bits))

    def copy(self, k):
        bit = self.bits[self.stage(k)]
        return pltpu.make_async_remote_copy(
            src_ref=self.send.at[self.place(k)],
            dst_ref=self.recv.at[k - 1],
            send_sem=self.send_sem.at[k],
            recv_sem=self.recv_sem.at[k],
            device_id={"tensor": self.me ^ (1 << bit)},
            device_id_type=MESH,
        )

    def put(self, k, value):
        self.claim(k)[...] = value.astype(BF)
        if self.stage(k) == 0:
            self.launch(k)

    def total(self, k):
        value = self.send[self.place(k)].astype(F32)
        for bit in self.bits[: self.stage(k)]:
            self.copy(k | (1 << bit)).wait_recv()
            value = value + self.recv[(k | (1 << bit)) - 1].astype(F32)
        return value

    def forward(self, k):
        self.send[self.place(k)] = self.total(k).astype(BF)
        self.launch(k)

    def drain(self):
        for k in self.busy.values():
            self.copy(k).wait_send()
        self.busy = {}


def scatter_order(bits):
    n = 1 << len(bits)
    rank = lambda k: next(i for i, b in enumerate(bits) if k >> b & 1)
    return sorted(range(2, n, 2), key=lambda k: (rank(k), -k))


def attention_grads_kernel(a_ref, gm_ref, dq_ref, h_ref, dkv_ref, wo_ref, wq_ref, kv_ref,
                           send, recv, ksend, krecv, ssem, rsem, ksem, krsem, *, orders, qw):
    bits_of = [[0] + list(o)[::-1] for o in orders]
    count = len(bits_of[0])
    n = 1 << count
    half = gm_ref.shape[1] // 2
    greet(range(count))
    kv = Scatter(bits_of[0], ksend, krecv, ksem, krsem)
    for k in list(range(1, n, 2)) + list(range(0, n, 2)):
        kv.put(k, dkv_ref[k])

    pairs = ((a_ref, gm_ref, wo_ref), (dq_ref, h_ref, wq_ref))
    work = [
        [Scatter(bits_of[p], send.at[m, p], recv.at[m, p], ssem.at[m, p], rsem.at[m, p], shared=2) for p in range(2)]
        for m in range(2)
    ]
    sequence = [scatter_order(b) for b in bits_of]

    def products(m):
        x, y, _ = pairs[m]
        for i in range(n // 2):
            for p in range(2):
                k = (sequence[p] + [0])[i]
                for j in (k + 1, k):
                    work[m][p].put(j, dot_tn(x[:, j * qw : (j + 1) * qw], y[:, p * half : (p + 1) * half]))

    def stage(m, i):
        for at in range(n // 2 - 1):
            for p in range(2):
                k = sequence[p][at]
                if work[m][p].stage(k) == i:
                    work[m][p].forward(k)

    def kv_stage(i):
        for k in scatter_order(bits_of[0]):
            if kv.stage(k) == i:
                kv.forward(k)

    def finish(m):
        for p in range(2):
            pairs[m][2][p] = work[m][p].total(0).astype(BF)

    products(0)
    stage(0, 1)
    products(1)
    for i in range(1, count):
        kv_stage(i)
        if i + 1 < count:
            stage(0, i + 1)
        else:
            finish(0)
        stage(1, i)
    kv_ref[...] = kv.total(0).astype(BF)
    finish(1)
    kv.drain()
    for m in range(2):
        for p in range(2):
            work[m][p].drain()


def attention_grads(a, gm, dq, h, dkv, orders):
    n = lax.axis_size("tensor")
    tokens, d = gm.shape
    qw = a.shape[1] // n
    slot = dkv.shape[1:]
    dma = pltpu.SemaphoreType.DMA
    vmem = pl.BlockSpec(memory_space=pltpu.VMEM)
    return pl.pallas_call(
        functools.partial(attention_grads_kernel, orders=orders, qw=qw),
        in_specs=[vmem] * 5,
        out_specs=[vmem] * 3,
        out_shape=[
            jax.ShapeDtypeStruct((2, qw, d // 2), BF),
            jax.ShapeDtypeStruct((2, qw, d // 2), BF),
            jax.ShapeDtypeStruct(slot, BF),
        ],
        scratch_shapes=[
            pltpu.VMEM((2, 2, n // 2 + 2, qw, d // 2), BF),
            pltpu.VMEM((2, 2, n - 1, qw, d // 2), BF),
            pltpu.VMEM((n,) + slot, BF),
            pltpu.VMEM((n - 1,) + slot, BF),
            dma((2, 2, n)), dma((2, 2, n)), dma((n,)), dma((n,)),
        ],
        compiler_params=pltpu.CompilerParams(
            collective_id=1, has_side_effects=True, vmem_limit_bytes=60 * MIB
        ),
        cost_estimate=pl.CostEstimate(flops=1000, bytes_accessed=MIB, transcendentals=0),
    )(a, gm, dq, h, dkv)


def last_kernel(wo_ref, wq_ref, dq_ref, kv_ref, shared_ref, h_ref, x_ref, gain_ref, mixed_ref, qb_ref, *refs,
                order, line, eps_rows):
    count = len(order) + 1
    n = 1 << count
    parts = refs[: 2 * n]
    (wog_ref, wqg_ref, grad_ref, late_ref, sg_ref,
     w_s, near, far, part, send, recv, dsend, drecv, piece_s, gathered, vsend, vrecv,
     zsem, ssem, rsem, dsem, gsem, vsem) = refs[2 * n :]
    me, z = lax.axis_index("tensor"), lax.axis_index("dp")
    dp_bits = range(lax.axis_size("dp").bit_length() - 1)
    tokens, d = x_ref.shape
    hd = kv_ref.shape[1] // 2
    piece = d // n
    greet(range(count), line, dp_bits)

    owns = [wo_ref.at[0], wo_ref.at[1], wq_ref.at[0], wq_ref.at[1]]
    chains = []
    if line:
        for i, ref in enumerate((wo_ref, wq_ref)):
            c = Line(ref, near.at[i], far.at[i], zsem.at[i])
            c.values = [lambda ref=ref, p=p: ref[p] for p in range(2)]
            chains.append(c)
            for p in range(2):
                c.start(p)

    ahead = [0, 0]

    def chain_to(middles, backs):
        while line and ahead[0] < min(middles, 4):
            i, p = divmod(ahead[0], 2)
            chains[i].middle(p, chains[i].values[p])
            ahead[0] += 1
        while line and ahead[1] < min(backs, 4):
            i, p = divmod(ahead[1], 2)
            chains[i].back(p)
            ahead[1] += 1

    part[...] = dot_tn(h_ref[...], kv_ref[...])
    scatter = Scatter([0] + list(order)[::-1], send, recv, ssem, rsem)
    for k in list(range(1, n, 2)) + list(range(0, n, 2)):
        scatter.put(k, part[pl.ds(pl.multiple_of((me ^ k) * piece, piece), piece), :])
    fill(w_s, split_parts(parts), 1)
    for i in range(1, count):
        for k in scatter_order(scatter.bits):
            if scatter.stage(k) == i:
                scatter.forward(k)
    chain_to(1, 0)

    gain_part, shift_part = jnp.zeros((1, d), F32), jnp.zeros((1, d), F32)
    for t in range(tokens // eps_rows):
        rows = slice(t * eps_rows, (t + 1) * eps_rows)
        grad = dot_nt(dq_ref[rows], w_s[...]) + dot_nt(kv_ref[rows], shared_ref[...])
        unit, scale = norm_parts(x_ref[rows].astype(F32))
        e = gain_ref[...] * grad
        back = e - jnp.mean(e, axis=-1, keepdims=True) - unit * jnp.mean(e * unit, axis=-1, keepdims=True)
        grad_ref[rows] = mixed_ref[rows] + scale * back
        gain_part += jnp.sum(grad * unit, axis=0, keepdims=True)
        shift_part += jnp.sum(grad, axis=0, keepdims=True)
        chain_to(2 + t, 1 + t)
    at = 0
    for value in (gain_part, shift_part, jnp.sum(kv_ref[:, hd:].astype(F32), axis=0, keepdims=True), qb_ref[...]):
        late_ref[:, at : at + value.shape[1]] = value
        at += value.shape[1]

    hops = [("tensor", me, b) for b in range(count)] + [("dp", z, b) for b in dp_bits]

    def small(buffers, sems, i, axis, at, bit):
        return pltpu.make_async_remote_copy(
            src_ref=buffers[0].at[i], dst_ref=buffers[1].at[i], send_sem=sems.at[0, i], recv_sem=sems.at[1, i],
            device_id={axis: at ^ (1 << bit)}, device_id_type=MESH,
        )

    piece_s[...] = scatter.total(0)
    pending = []
    for i, (axis, at, bit) in enumerate(hops):
        vsend[i] = late_ref[...]
        c = small((vsend, vrecv), vsem, i, axis, at, bit)
        c.start()
        j = i if i < len(dp_bits) else None
        if j is not None:
            dsend[j] = piece_s[...]
            e = small((dsend, drecv), dsem, j, "dp", z, dp_bits[j])
            e.start()
        if i:
            chain_to(3 + i, 2 + i)
        c.wait_recv()
        late_ref[...] = late_ref[...] + vrecv[i]
        pending.append(c)
        if j is not None:
            e.wait_recv()
            piece_s[...] = piece_s[...] + drecv[j]
            pending.append(e)
        if j == len(dp_bits) - 1:
            gathered[me] = piece_s[...].astype(BF)
            held = [0]
    sent = []
    for bit in list(order) + [0]:
        new = []
        for k in held:
            c = pltpu.make_async_remote_copy(
                src_ref=gathered.at[me ^ k], dst_ref=gathered.at[me ^ k], send_sem=gsem.at[0, k | (1 << bit)],
                recv_sem=gsem.at[1, k | (1 << bit)], device_id={"tensor": me ^ (1 << bit)}, device_id_type=MESH,
            )
            c.start()
            sent.append(c)
            new.append(c)
        for c in new:
            c.wait_recv()
        held = held + [k | (1 << bit) for k in held]
    chain_to(4, 4)
    for k in range(n):
        sg_ref[k * piece : (k + 1) * piece] = gathered[k].astype(F32)
    if line:
        for c in chains:
            for p in range(2):
                c.close(p)
    half = d // 2
    for i, ref in enumerate((wog_ref, wqg_ref)):
        for p in range(2):
            value = near[i, p] if line else (wo_ref, wq_ref)[i][p]
            ref[:, p * half : (p + 1) * half] = value.astype(F32)
    for c in pending + sent:
        c.wait_send()
    scatter.drain()


def last(wo, wq, dq, kv, shared, h, x, gain, mixed, qb, parts, order):
    n, dp = lax.axis_size("tensor"), lax.axis_size("dp")
    line = dp == 4
    tokens, d = x.shape
    qw = wo.shape[1]
    flat = parts[0] + parts[1]
    piece, width = d // n, kv.shape[1]
    size = 2 * d + qb.shape[1] + width // 2
    bits = n.bit_length() - 1
    dbits = dp.bit_length() - 1
    dma = pltpu.SemaphoreType.DMA
    vmem = pl.BlockSpec(memory_space=pltpu.VMEM)
    item = (2, 2, qw, d // 2)
    return pl.pallas_call(
        functools.partial(last_kernel, order=order, line=line, eps_rows=tokens // 2),
        in_specs=[vmem] * (10 + len(flat)),
        out_specs=[vmem] * 5,
        out_shape=[
            jax.ShapeDtypeStruct((qw, d), F32),
            jax.ShapeDtypeStruct((qw, d), F32),
            jax.ShapeDtypeStruct((tokens, d), F32),
            jax.ShapeDtypeStruct((1, size), F32),
            jax.ShapeDtypeStruct((d, width), F32),
        ],
        scratch_shapes=[
            pltpu.VMEM((d, n * qw), BF),
            pltpu.VMEM(item, BF),
            pltpu.VMEM(item, BF),
            pltpu.VMEM((d, width), F32),
            pltpu.VMEM((n, piece, width), BF),
            pltpu.VMEM((n - 1, piece, width), BF),
            pltpu.VMEM((dbits, piece, width), F32),
            pltpu.VMEM((dbits, piece, width), F32),
            pltpu.VMEM((piece, width), F32),
            pltpu.VMEM((n, piece, width), BF),
            pltpu.VMEM((bits + dbits, 1, size), F32),
            pltpu.VMEM((bits + dbits, 1, size), F32),
            dma((2, 2, 3, 2)), dma((n,)), dma((n,)), dma((2, dbits)), dma((2, n)), dma((2, bits + dbits)),
        ],
        compiler_params=pltpu.CompilerParams(
            collective_id=4, has_side_effects=True, vmem_limit_bytes=60 * MIB
        ),
        cost_estimate=pl.CostEstimate(flops=1000, bytes_accessed=MIB, transcendentals=0),
    )(wo, wq, dq, kv, shared, h, x, gain, mixed, qb, *flat)


def mlp_kernel(x_ref, cot_ref, up_ref, bias_ref, down_ref, gn_ref, gb_ref, xg_ref, act_ref, gr_ref, *rest, orders):
    n, seqs, span, d = cot_ref.shape
    (ff_ref, x_s, c_s, act_s, gr_s, ff_s, send, recv, gsend, grecv, ssem, rsem, load, own, out) = rest
    hidden = up_ref.shape[1]
    tile, wide = min(512, hidden), 512
    me = lax.axis_index("tensor")
    paths = [list(o) + [0] for o in orders]
    bits_of = [[0] + list(o)[::-1] for o in orders]
    work = [Scatter(bits_of[p], send.at[p], recv.at[p], ssem.at[p], rsem.at[p], shared=2) for p in range(seqs)]

    def last_bit(p, k):
        return max((b for b in paths[p] if k >> b & 1), key=paths[p].index)

    def hop(p, k, bit):
        to = k | (1 << bit)
        src = x_ref.at[p] if k == 0 else xg_ref.at[me ^ k, p]
        return pltpu.make_async_remote_copy(
            src_ref=src, dst_ref=xg_ref.at[me ^ k, p], send_sem=gsend.at[p, to], recv_sem=grecv.at[p, to],
            device_id={"tensor": me ^ (1 << bit)}, device_id_type=MESH,
        )

    def arrival(p, k):
        bit = last_bit(p, k)
        return pltpu.make_async_remote_copy(
            src_ref=x_ref.at[p], dst_ref=xg_ref.at[me ^ k, p], send_sem=gsend.at[p, k], recv_sem=grecv.at[p, k],
            device_id={"tensor": me ^ (1 << bit)}, device_id_type=MESH,
        )

    def slots_at(p, t):
        if t == 0:
            return [0]
        return sorted((k for k in range(2, n, 2) if last_bit(p, k) == paths[p][t - 1]), reverse=True)

    steps = len(paths[0])
    units = [(p, k) for t in range(steps) for i in range(len(slots_at(0, t))) for p in range(seqs) for k in [slots_at(p, t)[i]]]

    def cot_loads(u):
        p, e = units[u]
        return [
            pltpu.make_async_copy(
                cot_ref.at[me ^ (e + j), p], c_s.at[u % 2, j * span : (j + 1) * span], load.at[u % 2, j]
            )
            for j in range(2)
        ]

    def x_loads(u):
        p, e = units[u]
        return [
            pltpu.make_async_copy(
                x_ref.at[p] if e + j == 0 else xg_ref.at[me ^ (e + j), p],
                x_s.at[j * span : (j + 1) * span], load.at[2, j],
            )
            for j in range(2)
        ]

    def hidden_stores(u):
        p, e = units[u]
        return [
            pltpu.make_async_copy(
                buf.at[j * span : (j + 1) * span], ref.at[me ^ (e + j), p], out.at[i, j]
            )
            for i, (buf, ref) in enumerate(((act_s, act_ref), (gr_s, gr_ref)))
            for j in range(2)
        ]

    def ff_stores(u):
        p, e = units[u]
        return [
            pltpu.make_async_copy(ff_s.at[j * span : (j + 1) * span], ff_ref.at[p, e + j], out.at[2, j])
            for j in range(2)
        ]

    waiting = []

    def run(u):
        p, e = units[u]
        for j in range(2):
            if e + j and (e + j) % 2 == 1:
                arrival(p, e + j).wait_recv()
        for c in x_loads(u):
            c.start()
        if u + 1 < len(units):
            for c in cot_loads(u + 1):
                c.start()
        if u:
            for c in hidden_stores(u - 1):
                c.wait()
        for c in x_loads(u) + cot_loads(u):
            c.wait()

        @pl.loop(0, hidden // tile)
        def _(i):
            here = pl.ds(pl.multiple_of(i * tile, tile), tile)
            raised = dot(x_s[...], up_ref[:, here]) + bias_ref[:, here]
            square = raised * raised
            th = jnp.tanh(0.7978845608028654 * raised * (1.0 + 0.044715 * square))
            act_s[:, here] = (0.5 * raised * (1.0 + th)).astype(BF)
            slope = 0.5 * (1.0 + th) + 0.5 * raised * (1.0 - th * th) * (
                0.7978845608028654 * (1.0 + 3 * 0.044715 * square)
            )
            gr = (dot_nt(c_s[u % 2], down_ref[here, :]) * slope).astype(BF)
            gr_s[:, here] = gr
            gb = jnp.sum(gr.astype(F32), axis=0, keepdims=True)
            gb_ref[:, here] = gb if u == 0 else gb_ref[:, here] + gb

        for c in hidden_stores(u):
            c.start()
        while waiting:
            q, k = waiting.pop(0)
            work[q].forward(k)
        if u:
            for c in ff_stores(u - 1):
                c.wait()
        odd, even = work[p].claim(e + 1), work[p].claim(e)

        @pl.loop(0, d // wide)
        def _(i):
            here = pl.ds(pl.multiple_of(i * wide, wide), wide)
            gn = dot_nt(gr_s[...], up_ref[here, :]).astype(BF)
            even[:, here] = gn[:span]
            odd[:, here] = gn[span:]
            ff_s[:, here] = dot(act_s[...], down_ref[:, here]).astype(BF)

        work[p].launch(e + 1)
        for c in ff_stores(u):
            c.start()

    keep = [pltpu.make_async_copy(x_ref.at[p], xg_ref.at[me, p], own.at[p]) for p in range(seqs)]
    greet(range(steps))
    for p in range(seqs):
        hop(p, 0, paths[p][0]).start()
    for p in range(seqs):
        hop(p, 0, 0).start()
        keep[p].start()
    for c in cot_loads(0):
        c.start()
    sent = [(p, 0, b) for p in range(seqs) for b in (paths[p][0], 0)]
    u = 0
    for t in range(steps):
        while u < len(units) and units[u][1] in slots_at(units[u][0], t):
            if t and units[u][0] == 0:
                for p in range(seqs):
                    k = units[u + p][1]
                    arrival(p, k).wait_recv()
                    if t < steps - 1:
                        hop(p, k, paths[p][t]).start()
                        sent.append((p, k, paths[p][t]))
                    hop(p, k, 0).start()
                    sent.append((p, k, 0))
            run(u)
            p, k = units[u]
            if work[p].stage(k) == 1:
                waiting.append((p, k))
            u += 1
        if 0 < t < steps - 1:
            for p in range(seqs):
                for before in range(t - 1, -1, -1):
                    for k in slots_at(p, before):
                        hop(p, k, paths[p][t]).start()
                        sent.append((p, k, paths[p][t]))
    for p, k in waiting:
        work[p].forward(k)
    for i in range(2, steps):
        for at in range(n // 2 - 1):
            for p in range(seqs):
                k = scatter_order(bits_of[p])[at]
                if work[p].stage(k) == i:
                    work[p].forward(k)
    for p in range(seqs):
        gn_ref[p] = work[p].total(0)
    for c in hidden_stores(len(units) - 1) + ff_stores(len(units) - 1) + keep:
        c.wait()
    for p, k, b in sent:
        hop(p, k, b).wait_send()
    for p in range(seqs):
        work[p].drain()


def mlp(normed, cot, up, bias, down, orders):
    n, seqs, span, d = cot.shape
    ff = up.shape[1]
    dma = pltpu.SemaphoreType.DMA
    hbm, vmem = pl.BlockSpec(memory_space=pl.ANY), pl.BlockSpec(memory_space=pltpu.VMEM)
    return pl.pallas_call(
        functools.partial(mlp_kernel, orders=orders),
        in_specs=[hbm, hbm, vmem, vmem, vmem],
        out_specs=[vmem, vmem, hbm, hbm, hbm, hbm],
        out_shape=[
            jax.ShapeDtypeStruct((seqs, span, d), F32),
            jax.ShapeDtypeStruct((1, ff), F32),
            jax.ShapeDtypeStruct((n, seqs, span, d), BF),
            jax.ShapeDtypeStruct((n, seqs, span, ff), BF),
            jax.ShapeDtypeStruct((n, seqs, span, ff), BF),
            jax.ShapeDtypeStruct((seqs, n, span, d), BF),
        ],
        scratch_shapes=[
            pltpu.VMEM((2 * span, d), BF),
            pltpu.VMEM((2, 2 * span, d), BF),
            pltpu.VMEM((2 * span, ff), BF),
            pltpu.VMEM((2 * span, ff), BF),
            pltpu.VMEM((2 * span, d), BF),
            pltpu.VMEM((seqs, n // 2 + 2, span, d), BF),
            pltpu.VMEM((seqs, n - 1, span, d), BF),
            dma((seqs, n)), dma((seqs, n)), dma((seqs, n)), dma((seqs, n)), dma((3, 2)), dma((seqs,)), dma((3, 2)),
        ],
        compiler_params=pltpu.CompilerParams(collective_id=2, has_side_effects=True, vmem_limit_bytes=60 * MIB),
        cost_estimate=pl.CostEstimate(
            flops=8 * n * seqs * span * d * ff, bytes_accessed=100 * MIB, transcendentals=n * seqs * span * ff
        ),
    )(normed, cot, up, bias, down)


class ScatterParts(Scatter):
    def copy(self, k):
        if self.stage(k):
            return super().copy(k)
        return pltpu.make_async_remote_copy(
            src_ref=self.source.at[k],
            dst_ref=self.recv.at[k - 1],
            send_sem=self.send_sem.at[k],
            recv_sem=self.recv_sem.at[k],
            device_id={"tensor": self.me ^ (1 << self.bits[0])},
            device_id_type=MESH,
        )

    def place(self, k):
        return k // 2 if k % 2 == 0 else -k


def mlp_grads_kernel(gr_ref, x_ref, part_ref, down_ref, up_ref, ff_ref, sum_ref,
                     a_s, b_s, acc, send, recv, far, piece, ssem, rsem, load, own, zsem, psem, *, orders, line):
    seqs, n = part_ref.shape[:2]
    bits_of = [[0] + list(o)[::-1] for o in orders]
    work = []
    for p in range(seqs):
        w = ScatterParts(bits_of[p], send.at[p], recv.at[p], ssem.at[p], rsem.at[p])
        w.source = part_ref.at[p]
        work.append(w)
    evens = [
        pltpu.make_async_copy(part_ref.at[p, k], send.at[p, k // 2], own.at[p, k // 2])
        for p in range(seqs) for k in range(0, n, 2)
    ]
    wide = acc.shape[0]
    tile = min(256, wide)
    steps = n

    def loads(u):
        return [
            pltpu.make_async_copy(x_ref.at[u], a_s.at[u % 2], load.at[u % 2, 0]),
            pltpu.make_async_copy(gr_ref.at[u], b_s.at[u % 2], load.at[u % 2, 1]),
        ]

    greet(range(len(bits_of[0])), line)
    chain = Line(down_ref, sum_ref, far, zsem)
    pieces = down_ref.shape[0]
    for k in range(n - 1, 0, -2):
        for p in range(seqs):
            work[p].launch(k)
    if line:
        for i in range(pieces):
            chain.start(i)

    def own_piece(i):
        def value():
            c = pltpu.make_async_copy(down_ref.at[i], piece, psem)
            c.start()
            c.wait()
            return piece[...]

        return value

    ahead = [0, 0]

    def chain_to(middles):
        while line and ahead[0] < min(middles, pieces):
            chain.middle(ahead[0], own_piece(ahead[0]))
            ahead[0] += 1
            if ahead[0] > 1:
                chain.back(ahead[0] - 2)

    for c in loads(0) + evens:
        c.start()

    def forwards(i):
        for at in range(n // 2 - 1):
            for p in range(seqs):
                k = scatter_order(bits_of[p])[at]
                if work[p].stage(k) == i:
                    work[p].forward(k)

    stages = len(bits_of[0])
    when = {(i - 1) * (steps // (stages - 1)) + 1: i for i in range(1, stages)} if stages > 1 else {}
    when = {min(u + 2 * (i - 1), steps - 1): i for u, i in when.items()}
    for u in range(steps):
        if u + 1 < steps:
            for c in loads(u + 1):
                c.start()
        for c in loads(u):
            c.wait()

        @pl.loop(0, wide // tile)
        def _(i, u=u):
            here = pl.ds(pl.multiple_of(i * tile, tile), tile)
            term = dot_tn(a_s[u % 2, :, here], b_s[u % 2])
            if u == 0:
                acc[here, :] = term
            elif u < n - 1:
                acc[here, :] += term
            else:
                up_ref[here, :] = (acc[here, :] + term).astype(BF)

        if u == 0:
            for c in evens:
                c.wait()
        if u in when:
            forwards(when[u])
        chain_to((u + 1) // 3)
    chain_to(5)
    for p in range(seqs):
        ff_ref[p] = work[p].total(0)
        work[p].drain()
    if line:
        chain_to(pieces)
        chain.back(pieces - 1)
        for i in range(pieces):
            chain.close(i)


def weight_grad_kernel(a_ref, b_ref, o_ref, acc):
    step, last = pl.program_id(0), pl.num_programs(0) - 1
    wide = acc.shape[0]
    tile = min(256, wide)

    @pl.loop(0, wide // tile)
    def _(i):
        here = pl.ds(pl.multiple_of(i * tile, tile), tile)
        term = dot_tn(a_ref[:, here], b_ref[...])

        @pl.when(step == 0)
        def _():
            acc[here, :] = term

        @pl.when((step > 0) & (step < last))
        def _():
            acc[here, :] += term

        @pl.when(step == last)
        def _():
            o_ref[here, :] = (acc[here, :] + term).astype(BF)


def weight_grad(a, b):
    tokens, wide = a.shape
    cols = b.shape[1]
    tile = min(512, tokens // 2)
    return pl.pallas_call(
        weight_grad_kernel,
        grid=(tokens // tile,),
        in_specs=[pl.BlockSpec((tile, wide), lambda i: (i, 0)), pl.BlockSpec((tile, cols), lambda i: (i, 0))],
        out_specs=pl.BlockSpec((wide, cols), lambda i: (0, 0)),
        out_shape=jax.ShapeDtypeStruct((wide, cols), BF),
        scratch_shapes=[pltpu.VMEM((wide, cols), F32)],
        compiler_params=pltpu.CompilerParams(vmem_limit_bytes=40 * MIB),
        cost_estimate=pl.CostEstimate(flops=1000, bytes_accessed=MIB, transcendentals=0),
    )(a, b)


def mlp_grads(gr, x, parts, down, orders):
    line = lax.axis_size("dp") == 4
    seqs, n, span, d = parts.shape
    tokens, cols = seqs * span, gr.shape[-1]
    rows = down.shape[0] // 8
    down = down.reshape(8, rows, d)
    wait = down.shape if line else (1, 16, 128)
    dma = pltpu.SemaphoreType.DMA
    hbm, vmem = pl.BlockSpec(memory_space=pl.ANY), pl.BlockSpec(memory_space=pltpu.VMEM)
    flat = lambda v: v.reshape(n, tokens, v.shape[-1])
    up, ff, total = pl.pallas_call(
        functools.partial(mlp_grads_kernel, orders=orders, line=line),
        in_specs=[hbm] * 4,
        out_specs=[vmem] * 3,
        out_shape=[
            jax.ShapeDtypeStruct((d, cols), BF),
            jax.ShapeDtypeStruct((seqs, span, d), F32),
            jax.ShapeDtypeStruct(wait, BF),
        ],
        scratch_shapes=[
            pltpu.VMEM((2, tokens, d), BF),
            pltpu.VMEM((2, tokens, cols), BF),
            pltpu.VMEM((d, cols), F32),
            pltpu.VMEM((seqs, n // 2, span, d), BF),
            pltpu.VMEM((seqs, n - 1, span, d), BF),
            pltpu.VMEM(wait, BF),
            pltpu.VMEM((rows, d), BF),
            dma((seqs, n)), dma((seqs, n)), dma((2, 2)), dma((seqs, n // 2)), dma((2, 3, 8)), dma,
        ],
        compiler_params=pltpu.CompilerParams(collective_id=3, has_side_effects=True, vmem_limit_bytes=60 * MIB),
        cost_estimate=pl.CostEstimate(
            flops=1000, bytes_accessed=256 * MIB, transcendentals=0
        ),
    )(flat(gr), flat(x), parts, down)
    down = down.reshape(8 * rows, d)
    return up, ff, total.reshape(down.shape) if line else lax.psum(down, "dp")


def norm_parts(values):
    center = values - jnp.mean(values, axis=-1, keepdims=True)
    scale = lax.rsqrt(jnp.mean(center * center, axis=-1, keepdims=True) + EPSILON)
    return center * scale, scale


def norm_back(unit, scale, gain, grad):
    e = gain * grad
    back = scale * (e - jnp.mean(e, axis=-1, keepdims=True) - unit * jnp.mean(e * unit, axis=-1, keepdims=True))
    return back, jnp.sum(grad * unit, axis=(0, 1)), jnp.sum(grad, axis=(0, 1))


def body(
    inputs, cotangent, documents, padding, attn_gain, attn_shift, query_matrix, query_bias, shared_matrix,
    value_bias, output_matrix, output_bias, mlp_gain, mlp_shift, expansion_weights, up_bias, down_matrix, down_bias,
):
    n = lax.axis_size("tensor")
    me = lax.axis_index("tensor")
    hd = value_bias.shape[0]
    seqs, span, d = inputs.shape
    length = documents.shape[1]
    qw = query_matrix.shape[1]
    heads = qw // hd
    scale = hd**-0.5
    paths = bit_orders(n)
    tokens = seqs * span

    x32 = inputs.astype(F32)
    unit1, _ = norm_parts(x32)
    hidden = (unit1 * attn_gain + attn_shift).astype(BF)
    h2 = hidden.reshape(tokens, d)
    shared = dot(h2, shared_matrix)
    kv_own = jnp.concatenate([shared[:, :hd], shared[:, hd:] + value_bias], axis=1).astype(BF)
    kv_own = kv_own.reshape(seqs, span, 2 * hd)
    kv = jnp.concatenate(gather_slots(kv_own, paths[0]), axis=1)
    keys, values = kv[..., :hd], kv[..., hd:]
    keys_t, values_t = keys.swapaxes(1, 2), values.swapaxes(1, 2)

    half = d // 2
    wq = [gather_slots(query_matrix[i * half : (i + 1) * half], paths[i]) for i in range(2)]
    wo = [gather_slots(output_matrix[:, i * half : (i + 1) * half], paths[i]) for i in range(2)]
    bq = jnp.concatenate(gather_slots(query_bias[None], paths[0]), axis=1)

    like = lambda t, cols: jax.ShapeDtypeStruct((tokens, cols), t)
    (query,) = slot_product(
        functools.partial(q_kernel, factor=scale * LOG2E), [h2], [bq], wq, [like(BF, n * qw)], (d, n * qw)
    )
    query = query.reshape(seqs, span, n * qw)
    first = lax.dynamic_slice_in_dim(documents, me * span, 1, 1)
    low = (jnp.sum((documents < first).astype(jnp.int32), axis=1) // span).astype(jnp.int32)
    low = jnp.minimum(low, me)
    at = me.reshape(1).astype(jnp.int32)
    dock = jnp.where(padding == 1, documents, -1)
    dock = xor_order(dock.reshape(seqs, n, span).swapaxes(0, 1), me).swapaxes(0, 1).reshape(seqs, length, 1)
    docq = lax.dynamic_slice_in_dim(documents, me * span, span, 1)
    docq = jnp.concatenate([docq] * heads, axis=1)[:, None, :]
    attended, lse = attention_fwd(query, keys, values_t, low, at, dock, docq, heads, hd)
    a2 = attended.reshape(tokens, n * qw)
    mixed, normed = slot_product(
        o_kernel, [a2, inputs.reshape(tokens, d)], [output_bias[None], mlp_gain[None], mlp_shift[None]], wo,
        [like(F32, d), like(BF, d)], (n * qw, d),
    )
    mixed, normed = mixed.reshape(seqs, span, d), normed.reshape(seqs, span, d)
    unit2, scale2 = norm_parts(mixed)

    cot_every = lax.all_gather(cotangent, "tensor")
    grad_normed, up_bias_part, normed_every, acts, grs, ff_parts = mlp(
        normed, cot_every, expansion_weights, up_bias[None], down_matrix, paths
    )
    every = lambda v: v.reshape(n * tokens, v.shape[-1])
    down_part = weight_grad(every(acts), every(cot_every))
    up_part, mlp_branch, down_gradient = mlp_grads(grs, normed_every, ff_parts, down_part, paths)
    up_gradient = lax.psum(up_part, "dp")
    block_out = (mixed + mlp_branch + down_bias).astype(BF)

    cot_wide = cotangent.astype(F32)
    back2, mlp_gain_part, mlp_shift_part = norm_back(unit2, scale2, mlp_gain, grad_normed)
    grad_mixed = cot_wide + back2
    gm2 = grad_mixed.astype(BF).reshape(tokens, d)
    (grad_attended,) = slot_product(do_kernel, [gm2], [], wo, [like(BF, n * qw)], (n * qw, d))
    grad_attended = grad_attended.reshape(seqs, span, n * qw)
    dq, dk, dv = attention_bwd(
        query, grad_attended, attended, lse, keys, keys_t, values, low, at, dock, docq, heads, hd, scale
    )
    dq2 = dq.reshape(tokens, n * qw)

    dkv = jnp.concatenate([dk * LN2, dv], axis=-1).astype(BF).reshape(seqs, n, span, 2 * hd).swapaxes(0, 1)
    wo_own, wq_own, dkv_own = attention_grads(a2, gm2, dq2, h2, dkv.reshape(n, tokens, 2 * hd), paths)
    query_bias_part = xor_order(jnp.sum(dq2.astype(F32), axis=0).reshape(n, qw), me).reshape(-1)
    ff = up_bias.shape[0]
    up_bias_every = lax.dynamic_update_slice_in_dim(jnp.zeros((n * ff,), F32), up_bias_part[0], me * ff, 0)
    vector = jnp.concatenate(
        [query_bias_part, mlp_gain_part, mlp_shift_part, jnp.sum(grad_mixed, axis=(0, 1)),
         jnp.sum(cot_wide, axis=(0, 1)), up_bias_every]
    )[None]
    output_gradient, query_gradient, input_grad, late, shared_grad = last(
        wo_own, wq_own, dq2, dkv_own, shared_matrix, h2, inputs.reshape(tokens, d), attn_gain[None],
        grad_mixed.reshape(tokens, d), vector, wq, paths[0],
    )
    input_grad = input_grad.reshape(seqs, span, d)
    if lax.axis_size("dp") != 4:
        output_gradient, query_gradient = (
            g.astype(F32) for g in lax.psum((output_gradient.astype(BF), query_gradient.astype(BF)), "dp")
        )
    late = after(late, up_gradient)[0]
    ends = [d, 2 * d, 2 * d + hd, 2 * d + hd + n * qw]
    ends += [ends[-1] + d * (i + 1) for i in range(4)]
    (attn_gain_grad, attn_shift_grad, value_bias_grad, query_bias_all, mlp_gain_grad, mlp_shift_grad,
     output_bias_grad, down_bias_grad, up_bias_all) = jnp.split(late, ends)
    query_bias_grad = lax.dynamic_slice_in_dim(query_bias_all, me * qw, qw, 0)
    up_bias_grad = lax.dynamic_slice_in_dim(up_bias_all, me * ff, ff, 0)
    query_gradient, up_gradient, down_gradient = query_gradient.T, up_gradient.astype(F32), down_gradient.astype(F32)
    return (
        block_out, input_grad, attn_gain_grad, attn_shift_grad, query_gradient, query_bias_grad, shared_grad,
        value_bias_grad, output_gradient, output_bias_grad, mlp_gain_grad, mlp_shift_grad, up_gradient, up_bias_grad,
        down_gradient, down_bias_grad,
    )


def solution(mesh):
    act = P("dp", "tensor", None)
    cols, rows, vec, rep = P(None, "tensor"), P("tensor", None), P("tensor"), P()
    ids = P("dp", None)
    return jax.shard_map(
        body,
        mesh=mesh,
        in_specs=(act, act, ids, ids, rep, rep, cols, vec, rep, rep, rows, rep, rep, rep, cols, vec, rows, rep),
        out_specs=(act, act, rep, rep, cols, vec, rep, rep, rows, rep, rep, rep, cols, vec, rows, rep),
        check_vma=False,
    )
```

```python
import functools

import jax
import jax.numpy as jnp
from jax import lax
from jax.experimental import pallas as pl
from jax.experimental.pallas import tpu as pltpu
from jax.sharding import PartitionSpec as P

EPSILON = 1e-05
LOG2E = 1.4426950408889634
LN2 = 0.6931471805599453
BF = jnp.bfloat16
F32 = jnp.float32
NEG = -1e30
MIB = 1024 * 1024


def dot(a, b):
    return lax.dot_general(a, b, (((1,), (0,)), ((), ())), preferred_element_type=F32)


def dot_nt(a, b):
    return lax.dot_general(a, b, (((1,), (1,)), ((), ())), preferred_element_type=F32)


def dot_tn(a, b):
    return lax.dot_general(a, b, (((0,), (0,)), ((), ())), preferred_element_type=F32)


def bit_orders(n):
    bits = list(range(1, n.bit_length() - 1))
    return bits, bits[::-1]


def xor_order(x, me):
    n = x.shape[0]
    rest = x.shape[1:]
    for bit in range(n.bit_length() - 1):
        pairs = x.reshape((n >> (bit + 1), 2, 1 << bit) + rest)
        x = jnp.where((me >> bit) & 1 == 1, jnp.flip(pairs, 1), pairs).reshape((n,) + rest)
    return x


def stack_heads(block, heads, hd):
    return jnp.concatenate([block[:, i * hd : (i + 1) * hd] for i in range(heads)], axis=0)


def diagonal_mask(rows, cols, same):
    key_at = lax.broadcasted_iota(jnp.int32, (rows, cols), 0)
    query_at = lax.broadcasted_iota(jnp.int32, (rows, cols), 1) % rows
    return (same & (key_at < query_at)) | (key_at == query_at)


def below_blocks(low, at, step, carry):
    even = at - at % 2
    carry = lax.fori_loop(jnp.maximum(low, even), at, lambda b, c: step(b ^ at, 1, c), carry)
    return lax.fori_loop(low // 2, at // 2, lambda p, c: step((p ^ (at // 2)) * 2, 2, c), carry)


def attention_fwd_kernel(low_ref, at_ref, q_ref, k_ref, vt_ref, dock_ref, docq_ref, o_ref, lse_ref, *, heads, hd):
    row = pl.program_id(0)
    span = q_ref.shape[1]
    at = at_ref[0]
    q2 = stack_heads(q_ref[0], heads, hd)
    docq = docq_ref[0]

    def scores(slot, count):
        here = pl.ds(pl.multiple_of(slot * span, count * span), count * span)
        s = dot_nt(k_ref[0, here, :], q2)
        same = dock_ref[0, here, :] == docq
        return s, same, here

    s, same, here = scores(0, 1)
    s = jnp.where(diagonal_mask(span, heads * span, same), s, NEG)
    top = jnp.max(s, axis=0, keepdims=True)
    p = jnp.exp2(s - top)
    total = jnp.sum(p, axis=0, keepdims=True)
    acc = dot(vt_ref[0, :, here], p.astype(BF))

    def step(slot, count, carry):
        top, total, acc = carry
        s, same, here = scores(slot, count)
        s = jnp.where(same, s, NEG)
        new = jnp.maximum(top, jnp.max(s, axis=0, keepdims=True))
        shrink = jnp.exp2(top - new)
        p = jnp.exp2(s - new)
        total = total * shrink + jnp.sum(p, axis=0, keepdims=True)
        acc = acc * shrink + dot(vt_ref[0, :, here], p.astype(BF))
        return new, total, acc

    carry = below_blocks(low_ref[row], at, step, (top, total, acc))
    top, total, acc = carry
    out = (acc / total).T.astype(BF)
    for i in range(heads):
        o_ref[0, :, i * hd : (i + 1) * hd] = out[i * span : (i + 1) * span]
    lse_ref[0, 0] = top + jnp.log2(total)


def attention_bwd_kernel(
    low_ref, at_ref, q_ref, do_ref, o_ref, lse_ref, k_ref, kt_ref, v_ref, dock_ref, docq_ref,
    dq_ref, dk_ref, dv_ref, *, heads, hd, scale,
):
    row = pl.program_id(0)
    span = q_ref.shape[1]
    at = at_ref[0]

    @pl.when(pl.program_id(1) == 0)
    def _():
        dk_ref[...] = jnp.zeros_like(dk_ref)
        dv_ref[...] = jnp.zeros_like(dv_ref)

    q2 = stack_heads(q_ref[0], heads, hd)
    do2 = stack_heads(do_ref[0], heads, hd)
    o2 = stack_heads(o_ref[0], heads, hd)
    delta = jnp.sum((do2.astype(F32) * o2.astype(F32)).T, axis=0, keepdims=True)
    lse = lse_ref[0, 0]
    docq = docq_ref[0]

    def one(slot, count, dqt, diagonal=False):
        here = pl.ds(pl.multiple_of(slot * span, count * span), count * span)
        s = dot_nt(k_ref[0, here, :], q2)
        same = dock_ref[0, here, :] == docq
        if diagonal:
            same = diagonal_mask(span, heads * span, same)
        p = jnp.where(same, jnp.exp2(s - lse), 0.0)
        dp = dot_nt(v_ref[0, here, :], do2)
        ds = (p * (dp - delta)).astype(BF)
        dk_ref[0, here, :] += dot(ds, q2)
        dv_ref[0, here, :] += dot(p.astype(BF), do2)
        return dqt + dot(kt_ref[0, :, here], ds)

    dqt = one(0, 1, jnp.zeros((hd, heads * span), F32), True)
    dqt = below_blocks(low_ref[row], at, one, dqt)
    dq = (dqt * scale).T.astype(BF)
    for i in range(heads):
        dq_ref[0, :, i * hd : (i + 1) * hd] = dq[i * span : (i + 1) * span]


def attention_fwd(q, k, vt, low, at, dock, docq, heads, hd):
    rows, span, width = q.shape
    length = k.shape[1]
    groups = width // (heads * hd)
    gw = heads * hd
    return pl.pallas_call(
        functools.partial(attention_fwd_kernel, heads=heads, hd=hd),
        grid_spec=pltpu.PrefetchScalarGridSpec(
            num_scalar_prefetch=2,
            grid=(rows, groups),
            in_specs=[
                pl.BlockSpec((1, span, gw), lambda r, g, *_: (r, 0, g)),
                pl.BlockSpec((1, length, hd), lambda r, g, *_: (r, 0, 0)),
                pl.BlockSpec((1, hd, length), lambda r, g, *_: (r, 0, 0)),
                pl.BlockSpec((1, length, 1), lambda r, g, *_: (r, 0, 0)),
                pl.BlockSpec((1, 1, heads * span), lambda r, g, *_: (r, 0, 0)),
            ],
            out_specs=[
                pl.BlockSpec((1, span, gw), lambda r, g, *_: (r, 0, g)),
                pl.BlockSpec((1, 1, 1, heads * span), lambda r, g, *_: (r, g, 0, 0)),
            ],
        ),
        out_shape=[
            jax.ShapeDtypeStruct((rows, span, width), BF),
            jax.ShapeDtypeStruct((rows, groups, 1, heads * span), F32),
        ],
        compiler_params=pltpu.CompilerParams(vmem_limit_bytes=24 * MIB),
        cost_estimate=pl.CostEstimate(
            flops=2 * rows * span * width * length, bytes_accessed=8 * MIB, transcendentals=rows * span * length
        ),
    )(low, at, q, k, vt, dock, docq)


def attention_bwd(q, do, o, lse, k, kt, v, low, at, dock, docq, heads, hd, scale):
    rows, span, width = q.shape
    length = k.shape[1]
    groups = width // (heads * hd)
    gw = heads * hd
    blk = pl.BlockSpec((1, span, gw), lambda r, g, *_: (r, 0, g))
    full = pl.BlockSpec((1, length, hd), lambda r, g, *_: (r, 0, 0))
    return pl.pallas_call(
        functools.partial(attention_bwd_kernel, heads=heads, hd=hd, scale=scale),
        grid_spec=pltpu.PrefetchScalarGridSpec(
            num_scalar_prefetch=2,
            grid=(rows, groups),
            in_specs=[
                blk,
                blk,
                blk,
                pl.BlockSpec((1, 1, 1, heads * span), lambda r, g, *_: (r, g, 0, 0)),
                full,
                pl.BlockSpec((1, hd, length), lambda r, g, *_: (r, 0, 0)),
                full,
                pl.BlockSpec((1, length, 1), lambda r, g, *_: (r, 0, 0)),
                pl.BlockSpec((1, 1, heads * span), lambda r, g, *_: (r, 0, 0)),
            ],
            out_specs=[blk, full, full],
        ),
        out_shape=[
            jax.ShapeDtypeStruct((rows, span, width), BF),
            jax.ShapeDtypeStruct((rows, length, hd), F32),
            jax.ShapeDtypeStruct((rows, length, hd), F32),
        ],
        compiler_params=pltpu.CompilerParams(vmem_limit_bytes=32 * MIB),
        cost_estimate=pl.CostEstimate(
            flops=1000, bytes_accessed=MIB, transcendentals=0
        ),
    )(low, at, q, do, o, lse, k, kt, v, dock, docq)


def fill_rows(whole_ref, every_ref):
    n, rows, _ = every_ref.shape
    me = lax.axis_index("tensor")
    for k in range(n):
        whole_ref[k * rows : (k + 1) * rows, :] = every_ref[me ^ k]


def o_kernel(a_ref, x_ref, w_ref, b_ref, gain_ref, shift_ref, mixed_ref, normed_ref, w_s):
    @pl.when(pl.program_id(0) == 0)
    def _():
        fill_rows(w_s, w_ref)

    mixed = x_ref[...].astype(F32) + dot(a_ref[...], w_s[...]) + b_ref[...]
    mixed_ref[...] = mixed
    unit, _ = norm_parts(mixed)
    normed_ref[...] = (unit * gain_ref[...] + shift_ref[...]).astype(BF)


def do_kernel(g_ref, w_ref, o_ref, w_s):
    @pl.when(pl.program_id(0) == 0)
    def _():
        fill_rows(w_s, w_ref)

    o_ref[...] = dot_nt(g_ref[...], w_s[...]).astype(BF)


def slot_product(kernel, tiled, weights, fixed, outs):
    n, rows, cols = weights.shape
    tokens = tiled[0].shape[0]
    tile = tokens // 2
    still = lambda a: pl.BlockSpec(a.shape, lambda i: (0,) * a.ndim, pipeline_mode=pl.Buffered(1))
    flow = lambda a: pl.BlockSpec((tile, a.shape[1]), lambda i: (i, 0))
    return pl.pallas_call(
        kernel,
        grid=(2,),
        in_specs=[flow(a) for a in tiled] + [still(weights)] + [still(a) for a in fixed],
        out_specs=[flow(o) for o in outs],
        out_shape=outs,
        scratch_shapes=[pltpu.VMEM((n * rows, cols), BF)],
        compiler_params=pltpu.CompilerParams(vmem_limit_bytes=48 * MIB),
        cost_estimate=pl.CostEstimate(
            flops=2 * tokens * n * rows * cols, bytes_accessed=2 * n * rows * cols + 8 * MIB, transcendentals=0
        ),
    )(*tiled, weights, *fixed)


MESH = pl.DeviceIdType.MESH


def greet(bits, line=False, dp_bits=()):
    me, z = lax.axis_index("tensor"), lax.axis_index("dp")
    barrier = pltpu.get_barrier_semaphore()
    for bit in bits:
        pl.semaphore_signal(barrier, inc=1, device_id={"tensor": me ^ (1 << bit)}, device_id_type=MESH)
    count = len(bits)
    flips = {1 << bit for bit in dp_bits} | ({1} if line else set())
    for flip in sorted(flips):
        pl.semaphore_signal(barrier, inc=1, device_id={"dp": z ^ flip}, device_id_type=MESH)
    count += len(flips)
    if line:
        inner = (z == 1) | (z == 2)

        @pl.when(inner)
        def _():
            pl.semaphore_signal(barrier, inc=1, device_id={"dp": 3 - z}, device_id_type=MESH)

        count = count + inner.astype(jnp.int32)
    pl.semaphore_wait(barrier, count)


class Line:
    def __init__(self, own, near, far, sem):
        self.own, self.near, self.far, self.sem = own, near, far, sem
        self.z = lax.axis_index("dp")
        self.inner = (self.z == 1) | (self.z == 2)
        self.outer = jnp.logical_not(self.inner)

    def copy(self, i, hop):
        src = (self.own, self.near, self.near)[hop].at[i]
        dst = (self.near, self.far, self.near)[hop].at[i]
        return pltpu.make_async_remote_copy(
            src_ref=src, dst_ref=dst, send_sem=self.sem.at[0, hop, i], recv_sem=self.sem.at[1, hop, i],
            device_id={"dp": 3 - self.z if hop == 1 else self.z ^ 1}, device_id_type=MESH,
        )

    def start(self, i):
        @pl.when(self.outer)
        def _():
            self.copy(i, 0).start()

    def middle(self, i, own):
        @pl.when(self.inner)
        def _():
            self.copy(i, 0).wait_recv()
            self.near[i] = (own().astype(F32) + self.near[i].astype(F32)).astype(BF)
            self.copy(i, 1).start()

    def back(self, i):
        @pl.when(self.inner)
        def _():
            self.copy(i, 1).wait()
            self.near[i] = (self.near[i].astype(F32) + self.far[i].astype(F32)).astype(BF)
            self.copy(i, 2).start()

    def close(self, i):
        @pl.when(self.outer)
        def _():
            self.copy(i, 0).wait_send()
            self.copy(i, 2).wait_recv()

        @pl.when(self.inner)
        def _():
            self.copy(i, 2).wait_send()


class Scatter:
    def __init__(self, bits, send, recv, send_sem, recv_sem, shared=0):
        self.bits, self.send, self.recv, self.send_sem, self.recv_sem = bits, send, recv, send_sem, recv_sem
        self.me = lax.axis_index("tensor")
        self.shared = shared
        self.busy = {}

    def place(self, k):
        if not self.shared:
            return k
        return k // 2 if k % 2 == 0 else (1 << len(self.bits)) // 2 + k // 2 % self.shared

    def claim(self, k):
        place = self.place(k)
        if place in self.busy:
            self.copy(self.busy.pop(place)).wait_send()
        return self.send.at[place]

    def launch(self, k):
        self.copy(k).start()
        self.busy[self.place(k)] = k

    def stage(self, k):
        return next((i for i, b in enumerate(self.bits) if k >> b & 1), len(self.bits))

    def copy(self, k):
        bit = self.bits[self.stage(k)]
        return pltpu.make_async_remote_copy(
            src_ref=self.send.at[self.place(k)],
            dst_ref=self.recv.at[k - 1],
            send_sem=self.send_sem.at[k],
            recv_sem=self.recv_sem.at[k],
            device_id={"tensor": self.me ^ (1 << bit)},
            device_id_type=MESH,
        )

    def put(self, k, value):
        self.claim(k)[...] = value.astype(BF)
        if self.stage(k) == 0:
            self.launch(k)

    def total(self, k):
        value = self.send[self.place(k)].astype(F32)
        for bit in self.bits[: self.stage(k)]:
            self.copy(k | (1 << bit)).wait_recv()
            value = value + self.recv[(k | (1 << bit)) - 1].astype(F32)
        return value

    def forward(self, k):
        self.send[self.place(k)] = self.total(k).astype(BF)
        self.launch(k)

    def drain(self):
        for k in self.busy.values():
            self.copy(k).wait_send()
        self.busy = {}


def scatter_order(bits):
    n = 1 << len(bits)
    rank = lambda k: next(i for i, b in enumerate(bits) if k >> b & 1)
    return sorted(range(2, n, 2), key=lambda k: (rank(k), -k))


def attention_grads_kernel(a_ref, gm_ref, dq_ref, h_ref, dkv_ref, up_ref, after_ref, wo_ref, wq_ref, kv_ref, sum_ref,
                           send, recv, ksend, krecv, far, own, ssem, rsem, ksem, krsem, zsem, psem,
                           *, orders, line, qw):
    bits_of = [[0] + list(o)[::-1] for o in orders]
    count = len(bits_of[0])
    n = 1 << count
    half = gm_ref.shape[1] // 2
    greet(range(count), line)
    chain = Line(up_ref, sum_ref, far, zsem)
    pieces = up_ref.shape[0]
    if line:
        for i in range(pieces):
            chain.start(i)

    def own_piece(i):
        def value():
            c = pltpu.make_async_copy(up_ref.at[i], own, psem)
            c.start()
            c.wait()
            return own[...]

        return value

    ahead = [0]

    def chain_to(middles):
        while line and ahead[0] < min(middles, pieces):
            chain.middle(ahead[0], own_piece(ahead[0]))
            ahead[0] += 1
            if ahead[0] > 1:
                chain.back(ahead[0] - 2)

    kv = Scatter(bits_of[0], ksend, krecv, ksem, krsem)
    for k in list(range(1, n, 2)) + list(range(0, n, 2)):
        kv.put(k, dkv_ref[k])

    pairs = ((a_ref, gm_ref, wo_ref), (dq_ref, h_ref, wq_ref))
    work = [
        [Scatter(bits_of[p], send.at[m, p], recv.at[m, p], ssem.at[m, p], rsem.at[m, p], shared=2) for p in range(2)]
        for m in range(2)
    ]
    sequence = [scatter_order(b) for b in bits_of]

    def products(m):
        x, y, _ = pairs[m]
        for i in range(n // 2):
            for p in range(2):
                k = (sequence[p] + [0])[i]
                for j in (k + 1, k):
                    work[m][p].put(j, dot_tn(x[:, j * qw : (j + 1) * qw], y[:, p * half : (p + 1) * half]))

    def stage(m, i):
        for at in range(n // 2 - 1):
            for p in range(2):
                k = sequence[p][at]
                if work[m][p].stage(k) == i:
                    work[m][p].forward(k)

    def kv_stage(i):
        for k in scatter_order(bits_of[0]):
            if kv.stage(k) == i:
                kv.forward(k)

    def finish(m):
        for p in range(2):
            pairs[m][2][p] = work[m][p].total(0).astype(BF)

    products(0)
    stage(0, 1)
    products(1)
    chain_to(1)
    for i in range(1, count):
        kv_stage(i)
        if i + 1 < count:
            stage(0, i + 1)
            chain_to(i + 1)
        else:
            chain_to(3)
            finish(0)
        stage(1, i)
    chain_to(4)
    kv_ref[...] = kv.total(0).astype(BF)
    chain_to(5)
    finish(1)
    if line:
        chain_to(pieces)
        chain.back(pieces - 1)
        for i in range(pieces):
            chain.close(i)
    kv.drain()
    for m in range(2):
        for p in range(2):
            work[m][p].drain()


def attention_grads(a, gm, dq, h, dkv, up, early, orders):
    n, line = lax.axis_size("tensor"), lax.axis_size("dp") == 4
    tokens, d = gm.shape
    qw = a.shape[1] // n
    slot = dkv.shape[1:]
    rows, cols = up.shape
    pieces = 8
    up = up.reshape(pieces, rows // pieces, cols)
    wait = up.shape if line else (1, 16, 128)
    dma = pltpu.SemaphoreType.DMA
    vmem, hbm = pl.BlockSpec(memory_space=pltpu.VMEM), pl.BlockSpec(memory_space=pl.ANY)
    wo, wq, kv, total = pl.pallas_call(
        functools.partial(attention_grads_kernel, orders=orders, line=line, qw=qw),
        in_specs=[vmem] * 5 + [hbm] * 2,
        out_specs=[vmem] * 4,
        out_shape=[
            jax.ShapeDtypeStruct((2, qw, d // 2), BF),
            jax.ShapeDtypeStruct((2, qw, d // 2), BF),
            jax.ShapeDtypeStruct(slot, BF),
            jax.ShapeDtypeStruct(wait, BF),
        ],
        scratch_shapes=[
            pltpu.VMEM((2, 2, n // 2 + 2, qw, d // 2), BF),
            pltpu.VMEM((2, 2, n - 1, qw, d // 2), BF),
            pltpu.VMEM((n,) + slot, BF),
            pltpu.VMEM((n - 1,) + slot, BF),
            pltpu.VMEM(wait, BF),
            pltpu.VMEM(up.shape[1:], BF),
            dma((2, 2, n)), dma((2, 2, n)), dma((n,)), dma((n,)), dma((2, 3, pieces)), dma,
        ],
        compiler_params=pltpu.CompilerParams(
            collective_id=1, has_side_effects=True, vmem_limit_bytes=60 * MIB
        ),
        cost_estimate=pl.CostEstimate(flops=1000, bytes_accessed=MIB, transcendentals=0),
    )(a, gm, dq, h, dkv, up, early)
    up = up.reshape(rows, cols)
    return wo, wq, kv, total.reshape(rows, cols) if line else lax.psum(up, "dp")


def last_kernel(wo_ref, wq_ref, dq_ref, kv_ref, shared_ref, h_ref, x_ref, gain_ref, mixed_ref, qb_ref, w_ref, *refs,
                order, line, eps_rows):
    count = len(order) + 1
    n = 1 << count
    (wog_ref, wqg_ref, grad_ref, late_ref, sg_ref,
     w_s, near, far, part, send, recv, dsend, drecv, piece_s, gathered, vsend, vrecv,
     zsem, ssem, rsem, dsem, gsem, vsem) = refs
    me, z = lax.axis_index("tensor"), lax.axis_index("dp")
    dp_bits = range(lax.axis_size("dp").bit_length() - 1)
    tokens, d = x_ref.shape
    hd = kv_ref.shape[1] // 2
    piece = d // n
    greet(range(count), line, dp_bits)

    owns = [wo_ref.at[0], wo_ref.at[1], wq_ref.at[0], wq_ref.at[1]]
    chains = []
    if line:
        for i, ref in enumerate((wo_ref, wq_ref)):
            c = Line(ref, near.at[i], far.at[i], zsem.at[i])
            c.values = [lambda ref=ref, p=p: ref[p] for p in range(2)]
            chains.append(c)
            for p in range(2):
                c.start(p)

    ahead = [0, 0]

    def chain_to(middles, backs):
        while line and ahead[0] < min(middles, 4):
            i, p = divmod(ahead[0], 2)
            chains[i].middle(p, chains[i].values[p])
            ahead[0] += 1
        while line and ahead[1] < min(backs, 4):
            i, p = divmod(ahead[1], 2)
            chains[i].back(p)
            ahead[1] += 1

    part[...] = dot_tn(h_ref[...], kv_ref[...])
    scatter = Scatter([0] + list(order)[::-1], send, recv, ssem, rsem)
    for k in list(range(1, n, 2)) + list(range(0, n, 2)):
        scatter.put(k, part[pl.ds(pl.multiple_of((me ^ k) * piece, piece), piece), :])
    for k in range(n):
        w_s[:, k * w_ref.shape[2] : (k + 1) * w_ref.shape[2]] = w_ref[k]
    for i in range(1, count):
        for k in scatter_order(scatter.bits):
            if scatter.stage(k) == i:
                scatter.forward(k)
    chain_to(1, 0)

    gain_part, shift_part = jnp.zeros((1, d), F32), jnp.zeros((1, d), F32)
    for t in range(tokens // eps_rows):
        rows = slice(t * eps_rows, (t + 1) * eps_rows)
        grad = dot_nt(dq_ref[rows], w_s[...]) + dot_nt(kv_ref[rows], shared_ref[...])
        unit, scale = norm_parts(x_ref[rows].astype(F32))
        e = gain_ref[...] * grad
        back = e - jnp.mean(e, axis=-1, keepdims=True) - unit * jnp.mean(e * unit, axis=-1, keepdims=True)
        grad_ref[rows] = mixed_ref[rows] + scale * back
        gain_part += jnp.sum(grad * unit, axis=0, keepdims=True)
        shift_part += jnp.sum(grad, axis=0, keepdims=True)
        chain_to(2 + t, 1 + t)
    at = 0
    for value in (gain_part, shift_part, jnp.sum(kv_ref[:, hd:].astype(F32), axis=0, keepdims=True), qb_ref[...]):
        late_ref[:, at : at + value.shape[1]] = value
        at += value.shape[1]

    hops = [("tensor", me, b) for b in range(count)] + [("dp", z, b) for b in dp_bits]

    def small(buffers, sems, i, axis, at, bit):
        return pltpu.make_async_remote_copy(
            src_ref=buffers[0].at[i], dst_ref=buffers[1].at[i], send_sem=sems.at[0, i], recv_sem=sems.at[1, i],
            device_id={axis: at ^ (1 << bit)}, device_id_type=MESH,
        )

    piece_s[...] = scatter.total(0)
    pending = []
    for i, (axis, at, bit) in enumerate(hops):
        vsend[i] = late_ref[...]
        c = small((vsend, vrecv), vsem, i, axis, at, bit)
        c.start()
        j = i if i < len(dp_bits) else None
        if j is not None:
            dsend[j] = piece_s[...]
            e = small((dsend, drecv), dsem, j, "dp", z, dp_bits[j])
            e.start()
        if i:
            chain_to(3 + i, 2 + i)
        c.wait_recv()
        late_ref[...] = late_ref[...] + vrecv[i]
        pending.append(c)
        if j is not None:
            e.wait_recv()
            piece_s[...] = piece_s[...] + drecv[j]
            pending.append(e)
        if j == len(dp_bits) - 1:
            gathered[me] = piece_s[...].astype(BF)
            held = [0]
    sent = []
    for bit in list(order) + [0]:
        new = []
        for k in held:
            c = pltpu.make_async_remote_copy(
                src_ref=gathered.at[me ^ k], dst_ref=gathered.at[me ^ k], send_sem=gsem.at[0, k | (1 << bit)],
                recv_sem=gsem.at[1, k | (1 << bit)], device_id={"tensor": me ^ (1 << bit)}, device_id_type=MESH,
            )
            c.start()
            sent.append(c)
            new.append(c)
        for c in new:
            c.wait_recv()
        held = held + [k | (1 << bit) for k in held]
    chain_to(4, 4)
    for k in range(n):
        sg_ref[k * piece : (k + 1) * piece] = gathered[k].astype(F32)
    if line:
        for c in chains:
            for p in range(2):
                c.close(p)
    half = d // 2
    for i, ref in enumerate((wog_ref, wqg_ref)):
        for p in range(2):
            value = near[i, p] if line else (wo_ref, wq_ref)[i][p]
            ref[:, p * half : (p + 1) * half] = value.astype(F32)
    for c in pending + sent:
        c.wait_send()
    scatter.drain()


def last(wo, wq, dq, kv, shared, h, x, gain, mixed, qb, w, order):
    n, dp = lax.axis_size("tensor"), lax.axis_size("dp")
    line = dp == 4
    tokens, d = x.shape
    qw = wo.shape[1]
    piece, width = d // n, kv.shape[1]
    size = 2 * d + qb.shape[1] + width // 2
    bits = n.bit_length() - 1
    dbits = dp.bit_length() - 1
    dma = pltpu.SemaphoreType.DMA
    vmem = pl.BlockSpec(memory_space=pltpu.VMEM)
    item = (2, 2, qw, d // 2)
    return pl.pallas_call(
        functools.partial(last_kernel, order=order, line=line, eps_rows=tokens // 2),
        in_specs=[vmem] * 11,
        out_specs=[vmem] * 5,
        out_shape=[
            jax.ShapeDtypeStruct((qw, d), F32),
            jax.ShapeDtypeStruct((qw, d), F32),
            jax.ShapeDtypeStruct((tokens, d), F32),
            jax.ShapeDtypeStruct((1, size), F32),
            jax.ShapeDtypeStruct((d, width), F32),
        ],
        scratch_shapes=[
            pltpu.VMEM((d, n * qw), BF),
            pltpu.VMEM(item, BF),
            pltpu.VMEM(item, BF),
            pltpu.VMEM((d, width), F32),
            pltpu.VMEM((n, piece, width), BF),
            pltpu.VMEM((n - 1, piece, width), BF),
            pltpu.VMEM((dbits, piece, width), F32),
            pltpu.VMEM((dbits, piece, width), F32),
            pltpu.VMEM((piece, width), F32),
            pltpu.VMEM((n, piece, width), BF),
            pltpu.VMEM((bits + dbits, 1, size), F32),
            pltpu.VMEM((bits + dbits, 1, size), F32),
            dma((2, 2, 3, 2)), dma((n,)), dma((n,)), dma((2, dbits)), dma((2, n)), dma((2, bits + dbits)),
        ],
        compiler_params=pltpu.CompilerParams(
            collective_id=4, has_side_effects=True, vmem_limit_bytes=60 * MIB
        ),
        cost_estimate=pl.CostEstimate(flops=1000, bytes_accessed=MIB, transcendentals=0),
    )(wo, wq, dq, kv, shared, h, x, gain, mixed, qb, w)


class Gather:
    def __init__(self, orders, refs, send_sem, recv_sem):
        self.paths = [list(o) + [0] for o in orders]
        self.refs, self.send_sem, self.recv_sem = refs, send_sem, recv_sem
        self.me = lax.axis_index("tensor")
        self.n = 1 << len(self.paths[0])
        self.sent = []

    def last_bit(self, p, k):
        return max((b for b in self.paths[p] if k >> b & 1), key=self.paths[p].index)

    def copies(self, p, k, bit):
        to = k | (1 << bit)
        return [
            pltpu.make_async_remote_copy(
                src_ref=ref(p, k), dst_ref=ref(p, to), send_sem=self.send_sem.at[i, p, to],
                recv_sem=self.recv_sem.at[i, p, to], device_id={"tensor": self.me ^ (1 << bit)}, device_id_type=MESH,
            )
            for i, ref in enumerate(self.refs)
        ]

    def hop(self, p, k, bit):
        for c in self.copies(p, k, bit):
            c.start()
            self.sent.append(c)

    def arrived(self, p, k):
        bit = self.last_bit(p, k)
        for c in self.copies(p, k ^ (1 << bit), bit):
            c.wait_recv()

    def at_step(self, p, t):
        if t == 0:
            return [0]
        return sorted((k for k in range(2, self.n, 2) if self.last_bit(p, k) == self.paths[p][t - 1]), reverse=True)

    def drain(self):
        for c in self.sent:
            c.wait_send()


def first_kernel(x_ref, gain_ref, shift_ref, shared_ref, vb_ref, wq_ref, bq_ref, h_ref, kv_ref, w_ref, q_ref,
                 bias, send_sem, recv_sem, *, orders, factor, rows):
    n, d, qw = w_ref.shape
    seqs, span = kv_ref.shape[1:3]
    hd = vb_ref.shape[1]
    half = d // 2
    tokens = x_ref.shape[0]
    greet(range(len(orders[0]) + 1))
    weights = Gather(
        orders, [lambda p, k: w_ref.at[k, p * half : (p + 1) * half], lambda p, k: bias.at[p, k]],
        send_sem.at[0], recv_sem.at[0],
    )
    shared = Gather(orders, [lambda p, k: kv_ref.at[k, p]], send_sem.at[1], recv_sem.at[1])
    steps = len(weights.paths[0])
    w_ref[0] = wq_ref[...]
    for p in range(2):
        bias[p, 0] = bq_ref[...]
    for p in range(2):
        weights.hop(p, 0, weights.paths[p][0])
    for p in range(2):
        weights.hop(p, 0, 0)
    for t in range(tokens // rows):
        here = slice(t * rows, (t + 1) * rows)
        unit, _ = norm_parts(x_ref[here].astype(F32))
        h_ref[here] = (unit * gain_ref[...] + shift_ref[...]).astype(BF)
    kv = dot(h_ref[...], shared_ref[...])
    for r in range(seqs):
        here = slice(r * span, (r + 1) * span)
        kv_ref[0, r, :, :hd] = kv[here, :hd].astype(BF)
        kv_ref[0, r, :, hd:] = (kv[here, hd:] + vb_ref[...]).astype(BF)
    for p in range(2):
        shared.hop(p, 0, shared.paths[p][0])
    for p in range(2):
        shared.hop(p, 0, 0)

    def product(k):
        q_ref[:, k * qw : (k + 1) * qw] = ((dot(h_ref[...], w_ref[k]) + bias[0, k]) * factor).astype(BF)

    product(0)
    ready = [1]
    for t in range(1, steps):
        for g in (weights, shared):
            for p in range(2):
                for k in g.at_step(p, t):
                    g.arrived(p, k)
                    if t < steps - 1:
                        g.hop(p, k, g.paths[p][t])
                    g.hop(p, k, 0)
            if t < steps - 1:
                for p in range(2):
                    for before in range(t - 1, -1, -1):
                        for k in g.at_step(p, before):
                            g.hop(p, k, g.paths[p][t])
    for k in range(1, n, 2):
        for p in range(2):
            weights.arrived(p, k)
        product(k)
        if k > 1:
            product(k - 1)
    for k in range(1, n, 2):
        for p in range(2):
            shared.arrived(p, k)
    weights.drain()
    shared.drain()


def first(x, gain, shift, shared, vb, wq, bq, seqs, factor, orders):
    n = lax.axis_size("tensor")
    tokens, d = x.shape
    qw = wq.shape[1]
    dma = pltpu.SemaphoreType.DMA
    vmem = pl.BlockSpec(memory_space=pltpu.VMEM)
    return pl.pallas_call(
        functools.partial(first_kernel, orders=orders, factor=factor, rows=tokens // 4),
        in_specs=[vmem] * 7,
        out_specs=[vmem] * 4,
        out_shape=[
            jax.ShapeDtypeStruct((tokens, d), BF),
            jax.ShapeDtypeStruct((n, seqs, tokens // seqs, shared.shape[1]), BF),
            jax.ShapeDtypeStruct((n, d, qw), BF),
            jax.ShapeDtypeStruct((tokens, n * qw), BF),
        ],
        scratch_shapes=[
            pltpu.VMEM((2, n, 1, qw), F32),
            dma((2, 2, 2, n)), dma((2, 2, 2, n)),
        ],
        compiler_params=pltpu.CompilerParams(collective_id=5, has_side_effects=True, vmem_limit_bytes=48 * MIB),
        cost_estimate=pl.CostEstimate(
            flops=2 * tokens * d * n * qw, bytes_accessed=64 * MIB, transcendentals=0
        ),
    )(x, gain, shift, shared, vb, wq, bq)


def mlp_kernel(x_ref, cot_ref, up_ref, bias_ref, down_ref, gn_ref, gb_ref, xg_ref, act_ref, gr_ref, *rest, orders):
    n, seqs, span, d = cot_ref.shape
    (ff_ref, down_grad_ref, x_s, c_s, act_s, gr_s, ff_s, send, recv, a_s, acc,
     gsend, grecv, ssem, rsem, load, own, out, aload, gout) = rest
    hidden = up_ref.shape[1]
    tile, wide = min(512, hidden), 512
    me = lax.axis_index("tensor")
    paths = [list(o) + [0] for o in orders]
    bits_of = [[0] + list(o)[::-1] for o in orders]
    work = [Scatter(bits_of[p], send.at[p], recv.at[p], ssem.at[p], rsem.at[p], shared=2) for p in range(seqs)]

    def last_bit(p, k):
        return max((b for b in paths[p] if k >> b & 1), key=paths[p].index)

    def hop(p, k, bit):
        to = k | (1 << bit)
        src = x_ref.at[p] if k == 0 else xg_ref.at[me ^ k, p]
        return pltpu.make_async_remote_copy(
            src_ref=src, dst_ref=xg_ref.at[me ^ k, p], send_sem=gsend.at[p, to], recv_sem=grecv.at[p, to],
            device_id={"tensor": me ^ (1 << bit)}, device_id_type=MESH,
        )

    def arrival(p, k):
        bit = last_bit(p, k)
        return pltpu.make_async_remote_copy(
            src_ref=x_ref.at[p], dst_ref=xg_ref.at[me ^ k, p], send_sem=gsend.at[p, k], recv_sem=grecv.at[p, k],
            device_id={"tensor": me ^ (1 << bit)}, device_id_type=MESH,
        )

    def slots_at(p, t):
        if t == 0:
            return [0]
        return sorted((k for k in range(2, n, 2) if last_bit(p, k) == paths[p][t - 1]), reverse=True)

    steps = len(paths[0])
    units = [(p, k) for t in range(steps) for i in range(len(slots_at(0, t))) for p in range(seqs) for k in [slots_at(p, t)[i]]]

    def cot_loads(u):
        p, e = units[u]
        return [
            pltpu.make_async_copy(
                cot_ref.at[me ^ (e + j), p], c_s.at[u % 2, j * span : (j + 1) * span], load.at[u % 2, j]
            )
            for j in range(2)
        ]

    def x_loads(u):
        p, e = units[u]
        return [
            pltpu.make_async_copy(
                x_ref.at[p] if e + j == 0 else xg_ref.at[me ^ (e + j), p],
                x_s.at[j * span : (j + 1) * span], load.at[2, j],
            )
            for j in range(2)
        ]

    def hidden_stores(u):
        p, e = units[u]
        return [
            pltpu.make_async_copy(
                buf.at[j * span : (j + 1) * span], ref.at[me ^ (e + j), p], out.at[i, j]
            )
            for i, (buf, ref) in enumerate(((act_s, act_ref), (gr_s, gr_ref)))
            for j in range(2)
        ]

    def ff_stores(u):
        p, e = units[u]
        return [
            pltpu.make_async_copy(ff_s.at[j * span : (j + 1) * span], ff_ref.at[p, e + j], out.at[2, j])
            for j in range(2)
        ]

    waiting = []

    def run(u):
        p, e = units[u]
        for j in range(2):
            if e + j and (e + j) % 2 == 1:
                arrival(p, e + j).wait_recv()
        for c in x_loads(u):
            c.start()
        if u + 1 < len(units):
            for c in cot_loads(u + 1):
                c.start()
        if u:
            for c in hidden_stores(u - 1):
                c.wait()
        for c in x_loads(u) + cot_loads(u):
            c.wait()

        @pl.loop(0, hidden // tile)
        def _(i):
            here = pl.ds(pl.multiple_of(i * tile, tile), tile)
            raised = dot(x_s[...], up_ref[:, here]) + bias_ref[:, here]
            square = raised * raised
            th = jnp.tanh(0.7978845608028654 * raised * (1.0 + 0.044715 * square))
            act_s[:, here] = (0.5 * raised * (1.0 + th)).astype(BF)
            slope = 0.5 * (1.0 + th) + 0.5 * raised * (1.0 - th * th) * (
                0.7978845608028654 * (1.0 + 3 * 0.044715 * square)
            )
            gr = (dot_nt(c_s[u % 2], down_ref[here, :]) * slope).astype(BF)
            gr_s[:, here] = gr
            gb = jnp.sum(gr.astype(F32), axis=0, keepdims=True)
            gb_ref[:, here] = gb if u == 0 else gb_ref[:, here] + gb

        for c in hidden_stores(u):
            c.start()
        while waiting:
            q, k = waiting.pop(0)
            work[q].forward(k)
        if u:
            for c in ff_stores(u - 1):
                c.wait()
        odd, even = work[p].claim(e + 1), work[p].claim(e)

        @pl.loop(0, d // wide)
        def _(i):
            here = pl.ds(pl.multiple_of(i * wide, wide), wide)
            gn = dot_nt(gr_s[...], up_ref[here, :]).astype(BF)
            even[:, here] = gn[:span]
            odd[:, here] = gn[span:]
            ff_s[:, here] = dot(act_s[...], down_ref[:, here]).astype(BF)

        work[p].launch(e + 1)
        for c in ff_stores(u):
            c.start()

    keep = [pltpu.make_async_copy(x_ref.at[p], xg_ref.at[me, p], own.at[p]) for p in range(seqs)]
    greet(range(steps))
    for p in range(seqs):
        hop(p, 0, paths[p][0]).start()
    for p in range(seqs):
        hop(p, 0, 0).start()
        keep[p].start()
    for c in cot_loads(0):
        c.start()
    sent = [(p, 0, b) for p in range(seqs) for b in (paths[p][0], 0)]
    u = 0
    for t in range(steps):
        while u < len(units) and units[u][1] in slots_at(units[u][0], t):
            if t and units[u][0] == 0:
                for p in range(seqs):
                    k = units[u + p][1]
                    arrival(p, k).wait_recv()
                    if t < steps - 1:
                        hop(p, k, paths[p][t]).start()
                        sent.append((p, k, paths[p][t]))
                    hop(p, k, 0).start()
                    sent.append((p, k, 0))
            run(u)
            p, k = units[u]
            if work[p].stage(k) == 1:
                waiting.append((p, k))
            u += 1
        if 0 < t < steps - 1:
            for p in range(seqs):
                for before in range(t - 1, -1, -1):
                    for k in slots_at(p, before):
                        hop(p, k, paths[p][t]).start()
                        sent.append((p, k, paths[p][t]))
    for p, k in waiting:
        work[p].forward(k)
    for c in hidden_stores(len(units) - 1) + ff_stores(len(units) - 1):
        c.wait()

    strip = a_s.shape[2]
    strips = hidden // strip

    def grad_loads(q, j, slot):
        return [
            c
            for r in range(seqs)
            for c in (
                pltpu.make_async_copy(
                    act_ref.at[j, r, :, q * strip : (q + 1) * strip], a_s.at[slot, r * span : (r + 1) * span],
                    aload.at[slot, r],
                ),
                pltpu.make_async_copy(
                    cot_ref.at[j, r], c_s.at[slot, r * span : (r + 1) * span], load.at[slot, r]
                ),
            )
        ]

    def grad_store(q):
        return pltpu.make_async_copy(
            ff_s.at[:strip], down_grad_ref.at[q * strip : (q + 1) * strip], gout
        )

    def grad_strip(q):
        for c in grad_loads(q, 0, 0):
            c.start()

        @pl.loop(0, n)
        def _(j):
            slot = lax.rem(j, 2)

            @pl.when(j + 1 < n)
            def _():
                for c in grad_loads(q, j + 1, 1 - slot):
                    c.start()

            for c in grad_loads(q, j, slot):
                c.wait()
            term = dot_tn(a_s[slot], c_s[slot])

            @pl.when(j == 0)
            def _():
                acc[...] = term

            @pl.when(j > 0)
            def _():
                acc[...] += term

        if q:
            grad_store(q - 1).wait()
        ff_s[:strip] = acc[...].astype(BF)
        grad_store(q).start()

    for q in range(strips // 2):
        grad_strip(q)
    for i in range(2, steps):
        for at in range(n // 2 - 1):
            for p in range(seqs):
                k = scatter_order(bits_of[p])[at]
                if work[p].stage(k) == i:
                    work[p].forward(k)
    for q in range(strips // 2, strips):
        grad_strip(q)
    grad_store(strips - 1).wait()
    for p in range(seqs):
        gn_ref[p] = work[p].total(0)
    for c in keep:
        c.wait()
    for p, k, b in sent:
        hop(p, k, b).wait_send()
    for p in range(seqs):
        work[p].drain()


def mlp(normed, cot, up, bias, down, orders):
    n, seqs, span, d = cot.shape
    ff = up.shape[1]
    strip = min(2 * span, ff // 2, 256)
    dma = pltpu.SemaphoreType.DMA
    hbm, vmem = pl.BlockSpec(memory_space=pl.ANY), pl.BlockSpec(memory_space=pltpu.VMEM)
    return pl.pallas_call(
        functools.partial(mlp_kernel, orders=orders),
        in_specs=[hbm, hbm, vmem, vmem, vmem],
        out_specs=[vmem, vmem, hbm, hbm, hbm, hbm, hbm],
        out_shape=[
            jax.ShapeDtypeStruct((seqs, span, d), F32),
            jax.ShapeDtypeStruct((1, ff), F32),
            jax.ShapeDtypeStruct((n, seqs, span, d), BF),
            jax.ShapeDtypeStruct((n, seqs, span, ff), BF),
            jax.ShapeDtypeStruct((n, seqs, span, ff), BF),
            jax.ShapeDtypeStruct((seqs, n, span, d), BF),
            jax.ShapeDtypeStruct((ff, d), BF),
        ],
        scratch_shapes=[
            pltpu.VMEM((2 * span, d), BF),
            pltpu.VMEM((2, 2 * span, d), BF),
            pltpu.VMEM((2 * span, ff), BF),
            pltpu.VMEM((2 * span, ff), BF),
            pltpu.VMEM((2 * span, d), BF),
            pltpu.VMEM((seqs, n // 2 + 2, span, d), BF),
            pltpu.VMEM((seqs, n - 1, span, d), BF),
            pltpu.VMEM((2, seqs * span, strip), BF),
            pltpu.VMEM((strip, d), F32),
            dma((seqs, n)), dma((seqs, n)), dma((seqs, n)), dma((seqs, n)), dma((3, 2)), dma((seqs,)), dma((3, 2)),
            dma((2, seqs)), dma,
        ],
        compiler_params=pltpu.CompilerParams(collective_id=2, has_side_effects=True, vmem_limit_bytes=60 * MIB),
        cost_estimate=pl.CostEstimate(
            flops=8 * n * seqs * span * d * ff, bytes_accessed=100 * MIB, transcendentals=n * seqs * span * ff
        ),
    )(normed, cot, up, bias, down)


class ScatterParts(Scatter):
    def copy(self, k):
        if self.stage(k):
            return super().copy(k)
        return pltpu.make_async_remote_copy(
            src_ref=self.source.at[k],
            dst_ref=self.recv.at[k - 1],
            send_sem=self.send_sem.at[k],
            recv_sem=self.recv_sem.at[k],
            device_id={"tensor": self.me ^ (1 << self.bits[0])},
            device_id_type=MESH,
        )

    def place(self, k):
        return k // 2 if k % 2 == 0 else -k


def mlp_grads_kernel(gr_ref, x_ref, part_ref, after_ref, up_ref, ff_ref,
                     a_s, b_s, acc, send, recv, ssem, rsem, load, own, *, orders):
    seqs, n = part_ref.shape[:2]
    bits_of = [[0] + list(o)[::-1] for o in orders]
    work = []
    for p in range(seqs):
        w = ScatterParts(bits_of[p], send.at[p], recv.at[p], ssem.at[p], rsem.at[p])
        w.source = part_ref.at[p]
        work.append(w)
    evens = [
        pltpu.make_async_copy(part_ref.at[p, k], send.at[p, k // 2], own.at[p, k // 2])
        for p in range(seqs) for k in range(0, n, 2)
    ]
    wide = acc.shape[0]
    tile = min(256, wide)
    steps = n

    def loads(u):
        return [
            pltpu.make_async_copy(x_ref.at[u], a_s.at[u % 2], load.at[u % 2, 0]),
            pltpu.make_async_copy(gr_ref.at[u], b_s.at[u % 2], load.at[u % 2, 1]),
        ]

    greet(range(len(bits_of[0])))
    for k in range(n - 1, 0, -2):
        for p in range(seqs):
            work[p].launch(k)
    for c in loads(0) + evens:
        c.start()

    def forwards(i):
        for at in range(n // 2 - 1):
            for p in range(seqs):
                k = scatter_order(bits_of[p])[at]
                if work[p].stage(k) == i:
                    work[p].forward(k)

    stages = len(bits_of[0])
    when = {(i - 1) * (steps // (stages - 1)) + 1: i for i in range(1, stages)} if stages > 1 else {}
    when = {min(u + 2 * (i - 1), steps - 1): i for u, i in when.items()}
    for u in range(steps):
        if u + 1 < steps:
            for c in loads(u + 1):
                c.start()
        for c in loads(u):
            c.wait()

        @pl.loop(0, wide // tile)
        def _(i, u=u):
            here = pl.ds(pl.multiple_of(i * tile, tile), tile)
            term = dot_tn(a_s[u % 2, :, here], b_s[u % 2])
            if u == 0:
                acc[here, :] = term
            elif u < n - 1:
                acc[here, :] += term
            else:
                up_ref[here, :] = (acc[here, :] + term).astype(BF)

        if u == 0:
            for c in evens:
                c.wait()
        if u in when:
            forwards(when[u])
    for p in range(seqs):
        ff_ref[p] = work[p].total(0)
        work[p].drain()


def mlp_grads(gr, x, parts, early, orders):
    seqs, n, span, d = parts.shape
    tokens, cols = seqs * span, gr.shape[-1]
    dma = pltpu.SemaphoreType.DMA
    hbm, vmem = pl.BlockSpec(memory_space=pl.ANY), pl.BlockSpec(memory_space=pltpu.VMEM)
    flat = lambda v: v.reshape(n, tokens, v.shape[-1])
    return pl.pallas_call(
        functools.partial(mlp_grads_kernel, orders=orders),
        in_specs=[hbm] * 4,
        out_specs=[vmem] * 2,
        out_shape=[
            jax.ShapeDtypeStruct((d, cols), BF),
            jax.ShapeDtypeStruct((seqs, span, d), F32),
        ],
        scratch_shapes=[
            pltpu.VMEM((2, tokens, d), BF),
            pltpu.VMEM((2, tokens, cols), BF),
            pltpu.VMEM((d, cols), F32),
            pltpu.VMEM((seqs, n // 2, span, d), BF),
            pltpu.VMEM((seqs, n - 1, span, d), BF),
            dma((seqs, n)), dma((seqs, n)), dma((2, 2)), dma((seqs, n // 2)),
        ],
        compiler_params=pltpu.CompilerParams(collective_id=3, has_side_effects=True, vmem_limit_bytes=60 * MIB),
        cost_estimate=pl.CostEstimate(flops=1000, bytes_accessed=MIB, transcendentals=0),
    )(flat(gr), flat(x), parts, early)


def norm_parts(values):
    center = values - jnp.mean(values, axis=-1, keepdims=True)
    scale = lax.rsqrt(jnp.mean(center * center, axis=-1, keepdims=True) + EPSILON)
    return center * scale, scale


def norm_back(unit, scale, gain, grad):
    e = gain * grad
    back = scale * (e - jnp.mean(e, axis=-1, keepdims=True) - unit * jnp.mean(e * unit, axis=-1, keepdims=True))
    return back, jnp.sum(grad * unit, axis=(0, 1)), jnp.sum(grad, axis=(0, 1))


def body(
    inputs, cotangent, documents, padding, attn_gain, attn_shift, query_matrix, query_bias, shared_matrix,
    value_bias, output_matrix, output_bias, mlp_gain, mlp_shift, expansion_weights, up_bias, down_matrix, down_bias,
):
    n = lax.axis_size("tensor")
    me = lax.axis_index("tensor")
    hd = value_bias.shape[0]
    seqs, span, d = inputs.shape
    length = documents.shape[1]
    qw = query_matrix.shape[1]
    heads = qw // hd
    scale = hd**-0.5
    paths = bit_orders(n)
    tokens = seqs * span
    ff = up_bias.shape[0]

    x32 = inputs.astype(F32)
    output_every = lax.all_gather(output_matrix, "tensor")
    cot_every = lax.all_gather(cotangent, "tensor")
    h2, kv, wq, query = first(
        inputs.reshape(tokens, d), attn_gain[None], attn_shift[None], shared_matrix, value_bias[None], query_matrix,
        query_bias[None], seqs, scale * LOG2E, paths,
    )
    kv = kv.swapaxes(0, 1).reshape(seqs, length, 2 * hd)
    keys, values = kv[..., :hd], kv[..., hd:]
    keys_t, values_t = keys.swapaxes(1, 2), values.swapaxes(1, 2)
    query = query.reshape(seqs, span, n * qw)
    like = lambda t, cols: jax.ShapeDtypeStruct((tokens, cols), t)

    begin = lax.dynamic_slice_in_dim(documents, me * span, 1, 1)
    low = (jnp.sum((documents < begin).astype(jnp.int32), axis=1) // span).astype(jnp.int32)
    low = jnp.minimum(low, me)
    at = me.reshape(1).astype(jnp.int32)
    dock = jnp.where(padding == 1, documents, -1)
    dock = xor_order(dock.reshape(seqs, n, span).swapaxes(0, 1), me).swapaxes(0, 1).reshape(seqs, length, 1)
    docq = lax.dynamic_slice_in_dim(documents, me * span, span, 1)
    docq = jnp.concatenate([docq] * heads, axis=1)[:, None, :]
    attended, lse = attention_fwd(query, keys, values_t, low, at, dock, docq, heads, hd)
    a2 = attended.reshape(tokens, n * qw)
    mixed, normed = slot_product(
        o_kernel, [a2, inputs.reshape(tokens, d)], output_every, [output_bias[None], mlp_gain[None], mlp_shift[None]],
        [like(F32, d), like(BF, d)],
    )
    mixed, normed = mixed.reshape(seqs, span, d), normed.reshape(seqs, span, d)
    unit2, scale2 = norm_parts(mixed)

    grad_normed, up_bias_part, normed_every, acts, grs, ff_parts, down_part = mlp(
        normed, cot_every, expansion_weights, up_bias[None], down_matrix, paths
    )
    down_gradient = lax.psum(down_part, "dp")

    cot_wide = cotangent.astype(F32)
    back2, mlp_gain_part, mlp_shift_part = norm_back(unit2, scale2, mlp_gain, grad_normed)
    grad_mixed = cot_wide + back2
    gm2 = grad_mixed.astype(BF).reshape(tokens, d)
    (grad_attended,) = slot_product(do_kernel, [gm2], output_every, [], [like(BF, n * qw)])
    grad_attended = grad_attended.reshape(seqs, span, n * qw)
    dq, dk, dv = attention_bwd(
        query, grad_attended, attended, lse, keys, keys_t, values, low, at, dock, docq, heads, hd, scale
    )
    dq2 = dq.reshape(tokens, n * qw)
    up_part, mlp_branch = mlp_grads(grs, normed_every, ff_parts, dq2, paths)
    block_out = (mixed + mlp_branch + down_bias).astype(BF)

    dkv = jnp.concatenate([dk * LN2, dv], axis=-1).astype(BF).reshape(seqs, n, span, 2 * hd).swapaxes(0, 1)
    wo_own, wq_own, dkv_own, up_gradient = attention_grads(
        a2, gm2, dq2, h2, dkv.reshape(n, tokens, 2 * hd), up_part, down_gradient, paths
    )
    query_bias_part = xor_order(jnp.sum(dq2.astype(F32), axis=0).reshape(n, qw), me).reshape(-1)
    up_bias_every = lax.dynamic_update_slice_in_dim(jnp.zeros((n * ff,), F32), up_bias_part[0], me * ff, 0)
    vector = jnp.concatenate(
        [query_bias_part, mlp_gain_part, mlp_shift_part, jnp.sum(grad_mixed, axis=(0, 1)),
         jnp.sum(cot_wide, axis=(0, 1)), up_bias_every]
    )[None]
    output_gradient, query_gradient, input_grad, late, shared_grad = last(
        wo_own, wq_own, dq2, dkv_own, shared_matrix, h2, inputs.reshape(tokens, d), attn_gain[None],
        grad_mixed.reshape(tokens, d), vector, wq, paths[0],
    )
    input_grad = input_grad.reshape(seqs, span, d)
    if lax.axis_size("dp") != 4:
        output_gradient, query_gradient = (
            g.astype(F32) for g in lax.psum((output_gradient.astype(BF), query_gradient.astype(BF)), "dp")
        )
    late = late[0]
    ends = [d, 2 * d, 2 * d + hd, 2 * d + hd + n * qw]
    ends += [ends[-1] + d * (i + 1) for i in range(4)]
    (attn_gain_grad, attn_shift_grad, value_bias_grad, query_bias_all, mlp_gain_grad, mlp_shift_grad,
     output_bias_grad, down_bias_grad, up_bias_all) = jnp.split(late, ends)
    query_bias_grad = lax.dynamic_slice_in_dim(query_bias_all, me * qw, qw, 0)
    up_bias_grad = lax.dynamic_slice_in_dim(up_bias_all, me * ff, ff, 0)
    query_gradient, up_gradient, down_gradient = query_gradient.T, up_gradient.astype(F32), down_gradient.astype(F32)
    return (
        block_out, input_grad, attn_gain_grad, attn_shift_grad, query_gradient, query_bias_grad, shared_grad,
        value_bias_grad, output_gradient, output_bias_grad, mlp_gain_grad, mlp_shift_grad, up_gradient, up_bias_grad,
        down_gradient, down_bias_grad,
    )


def solution(mesh):
    act = P("dp", "tensor", None)
    cols, rows, vec, rep = P(None, "tensor"), P("tensor", None), P("tensor"), P()
    ids = P("dp", None)
    return jax.shard_map(
        body,
        mesh=mesh,
        in_specs=(act, act, ids, ids, rep, rep, cols, vec, rep, rep, rows, rep, rep, rep, cols, vec, rows, rep),
        out_specs=(act, act, rep, rep, cols, vec, rep, rep, rows, rep, rep, rep, cols, vec, rows, rep),
        check_vma=False,
    )
```

```python
import functools

import jax
import jax.numpy as jnp
from jax import lax
from jax.experimental import pallas as pl
from jax.experimental.pallas import tpu as pltpu
from jax.sharding import PartitionSpec as P

EPSILON = 1e-05
LOG2E = 1.4426950408889634
LN2 = 0.6931471805599453
BF = jnp.bfloat16
F32 = jnp.float32
NEG = -1e30
MIB = 1024 * 1024


def dot(a, b):
    return lax.dot_general(a, b, (((1,), (0,)), ((), ())), preferred_element_type=F32)


def dot_nt(a, b):
    return lax.dot_general(a, b, (((1,), (1,)), ((), ())), preferred_element_type=F32)


def dot_tn(a, b):
    return lax.dot_general(a, b, (((0,), (0,)), ((), ())), preferred_element_type=F32)


def bit_orders(n):
    bits = list(range(1, n.bit_length() - 1))
    return bits, bits[::-1]


def xor_order(x, me):
    n = x.shape[0]
    rest = x.shape[1:]
    for bit in range(n.bit_length() - 1):
        pairs = x.reshape((n >> (bit + 1), 2, 1 << bit) + rest)
        x = jnp.where((me >> bit) & 1 == 1, jnp.flip(pairs, 1), pairs).reshape((n,) + rest)
    return x


def stack_heads(block, heads, hd):
    return jnp.concatenate([block[:, i * hd : (i + 1) * hd] for i in range(heads)], axis=0)


def diagonal_mask(rows, cols, same):
    key_at = lax.broadcasted_iota(jnp.int32, (rows, cols), 0)
    query_at = lax.broadcasted_iota(jnp.int32, (rows, cols), 1) % rows
    return (same & (key_at < query_at)) | (key_at == query_at)


def below_blocks(low, at, step, carry):
    even = at - at % 2
    carry = lax.fori_loop(jnp.maximum(low, even), at, lambda b, c: step(b ^ at, 1, c), carry)
    return lax.fori_loop(low // 2, at // 2, lambda p, c: step((p ^ (at // 2)) * 2, 2, c), carry)


def attention_fwd_kernel(low_ref, at_ref, q_ref, k_ref, vt_ref, dock_ref, docq_ref, o_ref, lse_ref, *, heads, hd):
    row = pl.program_id(0)
    span = q_ref.shape[1]
    at = at_ref[0]
    q2 = stack_heads(q_ref[0], heads, hd)
    docq = docq_ref[0]

    def scores(slot, count):
        here = pl.ds(pl.multiple_of(slot * span, count * span), count * span)
        s = dot_nt(k_ref[0, here, :], q2)
        same = dock_ref[0, here, :] == docq
        return s, same, here

    s, same, here = scores(0, 1)
    s = jnp.where(diagonal_mask(span, heads * span, same), s, NEG)
    top = jnp.max(s, axis=0, keepdims=True)
    p = jnp.exp2(s - top)
    total = jnp.sum(p, axis=0, keepdims=True)
    acc = dot(vt_ref[0, :, here], p.astype(BF))

    def step(slot, count, carry):
        top, total, acc = carry
        s, same, here = scores(slot, count)
        s = jnp.where(same, s, NEG)
        new = jnp.maximum(top, jnp.max(s, axis=0, keepdims=True))
        shrink = jnp.exp2(top - new)
        p = jnp.exp2(s - new)
        total = total * shrink + jnp.sum(p, axis=0, keepdims=True)
        acc = acc * shrink + dot(vt_ref[0, :, here], p.astype(BF))
        return new, total, acc

    carry = below_blocks(low_ref[row], at, step, (top, total, acc))
    top, total, acc = carry
    out = (acc / total).T.astype(BF)
    for i in range(heads):
        o_ref[0, :, i * hd : (i + 1) * hd] = out[i * span : (i + 1) * span]
    lse_ref[0, 0] = top + jnp.log2(total)


def attention_bwd_kernel(
    low_ref, at_ref, q_ref, do_ref, o_ref, lse_ref, k_ref, kt_ref, v_ref, dock_ref, docq_ref,
    dq_ref, dk_ref, dv_ref, *, heads, hd, scale,
):
    row = pl.program_id(0)
    span = q_ref.shape[1]
    at = at_ref[0]

    @pl.when(pl.program_id(1) == 0)
    def _():
        dk_ref[...] = jnp.zeros_like(dk_ref)
        dv_ref[...] = jnp.zeros_like(dv_ref)

    q2 = stack_heads(q_ref[0], heads, hd)
    do2 = stack_heads(do_ref[0], heads, hd)
    o2 = stack_heads(o_ref[0], heads, hd)
    delta = jnp.sum((do2.astype(F32) * o2.astype(F32)).T, axis=0, keepdims=True)
    lse = lse_ref[0, 0]
    docq = docq_ref[0]

    def one(slot, count, dqt, diagonal=False):
        here = pl.ds(pl.multiple_of(slot * span, count * span), count * span)
        s = dot_nt(k_ref[0, here, :], q2)
        same = dock_ref[0, here, :] == docq
        if diagonal:
            same = diagonal_mask(span, heads * span, same)
        p = jnp.where(same, jnp.exp2(s - lse), 0.0)
        dp = dot_nt(v_ref[0, here, :], do2)
        ds = (p * (dp - delta)).astype(BF)
        dk_ref[0, here, :] += dot(ds, q2)
        dv_ref[0, here, :] += dot(p.astype(BF), do2)
        return dqt + dot(kt_ref[0, :, here], ds)

    dqt = one(0, 1, jnp.zeros((hd, heads * span), F32), True)
    dqt = below_blocks(low_ref[row], at, one, dqt)
    dq = (dqt * scale).T.astype(BF)
    for i in range(heads):
        dq_ref[0, :, i * hd : (i + 1) * hd] = dq[i * span : (i + 1) * span]


def attention_fwd(q, k, vt, low, at, dock, docq, heads, hd):
    rows, span, width = q.shape
    length = k.shape[1]
    groups = width // (heads * hd)
    gw = heads * hd
    return pl.pallas_call(
        functools.partial(attention_fwd_kernel, heads=heads, hd=hd),
        grid_spec=pltpu.PrefetchScalarGridSpec(
            num_scalar_prefetch=2,
            grid=(rows, groups),
            in_specs=[
                pl.BlockSpec((1, span, gw), lambda r, g, *_: (r, 0, g)),
                pl.BlockSpec((1, length, hd), lambda r, g, *_: (r, 0, 0)),
                pl.BlockSpec((1, hd, length), lambda r, g, *_: (r, 0, 0)),
                pl.BlockSpec((1, length, 1), lambda r, g, *_: (r, 0, 0)),
                pl.BlockSpec((1, 1, heads * span), lambda r, g, *_: (r, 0, 0)),
            ],
            out_specs=[
                pl.BlockSpec((1, span, gw), lambda r, g, *_: (r, 0, g)),
                pl.BlockSpec((1, 1, 1, heads * span), lambda r, g, *_: (r, g, 0, 0)),
            ],
        ),
        out_shape=[
            jax.ShapeDtypeStruct((rows, span, width), BF),
            jax.ShapeDtypeStruct((rows, groups, 1, heads * span), F32),
        ],
        compiler_params=pltpu.CompilerParams(vmem_limit_bytes=24 * MIB),
        cost_estimate=pl.CostEstimate(
            flops=2 * rows * span * width * length, bytes_accessed=8 * MIB, transcendentals=rows * span * length
        ),
    )(low, at, q, k, vt, dock, docq)


def attention_bwd(q, do, o, lse, k, kt, v, low, at, dock, docq, heads, hd, scale):
    rows, span, width = q.shape
    length = k.shape[1]
    groups = width // (heads * hd)
    gw = heads * hd
    blk = pl.BlockSpec((1, span, gw), lambda r, g, *_: (r, 0, g))
    full = pl.BlockSpec((1, length, hd), lambda r, g, *_: (r, 0, 0))
    return pl.pallas_call(
        functools.partial(attention_bwd_kernel, heads=heads, hd=hd, scale=scale),
        grid_spec=pltpu.PrefetchScalarGridSpec(
            num_scalar_prefetch=2,
            grid=(rows, groups),
            in_specs=[
                blk,
                blk,
                blk,
                pl.BlockSpec((1, 1, 1, heads * span), lambda r, g, *_: (r, g, 0, 0)),
                full,
                pl.BlockSpec((1, hd, length), lambda r, g, *_: (r, 0, 0)),
                full,
                pl.BlockSpec((1, length, 1), lambda r, g, *_: (r, 0, 0)),
                pl.BlockSpec((1, 1, heads * span), lambda r, g, *_: (r, 0, 0)),
            ],
            out_specs=[blk, full, full],
        ),
        out_shape=[
            jax.ShapeDtypeStruct((rows, span, width), BF),
            jax.ShapeDtypeStruct((rows, length, hd), F32),
            jax.ShapeDtypeStruct((rows, length, hd), F32),
        ],
        compiler_params=pltpu.CompilerParams(vmem_limit_bytes=32 * MIB),
        cost_estimate=pl.CostEstimate(
            flops=1000, bytes_accessed=MIB, transcendentals=0
        ),
    )(low, at, q, do, o, lse, k, kt, v, dock, docq)


def fill_rows(whole_ref, every_ref):
    n, rows, _ = every_ref.shape
    me = lax.axis_index("tensor")
    for k in range(n):
        whole_ref[k * rows : (k + 1) * rows, :] = every_ref[me ^ k]


def o_kernel(a_ref, x_ref, w_ref, b_ref, gain_ref, shift_ref, mixed_ref, normed_ref, w_s):
    @pl.when(pl.program_id(0) == 0)
    def _():
        fill_rows(w_s, w_ref)

    mixed = x_ref[...].astype(F32) + dot(a_ref[...], w_s[...]) + b_ref[...]
    mixed_ref[...] = mixed
    unit, _ = norm_parts(mixed)
    normed_ref[...] = (unit * gain_ref[...] + shift_ref[...]).astype(BF)


def do_kernel(g_ref, w_ref, o_ref, w_s):
    @pl.when(pl.program_id(0) == 0)
    def _():
        fill_rows(w_s, w_ref)

    o_ref[...] = dot_nt(g_ref[...], w_s[...]).astype(BF)


def slot_product(kernel, tiled, weights, fixed, outs):
    n, rows, cols = weights.shape
    tokens = tiled[0].shape[0]
    tile = tokens // 2
    still = lambda a: pl.BlockSpec(a.shape, lambda i: (0,) * a.ndim, pipeline_mode=pl.Buffered(1))
    flow = lambda a: pl.BlockSpec((tile, a.shape[1]), lambda i: (i, 0))
    return pl.pallas_call(
        kernel,
        grid=(2,),
        in_specs=[flow(a) for a in tiled] + [still(weights)] + [still(a) for a in fixed],
        out_specs=[flow(o) for o in outs],
        out_shape=outs,
        scratch_shapes=[pltpu.VMEM((n * rows, cols), BF)],
        compiler_params=pltpu.CompilerParams(vmem_limit_bytes=48 * MIB),
        cost_estimate=pl.CostEstimate(
            flops=2 * tokens * n * rows * cols, bytes_accessed=2 * n * rows * cols + 8 * MIB, transcendentals=0
        ),
    )(*tiled, weights, *fixed)


MESH = pl.DeviceIdType.MESH


def greet(bits, line=False, dp_bits=()):
    me, z = lax.axis_index("tensor"), lax.axis_index("dp")
    barrier = pltpu.get_barrier_semaphore()
    for bit in bits:
        pl.semaphore_signal(barrier, inc=1, device_id={"tensor": me ^ (1 << bit)}, device_id_type=MESH)
    count = len(bits)
    flips = {1 << bit for bit in dp_bits} | ({1} if line else set())
    for flip in sorted(flips):
        pl.semaphore_signal(barrier, inc=1, device_id={"dp": z ^ flip}, device_id_type=MESH)
    count += len(flips)
    if line:
        inner = (z == 1) | (z == 2)

        @pl.when(inner)
        def _():
            pl.semaphore_signal(barrier, inc=1, device_id={"dp": 3 - z}, device_id_type=MESH)

        count = count + inner.astype(jnp.int32)
    pl.semaphore_wait(barrier, count)


class Line:
    def __init__(self, own, near, far, sem):
        self.own, self.near, self.far, self.sem = own, near, far, sem
        self.z = lax.axis_index("dp")
        self.inner = (self.z == 1) | (self.z == 2)
        self.outer = jnp.logical_not(self.inner)

    def copy(self, i, hop):
        src = (self.own, self.near, self.near)[hop].at[i]
        dst = (self.near, self.far, self.near)[hop].at[i]
        return pltpu.make_async_remote_copy(
            src_ref=src, dst_ref=dst, send_sem=self.sem.at[0, hop, i], recv_sem=self.sem.at[1, hop, i],
            device_id={"dp": 3 - self.z if hop == 1 else self.z ^ 1}, device_id_type=MESH,
        )

    def start(self, i):
        @pl.when(self.outer)
        def _():
            self.copy(i, 0).start()

    def middle(self, i, own):
        @pl.when(self.inner)
        def _():
            self.copy(i, 0).wait_recv()
            self.near[i] = (own().astype(F32) + self.near[i].astype(F32)).astype(BF)
            self.copy(i, 1).start()

    def back(self, i):
        @pl.when(self.inner)
        def _():
            self.copy(i, 1).wait()
            self.near[i] = (self.near[i].astype(F32) + self.far[i].astype(F32)).astype(BF)
            self.copy(i, 2).start()

    def close(self, i):
        @pl.when(self.outer)
        def _():
            self.copy(i, 0).wait_send()
            self.copy(i, 2).wait_recv()

        @pl.when(self.inner)
        def _():
            self.copy(i, 2).wait_send()


class Scatter:
    def __init__(self, bits, send, recv, send_sem, recv_sem, shared=0):
        self.bits, self.send, self.recv, self.send_sem, self.recv_sem = bits, send, recv, send_sem, recv_sem
        self.me = lax.axis_index("tensor")
        self.shared = shared
        self.busy = {}

    def place(self, k):
        if not self.shared:
            return k
        return k // 2 if k % 2 == 0 else (1 << len(self.bits)) // 2 + k // 2 % self.shared

    def claim(self, k):
        place = self.place(k)
        if place in self.busy:
            self.copy(self.busy.pop(place)).wait_send()
        return self.send.at[place]

    def launch(self, k):
        self.copy(k).start()
        self.busy[self.place(k)] = k

    def stage(self, k):
        return next((i for i, b in enumerate(self.bits) if k >> b & 1), len(self.bits))

    def copy(self, k):
        bit = self.bits[self.stage(k)]
        return pltpu.make_async_remote_copy(
            src_ref=self.send.at[self.place(k)],
            dst_ref=self.recv.at[k - 1],
            send_sem=self.send_sem.at[k],
            recv_sem=self.recv_sem.at[k],
            device_id={"tensor": self.me ^ (1 << bit)},
            device_id_type=MESH,
        )

    def put(self, k, value):
        self.claim(k)[...] = value.astype(BF)
        if self.stage(k) == 0:
            self.launch(k)

    def total(self, k):
        value = self.send[self.place(k)].astype(F32)
        for bit in self.bits[: self.stage(k)]:
            self.copy(k | (1 << bit)).wait_recv()
            value = value + self.recv[(k | (1 << bit)) - 1].astype(F32)
        return value

    def forward(self, k):
        self.send[self.place(k)] = self.total(k).astype(BF)
        self.launch(k)

    def drain(self):
        for k in self.busy.values():
            self.copy(k).wait_send()
        self.busy = {}


def scatter_order(bits):
    n = 1 << len(bits)
    rank = lambda k: next(i for i, b in enumerate(bits) if k >> b & 1)
    return sorted(range(2, n, 2), key=lambda k: (rank(k), -k))


def attention_grads_kernel(a_ref, gm_ref, dq_ref, h_ref, dkv_ref, up_ref, after_ref, wo_ref, wq_ref, kv_ref, sum_ref,
                           send, recv, ksend, krecv, far, own, ssem, rsem, ksem, krsem, zsem, psem,
                           *, orders, line, qw):
    bits_of = [[0] + list(o)[::-1] for o in orders]
    count = len(bits_of[0])
    n = 1 << count
    half = gm_ref.shape[1] // 2
    greet(range(count), line)
    chain = Line(up_ref, sum_ref, far, zsem)
    pieces = up_ref.shape[0]
    if line:
        for i in range(pieces):
            chain.start(i)

    def own_piece(i):
        def value():
            c = pltpu.make_async_copy(up_ref.at[i], own, psem)
            c.start()
            c.wait()
            return own[...]

        return value

    ahead = [0]

    def chain_to(middles):
        while line and ahead[0] < min(middles, pieces):
            chain.middle(ahead[0], own_piece(ahead[0]))
            ahead[0] += 1
            if ahead[0] > 1:
                chain.back(ahead[0] - 2)

    kv = Scatter(bits_of[0], ksend, krecv, ksem, krsem)
    for k in list(range(1, n, 2)) + list(range(0, n, 2)):
        kv.put(k, dkv_ref[k])

    pairs = ((a_ref, gm_ref, wo_ref), (dq_ref, h_ref, wq_ref))
    work = [
        [Scatter(bits_of[p], send.at[m, p], recv.at[m, p], ssem.at[m, p], rsem.at[m, p], shared=2) for p in range(2)]
        for m in range(2)
    ]
    sequence = [scatter_order(b) for b in bits_of]

    def products(m):
        x, y, _ = pairs[m]
        for i in range(n // 2):
            for p in range(2):
                k = (sequence[p] + [0])[i]
                for j in (k + 1, k):
                    work[m][p].put(j, dot_tn(x[:, j * qw : (j + 1) * qw], y[:, p * half : (p + 1) * half]))

    def stage(m, i):
        for at in range(n // 2 - 1):
            for p in range(2):
                k = sequence[p][at]
                if work[m][p].stage(k) == i:
                    work[m][p].forward(k)

    def kv_stage(i):
        for k in scatter_order(bits_of[0]):
            if kv.stage(k) == i:
                kv.forward(k)

    def finish(m):
        for p in range(2):
            pairs[m][2][p] = work[m][p].total(0).astype(BF)

    products(0)
    stage(0, 1)
    chain_to(1)
    products(1)
    chain_to(3)
    for i in range(1, count):
        kv_stage(i)
        if i + 1 < count:
            stage(0, i + 1)
            chain_to(2 * i + 2)
        else:
            chain_to(7)
            finish(0)
            chain_to(8)
        stage(1, i)
    chain_to(10)
    kv_ref[...] = kv.total(0).astype(BF)
    chain_to(pieces)
    finish(1)
    if line:
        chain.back(pieces - 1)
        for i in range(pieces):
            chain.close(i)
    kv.drain()
    for m in range(2):
        for p in range(2):
            work[m][p].drain()


def attention_grads(a, gm, dq, h, dkv, up, early, orders):
    n, line = lax.axis_size("tensor"), lax.axis_size("dp") == 4
    tokens, d = gm.shape
    qw = a.shape[1] // n
    slot = dkv.shape[1:]
    rows, cols = up.shape
    pieces = rows // 128
    up = up.reshape(pieces, rows // pieces, cols)
    wait = up.shape if line else (1, 16, 128)
    dma = pltpu.SemaphoreType.DMA
    vmem, hbm = pl.BlockSpec(memory_space=pltpu.VMEM), pl.BlockSpec(memory_space=pl.ANY)
    wo, wq, kv, total = pl.pallas_call(
        functools.partial(attention_grads_kernel, orders=orders, line=line, qw=qw),
        in_specs=[vmem] * 5 + [hbm] * 2,
        out_specs=[vmem] * 4,
        out_shape=[
            jax.ShapeDtypeStruct((2, qw, d // 2), BF),
            jax.ShapeDtypeStruct((2, qw, d // 2), BF),
            jax.ShapeDtypeStruct(slot, BF),
            jax.ShapeDtypeStruct(wait, BF),
        ],
        scratch_shapes=[
            pltpu.VMEM((2, 2, n // 2 + 2, qw, d // 2), BF),
            pltpu.VMEM((2, 2, n - 1, qw, d // 2), BF),
            pltpu.VMEM((n,) + slot, BF),
            pltpu.VMEM((n - 1,) + slot, BF),
            pltpu.VMEM(wait, BF),
            pltpu.VMEM(up.shape[1:], BF),
            dma((2, 2, n)), dma((2, 2, n)), dma((n,)), dma((n,)), dma((2, 3, pieces)), dma,
        ],
        compiler_params=pltpu.CompilerParams(
            collective_id=1, has_side_effects=True, vmem_limit_bytes=60 * MIB
        ),
        cost_estimate=pl.CostEstimate(flops=1000, bytes_accessed=MIB, transcendentals=0),
    )(a, gm, dq, h, dkv, up, early)
    up = up.reshape(rows, cols)
    return wo, wq, kv, total.reshape(rows, cols) if line else lax.psum(up, "dp")


def last_kernel(wo_ref, wq_ref, dq_ref, kv_ref, shared_ref, h_ref, x_ref, gain_ref, mixed_ref, qb_ref, w_ref, *refs,
                order, line, eps_rows):
    count = len(order) + 1
    n = 1 << count
    (wog_ref, wqg_ref, grad_ref, late_ref, sg_ref,
     w_s, near, far, part, send, recv, dsend, drecv, piece_s, gathered, vsend, vrecv, esend, erecv,
     zsem, ssem, rsem, dsem, gsem, vsem, esem) = refs
    me, z = lax.axis_index("tensor"), lax.axis_index("dp")
    dp_bits = range(lax.axis_size("dp").bit_length() - 1)
    tokens, d = x_ref.shape
    hd = kv_ref.shape[1] // 2
    piece = d // n
    greet(range(count), line, dp_bits)

    pieces = wo_ref.shape[0]
    owns = (wo_ref, wq_ref)
    chains = []
    if line:
        for i, ref in enumerate(owns):
            chains.append(Line(ref, near.at[i], far.at[i], zsem.at[i]))
    ahead = [0, 0]

    def chain_to(middles):
        while line and ahead[1] < min(middles + 2, len(owns) * pieces):
            i, p = divmod(ahead[1], pieces)
            chains[i].start(p)
            ahead[1] += 1
        while line and ahead[0] < min(middles, len(owns) * pieces):
            i, p = divmod(ahead[0], pieces)
            chains[i].middle(p, lambda: owns[i][p])
            ahead[0] += 1
            if ahead[0] > 1:
                i, p = divmod(ahead[0] - 2, pieces)
                chains[i].back(p)

    chain_to(0)

    part[...] = dot_tn(h_ref[...], kv_ref[...])
    scatter = Scatter([0] + list(order)[::-1], send, recv, ssem, rsem)
    for k in list(range(1, n, 2)) + list(range(0, n, 2)):
        scatter.put(k, part[pl.ds(pl.multiple_of((me ^ k) * piece, piece), piece), :])
    for k in range(n):
        w_s[:, k * w_ref.shape[2] : (k + 1) * w_ref.shape[2]] = w_ref[k]
    hops = [("tensor", me, b) for b in range(count)] + [("dp", z, b) for b in dp_bits]
    pending = []

    def swap_start(buffers, sems, value, i, axis, at, bit):
        buffers[0][i] = value
        c = pltpu.make_async_remote_copy(
            src_ref=buffers[0].at[i], dst_ref=buffers[1].at[i], send_sem=sems.at[0, i], recv_sem=sems.at[1, i],
            device_id={axis: at ^ (1 << bit)}, device_id_type=MESH,
        )
        c.start()
        pending.append(c)
        return lambda value: (c.wait_recv(), value + buffers[1][i])[1]

    size = 2 * d + hd
    tail = late_ref.at[:, size:]
    front = late_ref.at[:, :size]
    early_done, last_done, piece_done = [None], [None], [None]

    def early(i):
        if early_done[0] is not None:
            tail[...] = early_done[0](tail[...])
            early_done[0] = None
        if i < len(hops):
            early_done[0] = swap_start((esend, erecv), esem, tail[...], i, *hops[i])

    def late(i):
        if last_done[0] is not None:
            front[...] = last_done[0](front[...])
            last_done[0] = None
        if i < len(hops):
            last_done[0] = swap_start((vsend, vrecv), vsem, front[...], i, *hops[i])

    def shared_sum(i):
        if piece_done[0] is not None:
            piece_s[...] = piece_done[0](piece_s[...])
            piece_done[0] = None
        if i < len(dp_bits):
            piece_done[0] = swap_start((dsend, drecv), dsem, piece_s[...], i, "dp", z, dp_bits[i])

    tail[...] = qb_ref[...]
    early(0)
    at = 1
    chain_to(at)
    for i in range(1, count):
        for k in scatter_order(scatter.bits):
            if scatter.stage(k) == i:
                scatter.forward(k)
        early(i)
        at += 1
        chain_to(at)
    piece_s[...] = scatter.total(0)
    shared_sum(0)

    gain_part, shift_part = jnp.zeros((1, d), F32), jnp.zeros((1, d), F32)
    for t in range(tokens // eps_rows):
        rows = slice(t * eps_rows, (t + 1) * eps_rows)
        grad = dot_nt(dq_ref[rows], w_s[...]) + dot_nt(kv_ref[rows], shared_ref[...])
        unit, scale = norm_parts(x_ref[rows].astype(F32))
        e = gain_ref[...] * grad
        back = e - jnp.mean(e, axis=-1, keepdims=True) - unit * jnp.mean(e * unit, axis=-1, keepdims=True)
        grad_ref[rows] = mixed_ref[rows] + scale * back
        gain_part += jnp.sum(grad * unit, axis=0, keepdims=True)
        shift_part += jnp.sum(grad, axis=0, keepdims=True)
        if t + 1 < len(dp_bits):
            shared_sum(t + 1)
        if count + t < len(hops):
            early(count + t)
        at += 2
        chain_to(at)
    late_ref[:, :d] = gain_part
    late_ref[:, d : 2 * d] = shift_part
    late_ref[:, 2 * d : size] = jnp.sum(kv_ref[:, hd:].astype(F32), axis=0, keepdims=True)
    late(0)
    for i in range(max(tokens // eps_rows + 1, 1), len(dp_bits) + 1):
        shared_sum(i)
    shared_sum(len(dp_bits))
    for i in range(count + tokens // eps_rows, len(hops) + 1):
        early(i)
    early(len(hops))
    gathered[me] = piece_s[...].astype(BF)
    sent, held, step = [], [0], 0
    for bit in list(order) + [0]:
        new = []
        for k in held:
            c = pltpu.make_async_remote_copy(
                src_ref=gathered.at[me ^ k], dst_ref=gathered.at[me ^ k], send_sem=gsem.at[0, k | (1 << bit)],
                recv_sem=gsem.at[1, k | (1 << bit)], device_id={"tensor": me ^ (1 << bit)}, device_id_type=MESH,
            )
            c.start()
            sent.append(c)
            new.append(c)
        step += 1
        late(step)
        at += 1
        chain_to(at)
        for c in new:
            c.wait_recv()
        held = held + [k | (1 << bit) for k in held]
    while step < len(hops):
        step += 1
        late(step)
        at += 1
        chain_to(at)
    chain_to(len(owns) * pieces)
    if line:
        chains[-1].back(pieces - 1)
    for k in range(n):
        sg_ref[k * piece : (k + 1) * piece] = gathered[k].astype(F32)
    if line:
        for c in chains:
            for p in range(pieces):
                c.close(p)
    half, high = d // 2, wo_ref.shape[1]
    for j in range(pieces):
        values = [near[i, j] if line else owns[i][j] for i in range(len(owns))]
        p, q = divmod(j, pieces // 2)
        for ref, value in zip((wog_ref, wqg_ref), values):
            ref[q * high : (q + 1) * high, p * half : (p + 1) * half] = value.astype(F32)
    for c in pending + sent:
        c.wait_send()
    scatter.drain()


def last(wo, wq, dq, kv, shared, h, x, gain, mixed, qb, w, order):
    n, dp = lax.axis_size("tensor"), lax.axis_size("dp")
    line = dp == 4
    tokens, d = x.shape
    qw = wo.shape[1]
    cuts = 4
    wo, wq = (v.reshape(cuts, -1, d // 2) for v in (wo, wq))
    piece, width = d // n, kv.shape[1]
    size = 2 * d + qb.shape[1] + width // 2
    bits = n.bit_length() - 1
    dbits = dp.bit_length() - 1
    dma = pltpu.SemaphoreType.DMA
    vmem = pl.BlockSpec(memory_space=pltpu.VMEM)
    item = (2,) + wo.shape
    return pl.pallas_call(
        functools.partial(last_kernel, order=order, line=line, eps_rows=tokens // 2),
        in_specs=[vmem] * 11,
        out_specs=[vmem] * 5,
        out_shape=[
            jax.ShapeDtypeStruct((qw, d), F32),
            jax.ShapeDtypeStruct((qw, d), F32),
            jax.ShapeDtypeStruct((tokens, d), F32),
            jax.ShapeDtypeStruct((1, size), F32),
            jax.ShapeDtypeStruct((d, width), F32),
        ],
        scratch_shapes=[
            pltpu.VMEM((d, n * qw), BF),
            pltpu.VMEM(item, BF),
            pltpu.VMEM(item, BF),
            pltpu.VMEM((d, width), F32),
            pltpu.VMEM((n, piece, width), BF),
            pltpu.VMEM((n - 1, piece, width), BF),
            pltpu.VMEM((dbits, piece, width), F32),
            pltpu.VMEM((dbits, piece, width), F32),
            pltpu.VMEM((piece, width), F32),
            pltpu.VMEM((n, piece, width), BF),
            pltpu.VMEM((bits + dbits, 1, size - qb.shape[1]), F32),
            pltpu.VMEM((bits + dbits, 1, size - qb.shape[1]), F32),
            pltpu.VMEM((bits + dbits,) + qb.shape, F32),
            pltpu.VMEM((bits + dbits,) + qb.shape, F32),
            dma((2, 2, 3, cuts)), dma((n,)), dma((n,)), dma((2, dbits)), dma((2, n)), dma((2, bits + dbits)), dma((2, bits + dbits)),
        ],
        compiler_params=pltpu.CompilerParams(
            collective_id=4, has_side_effects=True, vmem_limit_bytes=60 * MIB
        ),
        cost_estimate=pl.CostEstimate(flops=1000, bytes_accessed=MIB, transcendentals=0),
    )(wo, wq, dq, kv, shared, h, x, gain, mixed, qb, w)


class Gather:
    def __init__(self, orders, refs, send_sem, recv_sem):
        self.paths = [list(o) + [0] for o in orders]
        self.refs, self.send_sem, self.recv_sem = refs, send_sem, recv_sem
        self.me = lax.axis_index("tensor")
        self.n = 1 << len(self.paths[0])
        self.sent = []

    def last_bit(self, p, k):
        return max((b for b in self.paths[p] if k >> b & 1), key=self.paths[p].index)

    def copies(self, p, k, bit):
        to = k | (1 << bit)
        return [
            pltpu.make_async_remote_copy(
                src_ref=ref(p, k), dst_ref=ref(p, to), send_sem=self.send_sem.at[i, p, to],
                recv_sem=self.recv_sem.at[i, p, to], device_id={"tensor": self.me ^ (1 << bit)}, device_id_type=MESH,
            )
            for i, ref in enumerate(self.refs)
        ]

    def hop(self, p, k, bit):
        for c in self.copies(p, k, bit):
            c.start()
            self.sent.append(c)

    def arrived(self, p, k):
        bit = self.last_bit(p, k)
        for c in self.copies(p, k ^ (1 << bit), bit):
            c.wait_recv()

    def at_step(self, p, t):
        if t == 0:
            return [0]
        return sorted((k for k in range(2, self.n, 2) if self.last_bit(p, k) == self.paths[p][t - 1]), reverse=True)

    def drain(self):
        for c in self.sent:
            c.wait_send()


def first_kernel(x_ref, gain_ref, shift_ref, shared_ref, vb_ref, wq_ref, bq_ref, h_ref, kv_ref, w_ref, q_ref,
                 bias, send_sem, recv_sem, *, orders, factor, rows):
    n, d, qw = w_ref.shape
    seqs, span = kv_ref.shape[1:3]
    hd = vb_ref.shape[1]
    half = d // 2
    tokens = x_ref.shape[0]
    greet(range(len(orders[0]) + 1))
    weights = Gather(
        orders, [lambda p, k: w_ref.at[k, p * half : (p + 1) * half], lambda p, k: bias.at[p, k]],
        send_sem.at[0], recv_sem.at[0],
    )
    shared = Gather(orders, [lambda p, k: kv_ref.at[k, p]], send_sem.at[1], recv_sem.at[1])
    steps = len(weights.paths[0])
    w_ref[0] = wq_ref[...]
    for p in range(2):
        bias[p, 0] = bq_ref[...]
    for p in range(2):
        weights.hop(p, 0, weights.paths[p][0])
    for p in range(2):
        weights.hop(p, 0, 0)
    for t in range(tokens // rows):
        here = slice(t * rows, (t + 1) * rows)
        unit, _ = norm_parts(x_ref[here].astype(F32))
        h_ref[here] = (unit * gain_ref[...] + shift_ref[...]).astype(BF)
    kv = dot(h_ref[...], shared_ref[...])
    for r in range(seqs):
        here = slice(r * span, (r + 1) * span)
        kv_ref[0, r, :, :hd] = kv[here, :hd].astype(BF)
        kv_ref[0, r, :, hd:] = (kv[here, hd:] + vb_ref[...]).astype(BF)
    for p in range(2):
        shared.hop(p, 0, shared.paths[p][0])
    for p in range(2):
        shared.hop(p, 0, 0)

    def product(k):
        q_ref[:, k * qw : (k + 1) * qw] = ((dot(h_ref[...], w_ref[k]) + bias[0, k]) * factor).astype(BF)

    product(0)
    ready = [1]
    for t in range(1, steps):
        for g in (weights, shared):
            for p in range(2):
                for k in g.at_step(p, t):
                    g.arrived(p, k)
                    if t < steps - 1:
                        g.hop(p, k, g.paths[p][t])
                    g.hop(p, k, 0)
            if t < steps - 1:
                for p in range(2):
                    for before in range(t - 1, -1, -1):
                        for k in g.at_step(p, before):
                            g.hop(p, k, g.paths[p][t])
    for k in range(1, n, 2):
        for p in range(2):
            weights.arrived(p, k)
        product(k)
        if k > 1:
            product(k - 1)
    for k in range(1, n, 2):
        for p in range(2):
            shared.arrived(p, k)
    weights.drain()
    shared.drain()


def first(x, gain, shift, shared, vb, wq, bq, seqs, factor, orders):
    n = lax.axis_size("tensor")
    tokens, d = x.shape
    qw = wq.shape[1]
    dma = pltpu.SemaphoreType.DMA
    vmem = pl.BlockSpec(memory_space=pltpu.VMEM)
    return pl.pallas_call(
        functools.partial(first_kernel, orders=orders, factor=factor, rows=tokens // 4),
        in_specs=[vmem] * 7,
        out_specs=[vmem] * 4,
        out_shape=[
            jax.ShapeDtypeStruct((tokens, d), BF),
            jax.ShapeDtypeStruct((n, seqs, tokens // seqs, shared.shape[1]), BF),
            jax.ShapeDtypeStruct((n, d, qw), BF),
            jax.ShapeDtypeStruct((tokens, n * qw), BF),
        ],
        scratch_shapes=[
            pltpu.VMEM((2, n, 1, qw), F32),
            dma((2, 2, 2, n)), dma((2, 2, 2, n)),
        ],
        compiler_params=pltpu.CompilerParams(collective_id=5, has_side_effects=True, vmem_limit_bytes=48 * MIB),
        cost_estimate=pl.CostEstimate(
            flops=2 * tokens * d * n * qw, bytes_accessed=64 * MIB, transcendentals=0
        ),
    )(x, gain, shift, shared, vb, wq, bq)


def mlp_kernel(x_ref, cot_ref, up_ref, bias_ref, down_ref, gn_ref, gb_ref, xg_ref, act_ref, gr_ref, *rest, orders):
    n, seqs, span, d = cot_ref.shape
    (ff_ref, down_grad_ref, x_s, c_s, act_s, gr_s, ff_s, send, recv, a_s, acc,
     gsend, grecv, ssem, rsem, load, own, out, aload, gout) = rest
    hidden = up_ref.shape[1]
    tile, wide = min(512, hidden), 512
    me = lax.axis_index("tensor")
    paths = [list(o) + [0] for o in orders]
    bits_of = [[0] + list(o)[::-1] for o in orders]
    work = [Scatter(bits_of[p], send.at[p], recv.at[p], ssem.at[p], rsem.at[p], shared=2) for p in range(seqs)]

    def last_bit(p, k):
        return max((b for b in paths[p] if k >> b & 1), key=paths[p].index)

    def hop(p, k, bit):
        to = k | (1 << bit)
        src = x_ref.at[p] if k == 0 else xg_ref.at[me ^ k, p]
        return pltpu.make_async_remote_copy(
            src_ref=src, dst_ref=xg_ref.at[me ^ k, p], send_sem=gsend.at[p, to], recv_sem=grecv.at[p, to],
            device_id={"tensor": me ^ (1 << bit)}, device_id_type=MESH,
        )

    def arrival(p, k):
        bit = last_bit(p, k)
        return pltpu.make_async_remote_copy(
            src_ref=x_ref.at[p], dst_ref=xg_ref.at[me ^ k, p], send_sem=gsend.at[p, k], recv_sem=grecv.at[p, k],
            device_id={"tensor": me ^ (1 << bit)}, device_id_type=MESH,
        )

    def slots_at(p, t):
        if t == 0:
            return [0]
        return sorted((k for k in range(2, n, 2) if last_bit(p, k) == paths[p][t - 1]), reverse=True)

    steps = len(paths[0])
    units = [(p, k) for t in range(steps) for i in range(len(slots_at(0, t))) for p in range(seqs) for k in [slots_at(p, t)[i]]]

    def cot_loads(u):
        p, e = units[u]
        return [
            pltpu.make_async_copy(
                cot_ref.at[me ^ (e + j), p], c_s.at[u % 2, j * span : (j + 1) * span], load.at[u % 2, j]
            )
            for j in range(2)
        ]

    def x_loads(u):
        p, e = units[u]
        return [
            pltpu.make_async_copy(
                x_ref.at[p] if e + j == 0 else xg_ref.at[me ^ (e + j), p],
                x_s.at[j * span : (j + 1) * span], load.at[2, j],
            )
            for j in range(2)
        ]

    def hidden_stores(u):
        p, e = units[u]
        return [
            pltpu.make_async_copy(
                buf.at[j * span : (j + 1) * span], ref.at[me ^ (e + j), p], out.at[i, j]
            )
            for i, (buf, ref) in enumerate(((act_s, act_ref), (gr_s, gr_ref)))
            for j in range(2)
        ]

    def ff_stores(u):
        p, e = units[u]
        return [
            pltpu.make_async_copy(ff_s.at[j * span : (j + 1) * span], ff_ref.at[p, e + j], out.at[2, j])
            for j in range(2)
        ]

    waiting = []

    def run(u):
        p, e = units[u]
        for j in range(2):
            if e + j and (e + j) % 2 == 1:
                arrival(p, e + j).wait_recv()
        for c in x_loads(u):
            c.start()
        if u + 1 < len(units):
            for c in cot_loads(u + 1):
                c.start()
        if u:
            for c in hidden_stores(u - 1):
                c.wait()
        for c in x_loads(u) + cot_loads(u):
            c.wait()

        @pl.loop(0, hidden // tile)
        def _(i):
            here = pl.ds(pl.multiple_of(i * tile, tile), tile)
            raised = dot(x_s[...], up_ref[:, here]) + bias_ref[:, here]
            square = raised * raised
            th = jnp.tanh(0.7978845608028654 * raised * (1.0 + 0.044715 * square))
            act_s[:, here] = (0.5 * raised * (1.0 + th)).astype(BF)
            slope = 0.5 * (1.0 + th) + 0.5 * raised * (1.0 - th * th) * (
                0.7978845608028654 * (1.0 + 3 * 0.044715 * square)
            )
            gr = (dot_nt(c_s[u % 2], down_ref[here, :]) * slope).astype(BF)
            gr_s[:, here] = gr
            gb = jnp.sum(gr.astype(F32), axis=0, keepdims=True)
            gb_ref[:, here] = gb if u == 0 else gb_ref[:, here] + gb

        for c in hidden_stores(u):
            c.start()
        while waiting:
            q, k = waiting.pop(0)
            work[q].forward(k)
        if u:
            for c in ff_stores(u - 1):
                c.wait()
        odd, even = work[p].claim(e + 1), work[p].claim(e)

        @pl.loop(0, d // wide)
        def _(i):
            here = pl.ds(pl.multiple_of(i * wide, wide), wide)
            gn = dot_nt(gr_s[...], up_ref[here, :]).astype(BF)
            even[:, here] = gn[:span]
            odd[:, here] = gn[span:]
            ff_s[:, here] = dot(act_s[...], down_ref[:, here]).astype(BF)

        work[p].launch(e + 1)
        for c in ff_stores(u):
            c.start()

    keep = [pltpu.make_async_copy(x_ref.at[p], xg_ref.at[me, p], own.at[p]) for p in range(seqs)]
    greet(range(steps))
    for p in range(seqs):
        hop(p, 0, paths[p][0]).start()
    for p in range(seqs):
        hop(p, 0, 0).start()
        keep[p].start()
    for c in cot_loads(0):
        c.start()
    sent = [(p, 0, b) for p in range(seqs) for b in (paths[p][0], 0)]
    u = 0
    for t in range(steps):
        while u < len(units) and units[u][1] in slots_at(units[u][0], t):
            if t and units[u][0] == 0:
                for p in range(seqs):
                    k = units[u + p][1]
                    arrival(p, k).wait_recv()
                    if t < steps - 1:
                        hop(p, k, paths[p][t]).start()
                        sent.append((p, k, paths[p][t]))
                    hop(p, k, 0).start()
                    sent.append((p, k, 0))
            run(u)
            p, k = units[u]
            if work[p].stage(k) == 1:
                waiting.append((p, k))
            u += 1
        if 0 < t < steps - 1:
            for p in range(seqs):
                for before in range(t - 1, -1, -1):
                    for k in slots_at(p, before):
                        hop(p, k, paths[p][t]).start()
                        sent.append((p, k, paths[p][t]))
    for p, k in waiting:
        work[p].forward(k)
    for c in hidden_stores(len(units) - 1) + ff_stores(len(units) - 1):
        c.wait()

    strip = a_s.shape[2]
    strips = hidden // strip

    def grad_loads(q, j, slot):
        return [
            c
            for r in range(seqs)
            for c in (
                pltpu.make_async_copy(
                    act_ref.at[j, r, :, q * strip : (q + 1) * strip], a_s.at[slot, r * span : (r + 1) * span],
                    aload.at[slot, r],
                ),
                pltpu.make_async_copy(
                    cot_ref.at[j, r], c_s.at[slot, r * span : (r + 1) * span], load.at[slot, r]
                ),
            )
        ]

    def grad_store(q):
        return pltpu.make_async_copy(
            ff_s.at[:strip], down_grad_ref.at[q * strip : (q + 1) * strip], gout
        )

    def grad_strip(q):
        for c in grad_loads(q, 0, 0):
            c.start()

        @pl.loop(0, n)
        def _(j):
            slot = lax.rem(j, 2)

            @pl.when(j + 1 < n)
            def _():
                for c in grad_loads(q, j + 1, 1 - slot):
                    c.start()

            for c in grad_loads(q, j, slot):
                c.wait()
            term = dot_tn(a_s[slot], c_s[slot])

            @pl.when(j == 0)
            def _():
                acc[...] = term

            @pl.when(j > 0)
            def _():
                acc[...] += term

        if q:
            grad_store(q - 1).wait()
        ff_s[:strip] = acc[...].astype(BF)
        grad_store(q).start()

    for q in range(strips // 2):
        grad_strip(q)
    for i in range(2, steps):
        for at in range(n // 2 - 1):
            for p in range(seqs):
                k = scatter_order(bits_of[p])[at]
                if work[p].stage(k) == i:
                    work[p].forward(k)
    for q in range(strips // 2, strips):
        grad_strip(q)
    grad_store(strips - 1).wait()
    for p in range(seqs):
        gn_ref[p] = work[p].total(0)
    for c in keep:
        c.wait()
    for p, k, b in sent:
        hop(p, k, b).wait_send()
    for p in range(seqs):
        work[p].drain()


def mlp(normed, cot, up, bias, down, orders):
    n, seqs, span, d = cot.shape
    ff = up.shape[1]
    strip = min(2 * span, ff // 2, 256)
    dma = pltpu.SemaphoreType.DMA
    hbm, vmem = pl.BlockSpec(memory_space=pl.ANY), pl.BlockSpec(memory_space=pltpu.VMEM)
    return pl.pallas_call(
        functools.partial(mlp_kernel, orders=orders),
        in_specs=[hbm, hbm, vmem, vmem, vmem],
        out_specs=[vmem, vmem, hbm, hbm, hbm, hbm, hbm],
        out_shape=[
            jax.ShapeDtypeStruct((seqs, span, d), F32),
            jax.ShapeDtypeStruct((1, ff), F32),
            jax.ShapeDtypeStruct((n, seqs, span, d), BF),
            jax.ShapeDtypeStruct((n, seqs, span, ff), BF),
            jax.ShapeDtypeStruct((n, seqs, span, ff), BF),
            jax.ShapeDtypeStruct((seqs, n, span, d), BF),
            jax.ShapeDtypeStruct((ff, d), BF),
        ],
        scratch_shapes=[
            pltpu.VMEM((2 * span, d), BF),
            pltpu.VMEM((2, 2 * span, d), BF),
            pltpu.VMEM((2 * span, ff), BF),
            pltpu.VMEM((2 * span, ff), BF),
            pltpu.VMEM((2 * span, d), BF),
            pltpu.VMEM((seqs, n // 2 + 2, span, d), BF),
            pltpu.VMEM((seqs, n - 1, span, d), BF),
            pltpu.VMEM((2, seqs * span, strip), BF),
            pltpu.VMEM((strip, d), F32),
            dma((seqs, n)), dma((seqs, n)), dma((seqs, n)), dma((seqs, n)), dma((3, 2)), dma((seqs,)), dma((3, 2)),
            dma((2, seqs)), dma,
        ],
        compiler_params=pltpu.CompilerParams(collective_id=2, has_side_effects=True, vmem_limit_bytes=60 * MIB),
        cost_estimate=pl.CostEstimate(
            flops=8 * n * seqs * span * d * ff, bytes_accessed=100 * MIB, transcendentals=n * seqs * span * ff
        ),
    )(normed, cot, up, bias, down)


class ScatterParts(Scatter):
    def copy(self, k):
        if self.stage(k):
            return super().copy(k)
        return pltpu.make_async_remote_copy(
            src_ref=self.source.at[k],
            dst_ref=self.recv.at[k - 1],
            send_sem=self.send_sem.at[k],
            recv_sem=self.recv_sem.at[k],
            device_id={"tensor": self.me ^ (1 << self.bits[0])},
            device_id_type=MESH,
        )

    def place(self, k):
        return k // 2 if k % 2 == 0 else -k


def mlp_grads_kernel(gr_ref, x_ref, part_ref, after_ref, up_ref, ff_ref,
                     a_s, b_s, acc, send, recv, ssem, rsem, load, own, *, orders):
    seqs, n = part_ref.shape[:2]
    bits_of = [[0] + list(o)[::-1] for o in orders]
    work = []
    for p in range(seqs):
        w = ScatterParts(bits_of[p], send.at[p], recv.at[p], ssem.at[p], rsem.at[p])
        w.source = part_ref.at[p]
        work.append(w)
    evens = [
        pltpu.make_async_copy(part_ref.at[p, k], send.at[p, k // 2], own.at[p, k // 2])
        for p in range(seqs) for k in range(0, n, 2)
    ]
    wide = acc.shape[0]
    tile = min(256, wide)
    steps = n

    def loads(u):
        return [
            pltpu.make_async_copy(x_ref.at[u], a_s.at[u % 2], load.at[u % 2, 0]),
            pltpu.make_async_copy(gr_ref.at[u], b_s.at[u % 2], load.at[u % 2, 1]),
        ]

    greet(range(len(bits_of[0])))
    for k in range(n - 1, 0, -2):
        for p in range(seqs):
            work[p].launch(k)
    for c in loads(0) + evens:
        c.start()

    def forwards(i):
        for at in range(n // 2 - 1):
            for p in range(seqs):
                k = scatter_order(bits_of[p])[at]
                if work[p].stage(k) == i:
                    work[p].forward(k)

    stages = len(bits_of[0])
    when = {(i - 1) * (steps // (stages - 1)) + 1: i for i in range(1, stages)} if stages > 1 else {}
    when = {min(u + 2 * (i - 1), steps - 1): i for u, i in when.items()}
    for u in range(steps):
        if u + 1 < steps:
            for c in loads(u + 1):
                c.start()
        for c in loads(u):
            c.wait()

        @pl.loop(0, wide // tile)
        def _(i, u=u):
            here = pl.ds(pl.multiple_of(i * tile, tile), tile)
            term = dot_tn(a_s[u % 2, :, here], b_s[u % 2])
            if u == 0:
                acc[here, :] = term
            elif u < n - 1:
                acc[here, :] += term
            else:
                up_ref[here, :] = (acc[here, :] + term).astype(BF)

        if u == 0:
            for c in evens:
                c.wait()
        if u in when:
            forwards(when[u])
    for p in range(seqs):
        ff_ref[p] = work[p].total(0)
        work[p].drain()


def mlp_grads(gr, x, parts, early, orders):
    seqs, n, span, d = parts.shape
    tokens, cols = seqs * span, gr.shape[-1]
    dma = pltpu.SemaphoreType.DMA
    hbm, vmem = pl.BlockSpec(memory_space=pl.ANY), pl.BlockSpec(memory_space=pltpu.VMEM)
    flat = lambda v: v.reshape(n, tokens, v.shape[-1])
    return pl.pallas_call(
        functools.partial(mlp_grads_kernel, orders=orders),
        in_specs=[hbm] * 4,
        out_specs=[vmem] * 2,
        out_shape=[
            jax.ShapeDtypeStruct((d, cols), BF),
            jax.ShapeDtypeStruct((seqs, span, d), F32),
        ],
        scratch_shapes=[
            pltpu.VMEM((2, tokens, d), BF),
            pltpu.VMEM((2, tokens, cols), BF),
            pltpu.VMEM((d, cols), F32),
            pltpu.VMEM((seqs, n // 2, span, d), BF),
            pltpu.VMEM((seqs, n - 1, span, d), BF),
            dma((seqs, n)), dma((seqs, n)), dma((2, 2)), dma((seqs, n // 2)),
        ],
        compiler_params=pltpu.CompilerParams(collective_id=3, has_side_effects=True, vmem_limit_bytes=60 * MIB),
        cost_estimate=pl.CostEstimate(flops=1000, bytes_accessed=MIB, transcendentals=0),
    )(flat(gr), flat(x), parts, early)


def norm_parts(values):
    center = values - jnp.mean(values, axis=-1, keepdims=True)
    scale = lax.rsqrt(jnp.mean(center * center, axis=-1, keepdims=True) + EPSILON)
    return center * scale, scale


def norm_back(unit, scale, gain, grad):
    e = gain * grad
    back = scale * (e - jnp.mean(e, axis=-1, keepdims=True) - unit * jnp.mean(e * unit, axis=-1, keepdims=True))
    return back, jnp.sum(grad * unit, axis=(0, 1)), jnp.sum(grad, axis=(0, 1))


def body(
    inputs, cotangent, documents, padding, attn_gain, attn_shift, query_matrix, query_bias, shared_matrix,
    value_bias, output_matrix, output_bias, mlp_gain, mlp_shift, expansion_weights, up_bias, down_matrix, down_bias,
):
    n = lax.axis_size("tensor")
    me = lax.axis_index("tensor")
    hd = value_bias.shape[0]
    seqs, span, d = inputs.shape
    length = documents.shape[1]
    qw = query_matrix.shape[1]
    heads = qw // hd
    scale = hd**-0.5
    paths = bit_orders(n)
    tokens = seqs * span
    ff = up_bias.shape[0]

    x32 = inputs.astype(F32)
    output_every = lax.all_gather(output_matrix, "tensor")
    cot_every = lax.all_gather(cotangent, "tensor")
    h2, kv, wq, query = first(
        inputs.reshape(tokens, d), attn_gain[None], attn_shift[None], shared_matrix, value_bias[None], query_matrix,
        query_bias[None], seqs, scale * LOG2E, paths,
    )
    kv = kv.swapaxes(0, 1).reshape(seqs, length, 2 * hd)
    keys, values = kv[..., :hd], kv[..., hd:]
    keys_t, values_t = keys.swapaxes(1, 2), values.swapaxes(1, 2)
    query = query.reshape(seqs, span, n * qw)
    like = lambda t, cols: jax.ShapeDtypeStruct((tokens, cols), t)

    begin = lax.dynamic_slice_in_dim(documents, me * span, 1, 1)
    low = (jnp.sum((documents < begin).astype(jnp.int32), axis=1) // span).astype(jnp.int32)
    low = jnp.minimum(low, me)
    at = me.reshape(1).astype(jnp.int32)
    dock = jnp.where(padding == 1, documents, -1)
    dock = xor_order(dock.reshape(seqs, n, span).swapaxes(0, 1), me).swapaxes(0, 1).reshape(seqs, length, 1)
    docq = lax.dynamic_slice_in_dim(documents, me * span, span, 1)
    docq = jnp.concatenate([docq] * heads, axis=1)[:, None, :]
    attended, lse = attention_fwd(query, keys, values_t, low, at, dock, docq, heads, hd)
    a2 = attended.reshape(tokens, n * qw)
    mixed, normed = slot_product(
        o_kernel, [a2, inputs.reshape(tokens, d)], output_every, [output_bias[None], mlp_gain[None], mlp_shift[None]],
        [like(F32, d), like(BF, d)],
    )
    mixed, normed = mixed.reshape(seqs, span, d), normed.reshape(seqs, span, d)
    unit2, scale2 = norm_parts(mixed)

    grad_normed, up_bias_part, normed_every, acts, grs, ff_parts, down_part = mlp(
        normed, cot_every, expansion_weights, up_bias[None], down_matrix, paths
    )
    down_gradient = lax.psum(down_part, "dp")

    cot_wide = cotangent.astype(F32)
    back2, mlp_gain_part, mlp_shift_part = norm_back(unit2, scale2, mlp_gain, grad_normed)
    grad_mixed = cot_wide + back2
    gm2 = grad_mixed.astype(BF).reshape(tokens, d)
    (grad_attended,) = slot_product(do_kernel, [gm2], output_every, [], [like(BF, n * qw)])
    grad_attended = grad_attended.reshape(seqs, span, n * qw)
    dq, dk, dv = attention_bwd(
        query, grad_attended, attended, lse, keys, keys_t, values, low, at, dock, docq, heads, hd, scale
    )
    dq2 = dq.reshape(tokens, n * qw)
    up_part, mlp_branch = mlp_grads(grs, normed_every, ff_parts, dq2, paths)
    block_out = (mixed + mlp_branch + down_bias).astype(BF)

    dkv = jnp.concatenate([dk * LN2, dv], axis=-1).astype(BF).reshape(seqs, n, span, 2 * hd).swapaxes(0, 1)
    wo_own, wq_own, dkv_own, up_gradient = attention_grads(
        a2, gm2, dq2, h2, dkv.reshape(n, tokens, 2 * hd), up_part, down_gradient, paths
    )
    query_bias_part = xor_order(jnp.sum(dq2.astype(F32), axis=0).reshape(n, qw), me).reshape(-1)
    up_bias_every = lax.dynamic_update_slice_in_dim(jnp.zeros((n * ff,), F32), up_bias_part[0], me * ff, 0)
    vector = jnp.concatenate(
        [query_bias_part, mlp_gain_part, mlp_shift_part, jnp.sum(grad_mixed, axis=(0, 1)),
         jnp.sum(cot_wide, axis=(0, 1)), up_bias_every]
    )[None]
    output_gradient, query_gradient, input_grad, late, shared_grad = last(
        wo_own, wq_own, dq2, dkv_own, shared_matrix, h2, inputs.reshape(tokens, d), attn_gain[None],
        grad_mixed.reshape(tokens, d), vector, wq, paths[0],
    )
    input_grad = input_grad.reshape(seqs, span, d)
    if lax.axis_size("dp") != 4:
        output_gradient, query_gradient = (
            g.astype(F32) for g in lax.psum((output_gradient.astype(BF), query_gradient.astype(BF)), "dp")
        )
    late = late[0]
    ends = [d, 2 * d, 2 * d + hd, 2 * d + hd + n * qw]
    ends += [ends[-1] + d * (i + 1) for i in range(4)]
    (attn_gain_grad, attn_shift_grad, value_bias_grad, query_bias_all, mlp_gain_grad, mlp_shift_grad,
     output_bias_grad, down_bias_grad, up_bias_all) = jnp.split(late, ends)
    query_bias_grad = lax.dynamic_slice_in_dim(query_bias_all, me * qw, qw, 0)
    up_bias_grad = lax.dynamic_slice_in_dim(up_bias_all, me * ff, ff, 0)
    query_gradient, up_gradient, down_gradient = query_gradient.T, up_gradient.astype(F32), down_gradient.astype(F32)
    return (
        block_out, input_grad, attn_gain_grad, attn_shift_grad, query_gradient, query_bias_grad, shared_grad,
        value_bias_grad, output_gradient, output_bias_grad, mlp_gain_grad, mlp_shift_grad, up_gradient, up_bias_grad,
        down_gradient, down_bias_grad,
    )


def solution(mesh):
    act = P("dp", "tensor", None)
    cols, rows, vec, rep = P(None, "tensor"), P("tensor", None), P("tensor"), P()
    ids = P("dp", None)
    return jax.shard_map(
        body,
        mesh=mesh,
        in_specs=(act, act, ids, ids, rep, rep, cols, vec, rep, rep, rows, rep, rep, rep, cols, vec, rows, rep),
        out_specs=(act, act, rep, rep, cols, vec, rep, rep, rows, rep, rep, rep, cols, vec, rows, rep),
        check_vma=False,
    )
```

```python
import functools

import jax
import jax.numpy as jnp
from jax import lax
from jax.experimental import pallas as pl
from jax.experimental.pallas import tpu as pltpu
from jax.sharding import PartitionSpec as P

EPSILON = 1e-05
LOG2E = 1.4426950408889634
LN2 = 0.6931471805599453
BF = jnp.bfloat16
F32 = jnp.float32
NEG = -1e30
MIB = 1024 * 1024


def dot(a, b):
    return lax.dot_general(a, b, (((1,), (0,)), ((), ())), preferred_element_type=F32)


def dot_nt(a, b):
    return lax.dot_general(a, b, (((1,), (1,)), ((), ())), preferred_element_type=F32)


def dot_tn(a, b):
    return lax.dot_general(a, b, (((0,), (0,)), ((), ())), preferred_element_type=F32)


def bit_orders(n):
    bits = list(range(1, n.bit_length() - 1))
    return bits, bits[::-1]


def xor_order(x, me):
    n = x.shape[0]
    rest = x.shape[1:]
    for bit in range(n.bit_length() - 1):
        pairs = x.reshape((n >> (bit + 1), 2, 1 << bit) + rest)
        x = jnp.where((me >> bit) & 1 == 1, jnp.flip(pairs, 1), pairs).reshape((n,) + rest)
    return x


def stack_heads(block, heads, hd):
    return jnp.concatenate([block[:, i * hd : (i + 1) * hd] for i in range(heads)], axis=0)


def diagonal_mask(rows, cols, same):
    key_at = lax.broadcasted_iota(jnp.int32, (rows, cols), 0)
    query_at = lax.broadcasted_iota(jnp.int32, (rows, cols), 1) % rows
    return (same & (key_at < query_at)) | (key_at == query_at)


def below_blocks(low, at, step, carry):
    even = at - at % 2
    carry = lax.fori_loop(jnp.maximum(low, even), at, lambda b, c: step(b ^ at, 1, c), carry)
    return lax.fori_loop(low // 2, at // 2, lambda p, c: step((p ^ (at // 2)) * 2, 2, c), carry)


def attention_fwd_kernel(low_ref, at_ref, q_ref, k_ref, vt_ref, dock_ref, docq_ref, o_ref, lse_ref, *, heads, hd):
    row = pl.program_id(0)
    span = q_ref.shape[1]
    at = at_ref[0]
    q2 = stack_heads(q_ref[0], heads, hd)
    docq = docq_ref[0]

    def scores(slot, count):
        here = pl.ds(pl.multiple_of(slot * span, count * span), count * span)
        s = dot_nt(k_ref[0, here, :], q2)
        same = dock_ref[0, here, :] == docq
        return s, same, here

    s, same, here = scores(0, 1)
    s = jnp.where(diagonal_mask(span, heads * span, same), s, NEG)
    top = jnp.max(s, axis=0, keepdims=True)
    p = jnp.exp2(s - top)
    total = jnp.sum(p, axis=0, keepdims=True)
    acc = dot(vt_ref[0, :, here], p.astype(BF))

    def step(slot, count, carry):
        top, total, acc = carry
        s, same, here = scores(slot, count)
        s = jnp.where(same, s, NEG)
        new = jnp.maximum(top, jnp.max(s, axis=0, keepdims=True))
        shrink = jnp.exp2(top - new)
        p = jnp.exp2(s - new)
        total = total * shrink + jnp.sum(p, axis=0, keepdims=True)
        acc = acc * shrink + dot(vt_ref[0, :, here], p.astype(BF))
        return new, total, acc

    carry = below_blocks(low_ref[row], at, step, (top, total, acc))
    top, total, acc = carry
    out = (acc / total).T.astype(BF)
    for i in range(heads):
        o_ref[0, :, i * hd : (i + 1) * hd] = out[i * span : (i + 1) * span]
    lse_ref[0, 0] = top + jnp.log2(total)


def attention_bwd_kernel(
    low_ref, at_ref, q_ref, do_ref, o_ref, lse_ref, k_ref, kt_ref, v_ref, dock_ref, docq_ref,
    dq_ref, dk_ref, dv_ref, *, heads, hd, scale,
):
    row = pl.program_id(0)
    span = q_ref.shape[1]
    at = at_ref[0]

    @pl.when(pl.program_id(1) == 0)
    def _():
        dk_ref[...] = jnp.zeros_like(dk_ref)
        dv_ref[...] = jnp.zeros_like(dv_ref)

    q2 = stack_heads(q_ref[0], heads, hd)
    do2 = stack_heads(do_ref[0], heads, hd)
    o2 = stack_heads(o_ref[0], heads, hd)
    delta = jnp.sum((do2.astype(F32) * o2.astype(F32)).T, axis=0, keepdims=True)
    lse = lse_ref[0, 0]
    docq = docq_ref[0]

    def one(slot, count, dqt, diagonal=False):
        here = pl.ds(pl.multiple_of(slot * span, count * span), count * span)
        s = dot_nt(k_ref[0, here, :], q2)
        same = dock_ref[0, here, :] == docq
        if diagonal:
            same = diagonal_mask(span, heads * span, same)
        p = jnp.where(same, jnp.exp2(s - lse), 0.0)
        dp = dot_nt(v_ref[0, here, :], do2)
        ds = (p * (dp - delta)).astype(BF)
        dk_ref[0, here, :] += dot(ds, q2)
        dv_ref[0, here, :] += dot(p.astype(BF), do2)
        return dqt + dot(kt_ref[0, :, here], ds)

    dqt = one(0, 1, jnp.zeros((hd, heads * span), F32), True)
    dqt = below_blocks(low_ref[row], at, one, dqt)
    dq = (dqt * scale).T.astype(BF)
    for i in range(heads):
        dq_ref[0, :, i * hd : (i + 1) * hd] = dq[i * span : (i + 1) * span]


def attention_fwd(q, k, vt, low, at, dock, docq, heads, hd):
    rows, span, width = q.shape
    length = k.shape[1]
    groups = width // (heads * hd)
    gw = heads * hd
    return pl.pallas_call(
        functools.partial(attention_fwd_kernel, heads=heads, hd=hd),
        grid_spec=pltpu.PrefetchScalarGridSpec(
            num_scalar_prefetch=2,
            grid=(rows, groups),
            in_specs=[
                pl.BlockSpec((1, span, gw), lambda r, g, *_: (r, 0, g)),
                pl.BlockSpec((1, length, hd), lambda r, g, *_: (r, 0, 0)),
                pl.BlockSpec((1, hd, length), lambda r, g, *_: (r, 0, 0)),
                pl.BlockSpec((1, length, 1), lambda r, g, *_: (r, 0, 0)),
                pl.BlockSpec((1, 1, heads * span), lambda r, g, *_: (r, 0, 0)),
            ],
            out_specs=[
                pl.BlockSpec((1, span, gw), lambda r, g, *_: (r, 0, g)),
                pl.BlockSpec((1, 1, 1, heads * span), lambda r, g, *_: (r, g, 0, 0)),
            ],
        ),
        out_shape=[
            jax.ShapeDtypeStruct((rows, span, width), BF),
            jax.ShapeDtypeStruct((rows, groups, 1, heads * span), F32),
        ],
        compiler_params=pltpu.CompilerParams(vmem_limit_bytes=24 * MIB),
        cost_estimate=pl.CostEstimate(
            flops=2 * rows * span * width * length, bytes_accessed=8 * MIB, transcendentals=rows * span * length
        ),
    )(low, at, q, k, vt, dock, docq)


def attention_bwd(q, do, o, lse, k, kt, v, low, at, dock, docq, heads, hd, scale):
    rows, span, width = q.shape
    length = k.shape[1]
    groups = width // (heads * hd)
    gw = heads * hd
    blk = pl.BlockSpec((1, span, gw), lambda r, g, *_: (r, 0, g))
    full = pl.BlockSpec((1, length, hd), lambda r, g, *_: (r, 0, 0))
    return pl.pallas_call(
        functools.partial(attention_bwd_kernel, heads=heads, hd=hd, scale=scale),
        grid_spec=pltpu.PrefetchScalarGridSpec(
            num_scalar_prefetch=2,
            grid=(rows, groups),
            in_specs=[
                blk,
                blk,
                blk,
                pl.BlockSpec((1, 1, 1, heads * span), lambda r, g, *_: (r, g, 0, 0)),
                full,
                pl.BlockSpec((1, hd, length), lambda r, g, *_: (r, 0, 0)),
                full,
                pl.BlockSpec((1, length, 1), lambda r, g, *_: (r, 0, 0)),
                pl.BlockSpec((1, 1, heads * span), lambda r, g, *_: (r, 0, 0)),
            ],
            out_specs=[blk, full, full],
        ),
        out_shape=[
            jax.ShapeDtypeStruct((rows, span, width), BF),
            jax.ShapeDtypeStruct((rows, length, hd), F32),
            jax.ShapeDtypeStruct((rows, length, hd), F32),
        ],
        compiler_params=pltpu.CompilerParams(vmem_limit_bytes=32 * MIB),
        cost_estimate=pl.CostEstimate(
            flops=1000, bytes_accessed=MIB, transcendentals=0
        ),
    )(low, at, q, do, o, lse, k, kt, v, dock, docq)


def fill_rows(whole_ref, every_ref):
    n, rows, _ = every_ref.shape
    me = lax.axis_index("tensor")
    for k in range(n):
        whole_ref[k * rows : (k + 1) * rows, :] = every_ref[me ^ k]


def o_kernel(a_ref, x_ref, w_ref, b_ref, gain_ref, shift_ref, mixed_ref, normed_ref, w_s):
    @pl.when(pl.program_id(0) == 0)
    def _():
        fill_rows(w_s, w_ref)

    mixed = x_ref[...].astype(F32) + dot(a_ref[...], w_s[...]) + b_ref[...]
    mixed_ref[...] = mixed
    unit, _ = norm_parts(mixed)
    normed_ref[...] = (unit * gain_ref[...] + shift_ref[...]).astype(BF)


def do_kernel(g_ref, w_ref, o_ref, w_s):
    @pl.when(pl.program_id(0) == 0)
    def _():
        fill_rows(w_s, w_ref)

    o_ref[...] = dot_nt(g_ref[...], w_s[...]).astype(BF)


def slot_product(kernel, tiled, weights, fixed, outs):
    n, rows, cols = weights.shape
    tokens = tiled[0].shape[0]
    tile = tokens // 2
    still = lambda a: pl.BlockSpec(a.shape, lambda i: (0,) * a.ndim, pipeline_mode=pl.Buffered(1))
    flow = lambda a: pl.BlockSpec((tile, a.shape[1]), lambda i: (i, 0))
    return pl.pallas_call(
        kernel,
        grid=(2,),
        in_specs=[flow(a) for a in tiled] + [still(weights)] + [still(a) for a in fixed],
        out_specs=[flow(o) for o in outs],
        out_shape=outs,
        scratch_shapes=[pltpu.VMEM((n * rows, cols), BF)],
        compiler_params=pltpu.CompilerParams(vmem_limit_bytes=48 * MIB),
        cost_estimate=pl.CostEstimate(
            flops=2 * tokens * n * rows * cols, bytes_accessed=2 * n * rows * cols + 8 * MIB, transcendentals=0
        ),
    )(*tiled, weights, *fixed)


MESH = pl.DeviceIdType.MESH


def greet(bits, line=False, dp_bits=()):
    me, z = lax.axis_index("tensor"), lax.axis_index("dp")
    barrier = pltpu.get_barrier_semaphore()
    for bit in bits:
        pl.semaphore_signal(barrier, inc=1, device_id={"tensor": me ^ (1 << bit)}, device_id_type=MESH)
    count = len(bits)
    flips = {1 << bit for bit in dp_bits} | ({1} if line else set())
    for flip in sorted(flips):
        pl.semaphore_signal(barrier, inc=1, device_id={"dp": z ^ flip}, device_id_type=MESH)
    count += len(flips)
    if line:
        inner = (z == 1) | (z == 2)

        @pl.when(inner)
        def _():
            pl.semaphore_signal(barrier, inc=1, device_id={"dp": 3 - z}, device_id_type=MESH)

        count = count + inner.astype(jnp.int32)
    pl.semaphore_wait(barrier, count)


class Line:
    def __init__(self, own, near, far, sem):
        self.own, self.near, self.far, self.sem = own, near, far, sem
        self.z = lax.axis_index("dp")
        self.inner = (self.z == 1) | (self.z == 2)
        self.outer = jnp.logical_not(self.inner)

    def copy(self, i, hop):
        src = (self.own, self.near, self.near)[hop].at[i]
        dst = (self.near, self.far, self.near)[hop].at[i]
        return pltpu.make_async_remote_copy(
            src_ref=src, dst_ref=dst, send_sem=self.sem.at[0, hop, i], recv_sem=self.sem.at[1, hop, i],
            device_id={"dp": 3 - self.z if hop == 1 else self.z ^ 1}, device_id_type=MESH,
        )

    def start(self, i):
        @pl.when(self.outer)
        def _():
            self.copy(i, 0).start()

    def middle(self, i, own):
        @pl.when(self.inner)
        def _():
            self.copy(i, 0).wait_recv()
            self.near[i] = (own().astype(F32) + self.near[i].astype(F32)).astype(BF)
            self.copy(i, 1).start()

    def back(self, i):
        @pl.when(self.inner)
        def _():
            self.copy(i, 1).wait()
            self.near[i] = (self.near[i].astype(F32) + self.far[i].astype(F32)).astype(BF)
            self.copy(i, 2).start()

    def close(self, i):
        @pl.when(self.outer)
        def _():
            self.copy(i, 0).wait_send()
            self.copy(i, 2).wait_recv()

        @pl.when(self.inner)
        def _():
            self.copy(i, 2).wait_send()


class Scatter:
    def __init__(self, bits, send, recv, send_sem, recv_sem, shared=0):
        self.bits, self.send, self.recv, self.send_sem, self.recv_sem = bits, send, recv, send_sem, recv_sem
        self.me = lax.axis_index("tensor")
        self.shared = shared
        self.busy = {}

    def place(self, k):
        if not self.shared:
            return k
        return k // 2 if k % 2 == 0 else (1 << len(self.bits)) // 2 + k // 2 % self.shared

    def claim(self, k):
        place = self.place(k)
        if place in self.busy:
            self.copy(self.busy.pop(place)).wait_send()
        return self.send.at[place]

    def launch(self, k):
        self.copy(k).start()
        self.busy[self.place(k)] = k

    def stage(self, k):
        return next((i for i, b in enumerate(self.bits) if k >> b & 1), len(self.bits))

    def copy(self, k):
        bit = self.bits[self.stage(k)]
        return pltpu.make_async_remote_copy(
            src_ref=self.send.at[self.place(k)],
            dst_ref=self.recv.at[k - 1],
            send_sem=self.send_sem.at[k],
            recv_sem=self.recv_sem.at[k],
            device_id={"tensor": self.me ^ (1 << bit)},
            device_id_type=MESH,
        )

    def put(self, k, value):
        self.claim(k)[...] = value.astype(BF)
        if self.stage(k) == 0:
            self.launch(k)

    def total(self, k):
        value = self.send[self.place(k)].astype(F32)
        for bit in self.bits[: self.stage(k)]:
            self.copy(k | (1 << bit)).wait_recv()
            value = value + self.recv[(k | (1 << bit)) - 1].astype(F32)
        return value

    def forward(self, k):
        self.send[self.place(k)] = self.total(k).astype(BF)
        self.launch(k)

    def drain(self):
        for k in self.busy.values():
            self.copy(k).wait_send()
        self.busy = {}


def scatter_order(bits):
    n = 1 << len(bits)
    rank = lambda k: next(i for i, b in enumerate(bits) if k >> b & 1)
    return sorted(range(2, n, 2), key=lambda k: (rank(k), -k))


def attention_grads_kernel(a_ref, gm_ref, dq_ref, h_ref, dkv_ref, up_ref, after_ref, wo_ref, wq_ref, kv_ref, sum_ref,
                           send, recv, ksend, krecv, far, own, ssem, rsem, ksem, krsem, zsem, psem,
                           *, orders, line, qw):
    bits_of = [[0] + list(o)[::-1] for o in orders]
    count = len(bits_of[0])
    n = 1 << count
    half = gm_ref.shape[1] // 2
    greet(range(count), line)
    chain = Line(up_ref, sum_ref, far, zsem)
    pieces = up_ref.shape[0]
    if line:
        for i in range(pieces):
            chain.start(i)

    def own_piece(i):
        def value():
            c = pltpu.make_async_copy(up_ref.at[i], own, psem)
            c.start()
            c.wait()
            return own[...]

        return value

    ahead = [0]

    def chain_to(middles):
        while line and ahead[0] < min(middles, pieces):
            chain.middle(ahead[0], own_piece(ahead[0]))
            ahead[0] += 1
            if ahead[0] > 1:
                chain.back(ahead[0] - 2)

    kv = Scatter(bits_of[0], ksend, krecv, ksem, krsem)
    for k in list(range(1, n, 2)) + list(range(0, n, 2)):
        kv.put(k, dkv_ref[k])

    pairs = ((a_ref, gm_ref, wo_ref), (dq_ref, h_ref, wq_ref))
    work = [
        [Scatter(bits_of[p], send.at[m, p], recv.at[m, p], ssem.at[m, p], rsem.at[m, p], shared=2) for p in range(2)]
        for m in range(2)
    ]
    sequence = [scatter_order(b) for b in bits_of]

    def products(m):
        x, y, _ = pairs[m]
        for i in range(n // 2):
            for p in range(2):
                k = (sequence[p] + [0])[i]
                for j in (k + 1, k):
                    work[m][p].put(j, dot_tn(x[:, j * qw : (j + 1) * qw], y[:, p * half : (p + 1) * half]))

    def stage(m, i):
        for at in range(n // 2 - 1):
            for p in range(2):
                k = sequence[p][at]
                if work[m][p].stage(k) == i:
                    work[m][p].forward(k)

    def kv_stage(i):
        for k in scatter_order(bits_of[0]):
            if kv.stage(k) == i:
                kv.forward(k)

    def finish(m):
        for p in range(2):
            pairs[m][2][p] = work[m][p].total(0).astype(BF)

    products(0)
    stage(0, 1)
    chain_to(1)
    products(1)
    chain_to(3)
    for i in range(1, count):
        kv_stage(i)
        if i + 1 < count:
            stage(0, i + 1)
            chain_to(2 * i + 2)
        else:
            chain_to(7)
            finish(0)
            chain_to(8)
        stage(1, i)
    chain_to(10)
    kv_ref[...] = kv.total(0).astype(BF)
    chain_to(pieces)
    finish(1)
    if line:
        chain.back(pieces - 1)
        for i in range(pieces):
            chain.close(i)
    kv.drain()
    for m in range(2):
        for p in range(2):
            work[m][p].drain()


def attention_grads(a, gm, dq, h, dkv, up, early, orders):
    n, line = lax.axis_size("tensor"), lax.axis_size("dp") == 4
    tokens, d = gm.shape
    qw = a.shape[1] // n
    slot = dkv.shape[1:]
    rows, cols = up.shape
    pieces = rows // 128
    up = up.reshape(pieces, rows // pieces, cols)
    wait = up.shape if line else (1, 16, 128)
    dma = pltpu.SemaphoreType.DMA
    vmem, hbm = pl.BlockSpec(memory_space=pltpu.VMEM), pl.BlockSpec(memory_space=pl.ANY)
    wo, wq, kv, total = pl.pallas_call(
        functools.partial(attention_grads_kernel, orders=orders, line=line, qw=qw),
        in_specs=[vmem] * 5 + [hbm] * 2,
        out_specs=[vmem] * 4,
        out_shape=[
            jax.ShapeDtypeStruct((2, qw, d // 2), BF),
            jax.ShapeDtypeStruct((2, qw, d // 2), BF),
            jax.ShapeDtypeStruct(slot, BF),
            jax.ShapeDtypeStruct(wait, BF),
        ],
        scratch_shapes=[
            pltpu.VMEM((2, 2, n // 2 + 2, qw, d // 2), BF),
            pltpu.VMEM((2, 2, n - 1, qw, d // 2), BF),
            pltpu.VMEM((n,) + slot, BF),
            pltpu.VMEM((n - 1,) + slot, BF),
            pltpu.VMEM(wait, BF),
            pltpu.VMEM(up.shape[1:], BF),
            dma((2, 2, n)), dma((2, 2, n)), dma((n,)), dma((n,)), dma((2, 3, pieces)), dma,
        ],
        compiler_params=pltpu.CompilerParams(
            collective_id=1, has_side_effects=True, vmem_limit_bytes=60 * MIB
        ),
        cost_estimate=pl.CostEstimate(flops=1000, bytes_accessed=MIB, transcendentals=0),
    )(a, gm, dq, h, dkv, up, early)
    up = up.reshape(rows, cols)
    return wo, wq, kv, total.reshape(rows, cols) if line else lax.psum(up, "dp")


def last_kernel(wo_ref, wq_ref, dq_ref, kv_ref, shared_ref, h_ref, x_ref, gain_ref, mixed_ref, qb_ref, w_ref, *refs,
                order, line, eps_rows):
    count = len(order) + 1
    n = 1 << count
    (wog_ref, wqg_ref, grad_ref, late_ref, sg_ref,
     w_s, near, far, part, send, recv, dsend, drecv, piece_s, gathered, vsend, vrecv, esend, erecv,
     zsem, ssem, rsem, dsem, gsem, vsem, esem) = refs
    me, z = lax.axis_index("tensor"), lax.axis_index("dp")
    dp_bits = range(lax.axis_size("dp").bit_length() - 1)
    tokens, d = x_ref.shape
    hd = kv_ref.shape[1] // 2
    piece = d // n
    greet(range(count), line, dp_bits)

    pieces = wo_ref.shape[0]
    owns = (wo_ref, wq_ref)
    chains = []
    if line:
        for i, ref in enumerate(owns):
            chains.append(Line(ref, near.at[i], far.at[i], zsem.at[i]))
    ahead = [0, 0]

    def chain_to(middles):
        while line and ahead[1] < min(middles + 2, len(owns) * pieces):
            i, p = divmod(ahead[1], pieces)
            chains[i].start(p)
            ahead[1] += 1
        while line and ahead[0] < min(middles, len(owns) * pieces):
            i, p = divmod(ahead[0], pieces)
            chains[i].middle(p, lambda: owns[i][p])
            ahead[0] += 1
            if ahead[0] > 1:
                i, p = divmod(ahead[0] - 2, pieces)
                chains[i].back(p)

    chain_to(0)

    part[...] = dot_tn(h_ref[...], kv_ref[...])
    scatter = Scatter([0] + list(order)[::-1], send, recv, ssem, rsem)
    for k in list(range(1, n, 2)) + list(range(0, n, 2)):
        scatter.put(k, part[pl.ds(pl.multiple_of((me ^ k) * piece, piece), piece), :])
    for k in range(n):
        w_s[:, k * w_ref.shape[2] : (k + 1) * w_ref.shape[2]] = w_ref[k]
    hops = [("tensor", me, b) for b in range(count)] + [("dp", z, b) for b in dp_bits]
    pending = []

    def swap_start(buffers, sems, value, i, axis, at, bit):
        buffers[0][i] = value
        c = pltpu.make_async_remote_copy(
            src_ref=buffers[0].at[i], dst_ref=buffers[1].at[i], send_sem=sems.at[0, i], recv_sem=sems.at[1, i],
            device_id={axis: at ^ (1 << bit)}, device_id_type=MESH,
        )
        c.start()
        pending.append(c)
        return lambda value: (c.wait_recv(), value + buffers[1][i])[1]

    size = 2 * d + hd
    tail = late_ref.at[:, size:]
    front = late_ref.at[:, :size]
    early_done, last_done, piece_done = [None], [None], [None]

    def early(i):
        if early_done[0] is not None:
            tail[...] = early_done[0](tail[...])
            early_done[0] = None
        if i < len(hops):
            early_done[0] = swap_start((esend, erecv), esem, tail[...], i, *hops[i])

    def late(i):
        if last_done[0] is not None:
            front[...] = last_done[0](front[...])
            last_done[0] = None
        if i < len(hops):
            last_done[0] = swap_start((vsend, vrecv), vsem, front[...], i, *hops[i])

    def shared_sum(i):
        if piece_done[0] is not None:
            piece_s[...] = piece_done[0](piece_s[...])
            piece_done[0] = None
        if i < len(dp_bits):
            piece_done[0] = swap_start((dsend, drecv), dsem, piece_s[...], i, "dp", z, dp_bits[i])

    tail[...] = qb_ref[...]
    early(0)
    at = 1
    chain_to(at)
    for i in range(1, count):
        for k in scatter_order(scatter.bits):
            if scatter.stage(k) == i:
                scatter.forward(k)
        early(i)
        at += 1
        chain_to(at)
    piece_s[...] = scatter.total(0)
    shared_sum(0)

    gain_part, shift_part = jnp.zeros((1, d), F32), jnp.zeros((1, d), F32)
    for t in range(tokens // eps_rows):
        rows = slice(t * eps_rows, (t + 1) * eps_rows)
        grad = dot_nt(dq_ref[rows], w_s[...]) + dot_nt(kv_ref[rows], shared_ref[...])
        unit, scale = norm_parts(x_ref[rows].astype(F32))
        e = gain_ref[...] * grad
        back = e - jnp.mean(e, axis=-1, keepdims=True) - unit * jnp.mean(e * unit, axis=-1, keepdims=True)
        grad_ref[rows] = mixed_ref[rows] + scale * back
        gain_part += jnp.sum(grad * unit, axis=0, keepdims=True)
        shift_part += jnp.sum(grad, axis=0, keepdims=True)
        if t + 1 < len(dp_bits):
            shared_sum(t + 1)
        if count + t < len(hops):
            early(count + t)
        at += 2
        chain_to(at)
    late_ref[:, :d] = gain_part
    late_ref[:, d : 2 * d] = shift_part
    late_ref[:, 2 * d : size] = jnp.sum(kv_ref[:, hd:].astype(F32), axis=0, keepdims=True)
    late(0)
    for i in range(max(tokens // eps_rows + 1, 1), len(dp_bits) + 1):
        shared_sum(i)
    shared_sum(len(dp_bits))
    for i in range(count + tokens // eps_rows, len(hops) + 1):
        early(i)
    early(len(hops))
    gathered[me] = piece_s[...].astype(BF)
    sent, held, step = [], [0], 0
    for bit in list(order) + [0]:
        new = []
        for k in held:
            c = pltpu.make_async_remote_copy(
                src_ref=gathered.at[me ^ k], dst_ref=gathered.at[me ^ k], send_sem=gsem.at[0, k | (1 << bit)],
                recv_sem=gsem.at[1, k | (1 << bit)], device_id={"tensor": me ^ (1 << bit)}, device_id_type=MESH,
            )
            c.start()
            sent.append(c)
            new.append(c)
        step += 1
        late(step)
        at += 1
        chain_to(at)
        for c in new:
            c.wait_recv()
        held = held + [k | (1 << bit) for k in held]
    while step < len(hops):
        step += 1
        late(step)
        at += 1
        chain_to(at)
    chain_to(len(owns) * pieces)
    if line:
        chains[-1].back(pieces - 1)
    for k in range(n):
        sg_ref[k * piece : (k + 1) * piece] = gathered[k].astype(F32)
    if line:
        for c in chains:
            for p in range(pieces):
                c.close(p)
    half, high = d // 2, wo_ref.shape[1]
    for j in range(pieces):
        values = [near[i, j] if line else owns[i][j] for i in range(len(owns))]
        p, q = divmod(j, pieces // 2)
        for ref, value in zip((wog_ref, wqg_ref), values):
            ref[q * high : (q + 1) * high, p * half : (p + 1) * half] = value.astype(F32)
    for c in pending + sent:
        c.wait_send()
    scatter.drain()


def last(wo, wq, dq, kv, shared, h, x, gain, mixed, qb, w, order):
    n, dp = lax.axis_size("tensor"), lax.axis_size("dp")
    line = dp == 4
    tokens, d = x.shape
    qw = wo.shape[1]
    cuts = 4
    wo, wq = (v.reshape(cuts, -1, d // 2) for v in (wo, wq))
    piece, width = d // n, kv.shape[1]
    size = 2 * d + qb.shape[1] + width // 2
    bits = n.bit_length() - 1
    dbits = dp.bit_length() - 1
    dma = pltpu.SemaphoreType.DMA
    vmem = pl.BlockSpec(memory_space=pltpu.VMEM)
    item = (2,) + wo.shape
    return pl.pallas_call(
        functools.partial(last_kernel, order=order, line=line, eps_rows=tokens // 2),
        in_specs=[vmem] * 11,
        out_specs=[vmem] * 5,
        out_shape=[
            jax.ShapeDtypeStruct((qw, d), F32),
            jax.ShapeDtypeStruct((qw, d), F32),
            jax.ShapeDtypeStruct((tokens, d), F32),
            jax.ShapeDtypeStruct((1, size), F32),
            jax.ShapeDtypeStruct((d, width), F32),
        ],
        scratch_shapes=[
            pltpu.VMEM((d, n * qw), BF),
            pltpu.VMEM(item, BF),
            pltpu.VMEM(item, BF),
            pltpu.VMEM((d, width), F32),
            pltpu.VMEM((n, piece, width), BF),
            pltpu.VMEM((n - 1, piece, width), BF),
            pltpu.VMEM((dbits, piece, width), F32),
            pltpu.VMEM((dbits, piece, width), F32),
            pltpu.VMEM((piece, width), F32),
            pltpu.VMEM((n, piece, width), BF),
            pltpu.VMEM((bits + dbits, 1, size - qb.shape[1]), F32),
            pltpu.VMEM((bits + dbits, 1, size - qb.shape[1]), F32),
            pltpu.VMEM((bits + dbits,) + qb.shape, F32),
            pltpu.VMEM((bits + dbits,) + qb.shape, F32),
            dma((2, 2, 3, cuts)), dma((n,)), dma((n,)), dma((2, dbits)), dma((2, n)), dma((2, bits + dbits)), dma((2, bits + dbits)),
        ],
        compiler_params=pltpu.CompilerParams(
            collective_id=4, has_side_effects=True, vmem_limit_bytes=60 * MIB
        ),
        cost_estimate=pl.CostEstimate(flops=1000, bytes_accessed=MIB, transcendentals=0),
    )(wo, wq, dq, kv, shared, h, x, gain, mixed, qb, w)


class Gather:
    def __init__(self, orders, refs, send_sem, recv_sem):
        self.paths = [list(o) + [0] for o in orders]
        self.refs, self.send_sem, self.recv_sem = refs, send_sem, recv_sem
        self.me = lax.axis_index("tensor")
        self.n = 1 << len(self.paths[0])
        self.sent = []

    def last_bit(self, p, k):
        return max((b for b in self.paths[p] if k >> b & 1), key=self.paths[p].index)

    def copies(self, p, k, bit):
        to = k | (1 << bit)
        return [
            pltpu.make_async_remote_copy(
                src_ref=ref(p, k), dst_ref=ref(p, to), send_sem=self.send_sem.at[i, p, to],
                recv_sem=self.recv_sem.at[i, p, to], device_id={"tensor": self.me ^ (1 << bit)}, device_id_type=MESH,
            )
            for i, ref in enumerate(self.refs)
        ]

    def hop(self, p, k, bit):
        for c in self.copies(p, k, bit):
            c.start()
            self.sent.append(c)

    def arrived(self, p, k):
        bit = self.last_bit(p, k)
        for c in self.copies(p, k ^ (1 << bit), bit):
            c.wait_recv()

    def at_step(self, p, t):
        if t == 0:
            return [0]
        return sorted((k for k in range(2, self.n, 2) if self.last_bit(p, k) == self.paths[p][t - 1]), reverse=True)

    def drain(self):
        for c in self.sent:
            c.wait_send()


def first_kernel(x_ref, gain_ref, shift_ref, shared_ref, vb_ref, wq_ref, bq_ref, h_ref, k_ref, kt_ref, v_ref, vt_ref,
                 w_ref, q_ref, kv_ref, bias, send_sem, recv_sem, *, orders, factor, rows):
    n, d, qw = w_ref.shape
    seqs, span = kv_ref.shape[1:3]
    hd = vb_ref.shape[1]
    half = d // 2
    tokens = x_ref.shape[0]
    greet(range(len(orders[0]) + 1))
    weights = Gather(
        orders, [lambda p, k: w_ref.at[k, p * half : (p + 1) * half], lambda p, k: bias.at[p, k]],
        send_sem.at[0], recv_sem.at[0],
    )
    shared = Gather(orders, [lambda p, k: kv_ref.at[k, p]], send_sem.at[1], recv_sem.at[1])
    steps = len(weights.paths[0])
    w_ref[0] = wq_ref[...]
    for p in range(2):
        bias[p, 0] = bq_ref[...]
    for p in range(2):
        weights.hop(p, 0, weights.paths[p][0])
    for p in range(2):
        weights.hop(p, 0, 0)
    for t in range(tokens // rows):
        here = slice(t * rows, (t + 1) * rows)
        unit, _ = norm_parts(x_ref[here].astype(F32))
        h_ref[here] = (unit * gain_ref[...] + shift_ref[...]).astype(BF)
    kv = dot(h_ref[...], shared_ref[...])
    for r in range(seqs):
        here = slice(r * span, (r + 1) * span)
        kv_ref[0, r, :, :hd] = kv[here, :hd].astype(BF)
        kv_ref[0, r, :, hd:] = (kv[here, hd:] + vb_ref[...]).astype(BF)
    for p in range(2):
        shared.hop(p, 0, shared.paths[p][0])
    for p in range(2):
        shared.hop(p, 0, 0)

    def product(k):
        q_ref[:, k * qw : (k + 1) * qw] = ((dot(h_ref[...], w_ref[k]) + bias[0, k]) * factor).astype(BF)

    product(0)
    ready = [1]
    for t in range(1, steps):
        for g in (weights, shared):
            for p in range(2):
                for k in g.at_step(p, t):
                    g.arrived(p, k)
                    if t < steps - 1:
                        g.hop(p, k, g.paths[p][t])
                    g.hop(p, k, 0)
            if t < steps - 1:
                for p in range(2):
                    for before in range(t - 1, -1, -1):
                        for k in g.at_step(p, before):
                            g.hop(p, k, g.paths[p][t])
    for k in range(n):
        here = slice(k * span, (k + 1) * span)
        for r in range(seqs):
            if k % 2:
                shared.arrived(r, k)
            block = kv_ref[k, r]
            k_ref[r, here, :] = block[:, :hd]
            v_ref[r, here, :] = block[:, hd:]
            kt_ref[r, :, here] = block[:, :hd].T
            vt_ref[r, :, here] = block[:, hd:].T
    for k in range(1, n, 2):
        for p in range(2):
            weights.arrived(p, k)
        product(k)
        if k > 1:
            product(k - 1)
    weights.drain()
    shared.drain()


def first(x, gain, shift, shared, vb, wq, bq, seqs, factor, orders):
    n = lax.axis_size("tensor")
    tokens, d = x.shape
    qw, hd = wq.shape[1], vb.shape[1]
    span = tokens // seqs
    plain = jax.ShapeDtypeStruct((seqs, n * span, hd), BF)
    turned = jax.ShapeDtypeStruct((seqs, hd, n * span), BF)
    dma = pltpu.SemaphoreType.DMA
    vmem = pl.BlockSpec(memory_space=pltpu.VMEM)
    return pl.pallas_call(
        functools.partial(first_kernel, orders=orders, factor=factor, rows=tokens // 4),
        in_specs=[vmem] * 7,
        out_specs=[vmem] * 7,
        out_shape=[
            jax.ShapeDtypeStruct((tokens, d), BF),
            plain, turned, plain, turned,
            jax.ShapeDtypeStruct((n, d, qw), BF),
            jax.ShapeDtypeStruct((tokens, n * qw), BF),
        ],
        scratch_shapes=[
            pltpu.VMEM((n, seqs, span, 2 * hd), BF),
            pltpu.VMEM((2, n, 1, qw), F32),
            dma((2, 2, 2, n)), dma((2, 2, 2, n)),
        ],
        compiler_params=pltpu.CompilerParams(collective_id=5, has_side_effects=True, vmem_limit_bytes=48 * MIB),
        cost_estimate=pl.CostEstimate(
            flops=2 * tokens * d * n * qw, bytes_accessed=64 * MIB, transcendentals=0
        ),
    )(x, gain, shift, shared, vb, wq, bq)


def mlp_kernel(x_ref, cot_ref, up_ref, bias_ref, down_ref, gn_ref, gb_ref, xg_ref, act_ref, gr_ref, *rest, orders):
    n, seqs, span, d = cot_ref.shape
    (ff_ref, down_grad_ref, x_s, c_s, act_s, gr_s, ff_s, send, recv, a_s, acc,
     gsend, grecv, ssem, rsem, load, own, out, aload, gout) = rest
    hidden = up_ref.shape[1]
    tile, wide = min(512, hidden), 512
    me = lax.axis_index("tensor")
    paths = [list(o) + [0] for o in orders]
    bits_of = [[0] + list(o)[::-1] for o in orders]
    work = [Scatter(bits_of[p], send.at[p], recv.at[p], ssem.at[p], rsem.at[p], shared=2) for p in range(seqs)]

    def last_bit(p, k):
        return max((b for b in paths[p] if k >> b & 1), key=paths[p].index)

    def hop(p, k, bit):
        to = k | (1 << bit)
        src = x_ref.at[p] if k == 0 else xg_ref.at[me ^ k, p]
        return pltpu.make_async_remote_copy(
            src_ref=src, dst_ref=xg_ref.at[me ^ k, p], send_sem=gsend.at[p, to], recv_sem=grecv.at[p, to],
            device_id={"tensor": me ^ (1 << bit)}, device_id_type=MESH,
        )

    def arrival(p, k):
        bit = last_bit(p, k)
        return pltpu.make_async_remote_copy(
            src_ref=x_ref.at[p], dst_ref=xg_ref.at[me ^ k, p], send_sem=gsend.at[p, k], recv_sem=grecv.at[p, k],
            device_id={"tensor": me ^ (1 << bit)}, device_id_type=MESH,
        )

    def slots_at(p, t):
        if t == 0:
            return [0]
        return sorted((k for k in range(2, n, 2) if last_bit(p, k) == paths[p][t - 1]), reverse=True)

    steps = len(paths[0])
    units = [(p, k) for t in range(steps) for i in range(len(slots_at(0, t))) for p in range(seqs) for k in [slots_at(p, t)[i]]]

    def cot_loads(u):
        p, e = units[u]
        return [
            pltpu.make_async_copy(
                cot_ref.at[me ^ (e + j), p], c_s.at[u % 2, j * span : (j + 1) * span], load.at[u % 2, j]
            )
            for j in range(2)
        ]

    def x_loads(u):
        p, e = units[u]
        return [
            pltpu.make_async_copy(
                x_ref.at[p] if e + j == 0 else xg_ref.at[me ^ (e + j), p],
                x_s.at[j * span : (j + 1) * span], load.at[2, j],
            )
            for j in range(2)
        ]

    def hidden_stores(u):
        p, e = units[u]
        return [
            pltpu.make_async_copy(
                buf.at[j * span : (j + 1) * span], ref.at[me ^ (e + j), p], out.at[i, j]
            )
            for i, (buf, ref) in enumerate(((act_s, act_ref), (gr_s, gr_ref)))
            for j in range(2)
        ]

    def ff_stores(u):
        p, e = units[u]
        return [
            pltpu.make_async_copy(ff_s.at[j * span : (j + 1) * span], ff_ref.at[p, e + j], out.at[2, j])
            for j in range(2)
        ]

    waiting = []

    def run(u):
        p, e = units[u]
        for j in range(2):
            if e + j and (e + j) % 2 == 1:
                arrival(p, e + j).wait_recv()
        for c in x_loads(u):
            c.start()
        if u + 1 < len(units):
            for c in cot_loads(u + 1):
                c.start()
        if u:
            for c in hidden_stores(u - 1):
                c.wait()
        for c in x_loads(u) + cot_loads(u):
            c.wait()

        @pl.loop(0, hidden // tile)
        def _(i):
            here = pl.ds(pl.multiple_of(i * tile, tile), tile)
            raised = dot(x_s[...], up_ref[:, here]) + bias_ref[:, here]
            square = raised * raised
            th = jnp.tanh(0.7978845608028654 * raised * (1.0 + 0.044715 * square))
            act_s[:, here] = (0.5 * raised * (1.0 + th)).astype(BF)
            slope = 0.5 * (1.0 + th) + 0.5 * raised * (1.0 - th * th) * (
                0.7978845608028654 * (1.0 + 3 * 0.044715 * square)
            )
            gr = (dot_nt(c_s[u % 2], down_ref[here, :]) * slope).astype(BF)
            gr_s[:, here] = gr
            gb = jnp.sum(gr.astype(F32), axis=0, keepdims=True)
            gb_ref[:, here] = gb if u == 0 else gb_ref[:, here] + gb

        for c in hidden_stores(u):
            c.start()
        while waiting:
            q, k = waiting.pop(0)
            work[q].forward(k)
        if u:
            for c in ff_stores(u - 1):
                c.wait()
        odd, even = work[p].claim(e + 1), work[p].claim(e)

        @pl.loop(0, d // wide)
        def _(i):
            here = pl.ds(pl.multiple_of(i * wide, wide), wide)
            gn = dot_nt(gr_s[...], up_ref[here, :]).astype(BF)
            even[:, here] = gn[:span]
            odd[:, here] = gn[span:]
            ff_s[:, here] = dot(act_s[...], down_ref[:, here]).astype(BF)

        work[p].launch(e + 1)
        for c in ff_stores(u):
            c.start()

    keep = [pltpu.make_async_copy(x_ref.at[p], xg_ref.at[me, p], own.at[p]) for p in range(seqs)]
    greet(range(steps))
    for p in range(seqs):
        hop(p, 0, paths[p][0]).start()
    for p in range(seqs):
        hop(p, 0, 0).start()
        keep[p].start()
    for c in cot_loads(0):
        c.start()
    sent = [(p, 0, b) for p in range(seqs) for b in (paths[p][0], 0)]
    u = 0
    for t in range(steps):
        while u < len(units) and units[u][1] in slots_at(units[u][0], t):
            if t and units[u][0] == 0:
                for p in range(seqs):
                    k = units[u + p][1]
                    arrival(p, k).wait_recv()
                    if t < steps - 1:
                        hop(p, k, paths[p][t]).start()
                        sent.append((p, k, paths[p][t]))
                    hop(p, k, 0).start()
                    sent.append((p, k, 0))
            run(u)
            p, k = units[u]
            if work[p].stage(k) == 1:
                waiting.append((p, k))
            u += 1
        if 0 < t < steps - 1:
            for p in range(seqs):
                for before in range(t - 1, -1, -1):
                    for k in slots_at(p, before):
                        hop(p, k, paths[p][t]).start()
                        sent.append((p, k, paths[p][t]))
    for p, k in waiting:
        work[p].forward(k)
    for c in hidden_stores(len(units) - 1) + ff_stores(len(units) - 1):
        c.wait()

    strip = a_s.shape[2]
    strips = hidden // strip

    def grad_loads(q, j, slot):
        return [
            c
            for r in range(seqs)
            for c in (
                pltpu.make_async_copy(
                    act_ref.at[j, r, :, q * strip : (q + 1) * strip], a_s.at[slot, r * span : (r + 1) * span],
                    aload.at[slot, r],
                ),
                pltpu.make_async_copy(
                    cot_ref.at[j, r], c_s.at[slot, r * span : (r + 1) * span], load.at[slot, r]
                ),
            )
        ]

    def grad_store(q):
        return pltpu.make_async_copy(
            ff_s.at[:strip], down_grad_ref.at[q * strip : (q + 1) * strip], gout
        )

    def grad_strip(q):
        for c in grad_loads(q, 0, 0):
            c.start()

        @pl.loop(0, n)
        def _(j):
            slot = lax.rem(j, 2)

            @pl.when(j + 1 < n)
            def _():
                for c in grad_loads(q, j + 1, 1 - slot):
                    c.start()

            for c in grad_loads(q, j, slot):
                c.wait()
            term = dot_tn(a_s[slot], c_s[slot])

            @pl.when(j == 0)
            def _():
                acc[...] = term

            @pl.when(j > 0)
            def _():
                acc[...] += term

        if q:
            grad_store(q - 1).wait()
        ff_s[:strip] = acc[...].astype(BF)
        grad_store(q).start()

    for q in range(strips // 2):
        grad_strip(q)
    for i in range(2, steps):
        for at in range(n // 2 - 1):
            for p in range(seqs):
                k = scatter_order(bits_of[p])[at]
                if work[p].stage(k) == i:
                    work[p].forward(k)
    for q in range(strips // 2, strips):
        grad_strip(q)
    grad_store(strips - 1).wait()
    for p in range(seqs):
        gn_ref[p] = work[p].total(0)
    for c in keep:
        c.wait()
    for p, k, b in sent:
        hop(p, k, b).wait_send()
    for p in range(seqs):
        work[p].drain()


def mlp(normed, cot, up, bias, down, orders):
    n, seqs, span, d = cot.shape
    ff = up.shape[1]
    strip = min(2 * span, ff // 2, 256)
    dma = pltpu.SemaphoreType.DMA
    hbm, vmem = pl.BlockSpec(memory_space=pl.ANY), pl.BlockSpec(memory_space=pltpu.VMEM)
    return pl.pallas_call(
        functools.partial(mlp_kernel, orders=orders),
        in_specs=[hbm, hbm, vmem, vmem, vmem],
        out_specs=[vmem, vmem, hbm, hbm, hbm, hbm, hbm],
        out_shape=[
            jax.ShapeDtypeStruct((seqs, span, d), F32),
            jax.ShapeDtypeStruct((1, ff), F32),
            jax.ShapeDtypeStruct((n, seqs, span, d), BF),
            jax.ShapeDtypeStruct((n, seqs, span, ff), BF),
            jax.ShapeDtypeStruct((n, seqs, span, ff), BF),
            jax.ShapeDtypeStruct((seqs, n, span, d), BF),
            jax.ShapeDtypeStruct((ff, d), BF),
        ],
        scratch_shapes=[
            pltpu.VMEM((2 * span, d), BF),
            pltpu.VMEM((2, 2 * span, d), BF),
            pltpu.VMEM((2 * span, ff), BF),
            pltpu.VMEM((2 * span, ff), BF),
            pltpu.VMEM((2 * span, d), BF),
            pltpu.VMEM((seqs, n // 2 + 2, span, d), BF),
            pltpu.VMEM((seqs, n - 1, span, d), BF),
            pltpu.VMEM((2, seqs * span, strip), BF),
            pltpu.VMEM((strip, d), F32),
            dma((seqs, n)), dma((seqs, n)), dma((seqs, n)), dma((seqs, n)), dma((3, 2)), dma((seqs,)), dma((3, 2)),
            dma((2, seqs)), dma,
        ],
        compiler_params=pltpu.CompilerParams(collective_id=2, has_side_effects=True, vmem_limit_bytes=60 * MIB),
        cost_estimate=pl.CostEstimate(
            flops=8 * n * seqs * span * d * ff, bytes_accessed=100 * MIB, transcendentals=n * seqs * span * ff
        ),
    )(normed, cot, up, bias, down)


class ScatterParts(Scatter):
    def copy(self, k):
        if self.stage(k):
            return super().copy(k)
        return pltpu.make_async_remote_copy(
            src_ref=self.source.at[k],
            dst_ref=self.recv.at[k - 1],
            send_sem=self.send_sem.at[k],
            recv_sem=self.recv_sem.at[k],
            device_id={"tensor": self.me ^ (1 << self.bits[0])},
            device_id_type=MESH,
        )

    def place(self, k):
        return k // 2 if k % 2 == 0 else -k


def mlp_grads_kernel(gr_ref, x_ref, part_ref, mixed_ref, bias_ref, after_ref, up_ref, ff_ref,
                     a_s, b_s, acc, send, recv, ssem, rsem, load, own, *, orders):
    seqs, n = part_ref.shape[:2]
    bits_of = [[0] + list(o)[::-1] for o in orders]
    work = []
    for p in range(seqs):
        w = ScatterParts(bits_of[p], send.at[p], recv.at[p], ssem.at[p], rsem.at[p])
        w.source = part_ref.at[p]
        work.append(w)
    evens = [
        pltpu.make_async_copy(part_ref.at[p, k], send.at[p, k // 2], own.at[p, k // 2])
        for p in range(seqs) for k in range(0, n, 2)
    ]
    wide = acc.shape[0]
    tile = min(256, wide)
    steps = n

    def loads(u):
        return [
            pltpu.make_async_copy(x_ref.at[u], a_s.at[u % 2], load.at[u % 2, 0]),
            pltpu.make_async_copy(gr_ref.at[u], b_s.at[u % 2], load.at[u % 2, 1]),
        ]

    greet(range(len(bits_of[0])))
    for k in range(n - 1, 0, -2):
        for p in range(seqs):
            work[p].launch(k)
    for c in loads(0) + evens:
        c.start()

    def forwards(i):
        for at in range(n // 2 - 1):
            for p in range(seqs):
                k = scatter_order(bits_of[p])[at]
                if work[p].stage(k) == i:
                    work[p].forward(k)

    stages = len(bits_of[0])
    when = {(i - 1) * (steps // (stages - 1)) + 1: i for i in range(1, stages)} if stages > 1 else {}
    when = {min(u + 2 * (i - 1), steps - 1): i for u, i in when.items()}
    for u in range(steps):
        if u + 1 < steps:
            for c in loads(u + 1):
                c.start()
        for c in loads(u):
            c.wait()

        @pl.loop(0, wide // tile)
        def _(i, u=u):
            here = pl.ds(pl.multiple_of(i * tile, tile), tile)
            term = dot_tn(a_s[u % 2, :, here], b_s[u % 2])
            if u == 0:
                acc[here, :] = term
            elif u < n - 1:
                acc[here, :] += term
            else:
                up_ref[here, :] = (acc[here, :] + term).astype(BF)

        if u == 0:
            for c in evens:
                c.wait()
        if u in when:
            forwards(when[u])
    for p in range(seqs):
        ff_ref[p] = (mixed_ref[p] + work[p].total(0) + bias_ref[...]).astype(BF)
        work[p].drain()


def mlp_grads(gr, x, parts, mixed, bias, early, orders):
    seqs, n, span, d = parts.shape
    tokens, cols = seqs * span, gr.shape[-1]
    dma = pltpu.SemaphoreType.DMA
    hbm, vmem = pl.BlockSpec(memory_space=pl.ANY), pl.BlockSpec(memory_space=pltpu.VMEM)
    flat = lambda v: v.reshape(n, tokens, v.shape[-1])
    return pl.pallas_call(
        functools.partial(mlp_grads_kernel, orders=orders),
        in_specs=[hbm] * 3 + [vmem] * 2 + [hbm],
        out_specs=[vmem] * 2,
        out_shape=[
            jax.ShapeDtypeStruct((d, cols), BF),
            jax.ShapeDtypeStruct((seqs, span, d), BF),
        ],
        scratch_shapes=[
            pltpu.VMEM((2, tokens, d), BF),
            pltpu.VMEM((2, tokens, cols), BF),
            pltpu.VMEM((d, cols), F32),
            pltpu.VMEM((seqs, n // 2, span, d), BF),
            pltpu.VMEM((seqs, n - 1, span, d), BF),
            dma((seqs, n)), dma((seqs, n)), dma((2, 2)), dma((seqs, n // 2)),
        ],
        compiler_params=pltpu.CompilerParams(collective_id=3, has_side_effects=True, vmem_limit_bytes=60 * MIB),
        cost_estimate=pl.CostEstimate(flops=1000, bytes_accessed=MIB, transcendentals=0),
    )(flat(gr), flat(x), parts, mixed, bias, early)


def norm_parts(values):
    center = values - jnp.mean(values, axis=-1, keepdims=True)
    scale = lax.rsqrt(jnp.mean(center * center, axis=-1, keepdims=True) + EPSILON)
    return center * scale, scale


def norm_back(unit, scale, gain, grad):
    e = gain * grad
    back = scale * (e - jnp.mean(e, axis=-1, keepdims=True) - unit * jnp.mean(e * unit, axis=-1, keepdims=True))
    return back, jnp.sum(grad * unit, axis=(0, 1)), jnp.sum(grad, axis=(0, 1))


def body(
    inputs, cotangent, documents, padding, attn_gain, attn_shift, query_matrix, query_bias, shared_matrix,
    value_bias, output_matrix, output_bias, mlp_gain, mlp_shift, expansion_weights, up_bias, down_matrix, down_bias,
):
    n = lax.axis_size("tensor")
    me = lax.axis_index("tensor")
    hd = value_bias.shape[0]
    seqs, span, d = inputs.shape
    length = documents.shape[1]
    qw = query_matrix.shape[1]
    heads = qw // hd
    scale = hd**-0.5
    paths = bit_orders(n)
    tokens = seqs * span
    ff = up_bias.shape[0]

    x32 = inputs.astype(F32)
    output_every = lax.all_gather(output_matrix, "tensor")
    cot_every = lax.all_gather(cotangent, "tensor")
    h2, keys, keys_t, values, values_t, wq, query = first(
        inputs.reshape(tokens, d), attn_gain[None], attn_shift[None], shared_matrix, value_bias[None], query_matrix,
        query_bias[None], seqs, scale * LOG2E, paths,
    )
    query = query.reshape(seqs, span, n * qw)
    like = lambda t, cols: jax.ShapeDtypeStruct((tokens, cols), t)

    begin = lax.dynamic_slice_in_dim(documents, me * span, 1, 1)
    low = (jnp.sum((documents < begin).astype(jnp.int32), axis=1) // span).astype(jnp.int32)
    low = jnp.minimum(low, me)
    at = me.reshape(1).astype(jnp.int32)
    dock = jnp.where(padding == 1, documents, -1)
    dock = xor_order(dock.reshape(seqs, n, span).swapaxes(0, 1), me).swapaxes(0, 1).reshape(seqs, length, 1)
    docq = lax.dynamic_slice_in_dim(documents, me * span, span, 1)
    docq = jnp.concatenate([docq] * heads, axis=1)[:, None, :]
    attended, lse = attention_fwd(query, keys, values_t, low, at, dock, docq, heads, hd)
    a2 = attended.reshape(tokens, n * qw)
    mixed, normed = slot_product(
        o_kernel, [a2, inputs.reshape(tokens, d)], output_every, [output_bias[None], mlp_gain[None], mlp_shift[None]],
        [like(F32, d), like(BF, d)],
    )
    mixed, normed = mixed.reshape(seqs, span, d), normed.reshape(seqs, span, d)
    unit2, scale2 = norm_parts(mixed)

    grad_normed, up_bias_part, normed_every, acts, grs, ff_parts, down_part = mlp(
        normed, cot_every, expansion_weights, up_bias[None], down_matrix, paths
    )
    down_gradient = lax.psum(down_part, "dp")

    cot_wide = cotangent.astype(F32)
    back2, mlp_gain_part, mlp_shift_part = norm_back(unit2, scale2, mlp_gain, grad_normed)
    grad_mixed = cot_wide + back2
    gm2 = grad_mixed.astype(BF).reshape(tokens, d)
    (grad_attended,) = slot_product(do_kernel, [gm2], output_every, [], [like(BF, n * qw)])
    grad_attended = grad_attended.reshape(seqs, span, n * qw)
    dq, dk, dv = attention_bwd(
        query, grad_attended, attended, lse, keys, keys_t, values, low, at, dock, docq, heads, hd, scale
    )
    dq2 = dq.reshape(tokens, n * qw)
    up_part, block_out = mlp_grads(grs, normed_every, ff_parts, mixed, down_bias[None], dq2, paths)

    dkv = jnp.concatenate([dk * LN2, dv], axis=-1).astype(BF).reshape(seqs, n, span, 2 * hd).swapaxes(0, 1)
    wo_own, wq_own, dkv_own, up_gradient = attention_grads(
        a2, gm2, dq2, h2, dkv.reshape(n, tokens, 2 * hd), up_part, down_gradient, paths
    )
    query_bias_part = xor_order(jnp.sum(dq2.astype(F32), axis=0).reshape(n, qw), me).reshape(-1)
    up_bias_every = lax.dynamic_update_slice_in_dim(jnp.zeros((n * ff,), F32), up_bias_part[0], me * ff, 0)
    vector = jnp.concatenate(
        [query_bias_part, mlp_gain_part, mlp_shift_part, jnp.sum(grad_mixed, axis=(0, 1)),
         jnp.sum(cot_wide, axis=(0, 1)), up_bias_every]
    )[None]
    output_gradient, query_gradient, input_grad, late, shared_grad = last(
        wo_own, wq_own, dq2, dkv_own, shared_matrix, h2, inputs.reshape(tokens, d), attn_gain[None],
        grad_mixed.reshape(tokens, d), vector, wq, paths[0],
    )
    input_grad = input_grad.reshape(seqs, span, d)
    if lax.axis_size("dp") != 4:
        output_gradient, query_gradient = (
            g.astype(F32) for g in lax.psum((output_gradient.astype(BF), query_gradient.astype(BF)), "dp")
        )
    late = late[0]
    ends = [d, 2 * d, 2 * d + hd, 2 * d + hd + n * qw]
    ends += [ends[-1] + d * (i + 1) for i in range(4)]
    (attn_gain_grad, attn_shift_grad, value_bias_grad, query_bias_all, mlp_gain_grad, mlp_shift_grad,
     output_bias_grad, down_bias_grad, up_bias_all) = jnp.split(late, ends)
    query_bias_grad = lax.dynamic_slice_in_dim(query_bias_all, me * qw, qw, 0)
    up_bias_grad = lax.dynamic_slice_in_dim(up_bias_all, me * ff, ff, 0)
    query_gradient, up_gradient, down_gradient = query_gradient.T, up_gradient.astype(F32), down_gradient.astype(F32)
    return (
        block_out, input_grad, attn_gain_grad, attn_shift_grad, query_gradient, query_bias_grad, shared_grad,
        value_bias_grad, output_gradient, output_bias_grad, mlp_gain_grad, mlp_shift_grad, up_gradient, up_bias_grad,
        down_gradient, down_bias_grad,
    )


def solution(mesh):
    act = P("dp", "tensor", None)
    cols, rows, vec, rep = P(None, "tensor"), P("tensor", None), P("tensor"), P()
    ids = P("dp", None)
    return jax.shard_map(
        body,
        mesh=mesh,
        in_specs=(act, act, ids, ids, rep, rep, cols, vec, rep, rep, rows, rep, rep, rep, cols, vec, rows, rep),
        out_specs=(act, act, rep, rep, cols, vec, rep, rep, rows, rep, rep, rep, cols, vec, rows, rep),
        check_vma=False,
    )
```

```python
import functools

import jax
import jax.numpy as jnp
from jax import lax
from jax.experimental import pallas as pl
from jax.experimental.pallas import tpu as pltpu
from jax.sharding import PartitionSpec as P

EPSILON = 1e-05
LOG2E = 1.4426950408889634
LN2 = 0.6931471805599453
BF = jnp.bfloat16
F32 = jnp.float32
NEG = -1e30
MIB = 1024 * 1024


def dot(a, b):
    return lax.dot_general(a, b, (((1,), (0,)), ((), ())), preferred_element_type=F32)


def dot_nt(a, b):
    return lax.dot_general(a, b, (((1,), (1,)), ((), ())), preferred_element_type=F32)


def dot_tn(a, b):
    return lax.dot_general(a, b, (((0,), (0,)), ((), ())), preferred_element_type=F32)


def bit_orders(n):
    bits = list(range(1, n.bit_length() - 1))
    return bits, bits[::-1]


def xor_order(x, me):
    n = x.shape[0]
    rest = x.shape[1:]
    for bit in range(n.bit_length() - 1):
        pairs = x.reshape((n >> (bit + 1), 2, 1 << bit) + rest)
        x = jnp.where((me >> bit) & 1 == 1, jnp.flip(pairs, 1), pairs).reshape((n,) + rest)
    return x


def stack_heads(block, heads, hd):
    return jnp.concatenate([block[:, i * hd : (i + 1) * hd] for i in range(heads)], axis=0)


def diagonal_mask(rows, cols, same):
    key_at = lax.broadcasted_iota(jnp.int32, (rows, cols), 0)
    query_at = lax.broadcasted_iota(jnp.int32, (rows, cols), 1) % rows
    return (same & (key_at < query_at)) | (key_at == query_at)


def below_blocks(low, at, step, carry):
    even = at - at % 2
    carry = lax.fori_loop(jnp.maximum(low, even), at, lambda b, c: step(b ^ at, 1, c), carry)
    return lax.fori_loop(low // 2, at // 2, lambda p, c: step((p ^ (at // 2)) * 2, 2, c), carry)


def attention_fwd_kernel(low_ref, at_ref, q_ref, k_ref, vt_ref, dock_ref, docq_ref, o_ref, lse_ref, *, heads, hd):
    row = pl.program_id(0)
    span = q_ref.shape[1]
    at = at_ref[0]
    q2 = stack_heads(q_ref[0], heads, hd)
    docq = docq_ref[0]

    def scores(slot, count):
        here = pl.ds(pl.multiple_of(slot * span, count * span), count * span)
        s = dot_nt(k_ref[0, here, :], q2)
        same = dock_ref[0, here, :] == docq
        return s, same, here

    s, same, here = scores(0, 1)
    s = jnp.where(diagonal_mask(span, heads * span, same), s, NEG)
    top = jnp.max(s, axis=0, keepdims=True)
    p = jnp.exp2(s - top)
    total = jnp.sum(p, axis=0, keepdims=True)
    acc = dot(vt_ref[0, :, here], p.astype(BF))

    def step(slot, count, carry):
        top, total, acc = carry
        s, same, here = scores(slot, count)
        s = jnp.where(same, s, NEG)
        new = jnp.maximum(top, jnp.max(s, axis=0, keepdims=True))
        shrink = jnp.exp2(top - new)
        p = jnp.exp2(s - new)
        total = total * shrink + jnp.sum(p, axis=0, keepdims=True)
        acc = acc * shrink + dot(vt_ref[0, :, here], p.astype(BF))
        return new, total, acc

    carry = below_blocks(low_ref[row], at, step, (top, total, acc))
    top, total, acc = carry
    out = (acc / total).T.astype(BF)
    for i in range(heads):
        o_ref[0, :, i * hd : (i + 1) * hd] = out[i * span : (i + 1) * span]
    lse_ref[0, 0] = top + jnp.log2(total)


def attention_bwd_kernel(
    low_ref, at_ref, q_ref, do_ref, o_ref, lse_ref, k_ref, kt_ref, v_ref, dock_ref, docq_ref,
    dq_ref, dk_ref, dv_ref, *, heads, hd, scale,
):
    row = pl.program_id(0)
    span = q_ref.shape[1]
    at = at_ref[0]

    @pl.when(pl.program_id(1) == 0)
    def _():
        dk_ref[...] = jnp.zeros_like(dk_ref)
        dv_ref[...] = jnp.zeros_like(dv_ref)

    q2 = stack_heads(q_ref[0], heads, hd)
    do2 = stack_heads(do_ref[0], heads, hd)
    o2 = stack_heads(o_ref[0], heads, hd)
    delta = jnp.sum((do2.astype(F32) * o2.astype(F32)).T, axis=0, keepdims=True)
    lse = lse_ref[0, 0]
    docq = docq_ref[0]

    def one(slot, count, dqt, diagonal=False):
        here = pl.ds(pl.multiple_of(slot * span, count * span), count * span)
        s = dot_nt(k_ref[0, here, :], q2)
        same = dock_ref[0, here, :] == docq
        if diagonal:
            same = diagonal_mask(span, heads * span, same)
        p = jnp.where(same, jnp.exp2(s - lse), 0.0)
        dp = dot_nt(v_ref[0, here, :], do2)
        ds = (p * (dp - delta)).astype(BF)
        dk_ref[0, here, :] += dot(ds, q2)
        dv_ref[0, here, :] += dot(p.astype(BF), do2)
        return dqt + dot(kt_ref[0, :, here], ds)

    dqt = one(0, 1, jnp.zeros((hd, heads * span), F32), True)
    dqt = below_blocks(low_ref[row], at, one, dqt)
    dq = (dqt * scale).T.astype(BF)
    for i in range(heads):
        dq_ref[0, :, i * hd : (i + 1) * hd] = dq[i * span : (i + 1) * span]


def attention_fwd(q, k, vt, low, at, dock, docq, heads, hd):
    rows, span, width = q.shape
    length = k.shape[1]
    groups = width // (heads * hd)
    gw = heads * hd
    return pl.pallas_call(
        functools.partial(attention_fwd_kernel, heads=heads, hd=hd),
        grid_spec=pltpu.PrefetchScalarGridSpec(
            num_scalar_prefetch=2,
            grid=(rows, groups),
            in_specs=[
                pl.BlockSpec((1, span, gw), lambda r, g, *_: (r, 0, g)),
                pl.BlockSpec((1, length, hd), lambda r, g, *_: (r, 0, 0)),
                pl.BlockSpec((1, hd, length), lambda r, g, *_: (r, 0, 0)),
                pl.BlockSpec((1, length, 1), lambda r, g, *_: (r, 0, 0)),
                pl.BlockSpec((1, 1, heads * span), lambda r, g, *_: (r, 0, 0)),
            ],
            out_specs=[
                pl.BlockSpec((1, span, gw), lambda r, g, *_: (r, 0, g)),
                pl.BlockSpec((1, 1, 1, heads * span), lambda r, g, *_: (r, g, 0, 0)),
            ],
        ),
        out_shape=[
            jax.ShapeDtypeStruct((rows, span, width), BF),
            jax.ShapeDtypeStruct((rows, groups, 1, heads * span), F32),
        ],
        compiler_params=pltpu.CompilerParams(vmem_limit_bytes=24 * MIB),
        cost_estimate=pl.CostEstimate(
            flops=2 * rows * span * width * length, bytes_accessed=8 * MIB, transcendentals=rows * span * length
        ),
    )(low, at, q, k, vt, dock, docq)


def attention_bwd(q, do, o, lse, k, kt, v, low, at, dock, docq, heads, hd, scale):
    rows, span, width = q.shape
    length = k.shape[1]
    groups = width // (heads * hd)
    gw = heads * hd
    blk = pl.BlockSpec((1, span, gw), lambda r, g, *_: (r, 0, g))
    full = pl.BlockSpec((1, length, hd), lambda r, g, *_: (r, 0, 0))
    return pl.pallas_call(
        functools.partial(attention_bwd_kernel, heads=heads, hd=hd, scale=scale),
        grid_spec=pltpu.PrefetchScalarGridSpec(
            num_scalar_prefetch=2,
            grid=(rows, groups),
            in_specs=[
                blk,
                blk,
                blk,
                pl.BlockSpec((1, 1, 1, heads * span), lambda r, g, *_: (r, g, 0, 0)),
                full,
                pl.BlockSpec((1, hd, length), lambda r, g, *_: (r, 0, 0)),
                full,
                pl.BlockSpec((1, length, 1), lambda r, g, *_: (r, 0, 0)),
                pl.BlockSpec((1, 1, heads * span), lambda r, g, *_: (r, 0, 0)),
            ],
            out_specs=[blk, full, full],
        ),
        out_shape=[
            jax.ShapeDtypeStruct((rows, span, width), BF),
            jax.ShapeDtypeStruct((rows, length, hd), F32),
            jax.ShapeDtypeStruct((rows, length, hd), F32),
        ],
        compiler_params=pltpu.CompilerParams(vmem_limit_bytes=32 * MIB),
        cost_estimate=pl.CostEstimate(
            flops=1000, bytes_accessed=MIB, transcendentals=0
        ),
    )(low, at, q, do, o, lse, k, kt, v, dock, docq)


def fill_rows(whole_ref, every_ref):
    n, rows, _ = every_ref.shape
    me = lax.axis_index("tensor")
    for k in range(n):
        whole_ref[k * rows : (k + 1) * rows, :] = every_ref[me ^ k]


def o_kernel(a_ref, x_ref, w_ref, b_ref, gain_ref, shift_ref, mixed_ref, normed_ref, w_s):
    @pl.when(pl.program_id(0) == 0)
    def _():
        fill_rows(w_s, w_ref)

    mixed = x_ref[...].astype(F32) + dot(a_ref[...], w_s[...]) + b_ref[...]
    mixed_ref[...] = mixed
    unit, _ = norm_parts(mixed)
    normed_ref[...] = (unit * gain_ref[...] + shift_ref[...]).astype(BF)


def do_kernel(g_ref, w_ref, o_ref, w_s):
    @pl.when(pl.program_id(0) == 0)
    def _():
        fill_rows(w_s, w_ref)

    o_ref[...] = dot_nt(g_ref[...], w_s[...]).astype(BF)


def slot_product(kernel, tiled, weights, fixed, outs):
    n, rows, cols = weights.shape
    tokens = tiled[0].shape[0]
    tile = tokens // 2
    still = lambda a: pl.BlockSpec(a.shape, lambda i: (0,) * a.ndim, pipeline_mode=pl.Buffered(1))
    flow = lambda a: pl.BlockSpec((tile, a.shape[1]), lambda i: (i, 0))
    return pl.pallas_call(
        kernel,
        grid=(2,),
        in_specs=[flow(a) for a in tiled] + [still(weights)] + [still(a) for a in fixed],
        out_specs=[flow(o) for o in outs],
        out_shape=outs,
        scratch_shapes=[pltpu.VMEM((n * rows, cols), BF)],
        compiler_params=pltpu.CompilerParams(vmem_limit_bytes=48 * MIB),
        cost_estimate=pl.CostEstimate(
            flops=2 * tokens * n * rows * cols, bytes_accessed=2 * n * rows * cols + 8 * MIB, transcendentals=0
        ),
    )(*tiled, weights, *fixed)


MESH = pl.DeviceIdType.MESH


def greet(bits, line=False, dp_bits=()):
    me, z = lax.axis_index("tensor"), lax.axis_index("dp")
    barrier = pltpu.get_barrier_semaphore()
    for bit in bits:
        pl.semaphore_signal(barrier, inc=1, device_id={"tensor": me ^ (1 << bit)}, device_id_type=MESH)
    count = len(bits)
    flips = {1 << bit for bit in dp_bits} | ({1} if line else set())
    for flip in sorted(flips):
        pl.semaphore_signal(barrier, inc=1, device_id={"dp": z ^ flip}, device_id_type=MESH)
    count += len(flips)
    if line:
        inner = (z == 1) | (z == 2)

        @pl.when(inner)
        def _():
            pl.semaphore_signal(barrier, inc=1, device_id={"dp": 3 - z}, device_id_type=MESH)

        count = count + inner.astype(jnp.int32)
    pl.semaphore_wait(barrier, count)


class Line:
    def __init__(self, own, near, far, sem):
        self.own, self.near, self.far, self.sem = own, near, far, sem
        self.z = lax.axis_index("dp")
        self.inner = (self.z == 1) | (self.z == 2)
        self.outer = jnp.logical_not(self.inner)

    def copy(self, i, hop):
        src = (self.own, self.near, self.near)[hop].at[i]
        dst = (self.near, self.far, self.near)[hop].at[i]
        return pltpu.make_async_remote_copy(
            src_ref=src, dst_ref=dst, send_sem=self.sem.at[0, hop, i], recv_sem=self.sem.at[1, hop, i],
            device_id={"dp": 3 - self.z if hop == 1 else self.z ^ 1}, device_id_type=MESH,
        )

    def start(self, i):
        @pl.when(self.outer)
        def _():
            self.copy(i, 0).start()

    def middle(self, i, own):
        @pl.when(self.inner)
        def _():
            self.copy(i, 0).wait_recv()
            self.near[i] = (own().astype(F32) + self.near[i].astype(F32)).astype(BF)
            self.copy(i, 1).start()

    def back(self, i):
        @pl.when(self.inner)
        def _():
            self.copy(i, 1).wait()
            self.near[i] = (self.near[i].astype(F32) + self.far[i].astype(F32)).astype(BF)
            self.copy(i, 2).start()

    def close(self, i):
        @pl.when(self.outer)
        def _():
            self.copy(i, 0).wait_send()
            self.copy(i, 2).wait_recv()

        @pl.when(self.inner)
        def _():
            self.copy(i, 2).wait_send()


class Scatter:
    def __init__(self, bits, send, recv, send_sem, recv_sem, shared=0):
        self.bits, self.send, self.recv, self.send_sem, self.recv_sem = bits, send, recv, send_sem, recv_sem
        self.me = lax.axis_index("tensor")
        self.shared = shared
        self.busy = {}

    def place(self, k):
        if not self.shared:
            return k
        return k // 2 if k % 2 == 0 else (1 << len(self.bits)) // 2 + k // 2 % self.shared

    def claim(self, k):
        place = self.place(k)
        if place in self.busy:
            self.copy(self.busy.pop(place)).wait_send()
        return self.send.at[place]

    def launch(self, k):
        self.copy(k).start()
        self.busy[self.place(k)] = k

    def stage(self, k):
        return next((i for i, b in enumerate(self.bits) if k >> b & 1), len(self.bits))

    def copy(self, k):
        bit = self.bits[self.stage(k)]
        return pltpu.make_async_remote_copy(
            src_ref=self.send.at[self.place(k)],
            dst_ref=self.recv.at[k - 1],
            send_sem=self.send_sem.at[k],
            recv_sem=self.recv_sem.at[k],
            device_id={"tensor": self.me ^ (1 << bit)},
            device_id_type=MESH,
        )

    def put(self, k, value):
        self.claim(k)[...] = value.astype(BF)
        if self.stage(k) == 0:
            self.launch(k)

    def total(self, k):
        value = self.send[self.place(k)].astype(F32)
        for bit in self.bits[: self.stage(k)]:
            self.copy(k | (1 << bit)).wait_recv()
            value = value + self.recv[(k | (1 << bit)) - 1].astype(F32)
        return value

    def forward(self, k):
        self.send[self.place(k)] = self.total(k).astype(BF)
        self.launch(k)

    def drain(self):
        for k in self.busy.values():
            self.copy(k).wait_send()
        self.busy = {}


def scatter_order(bits):
    n = 1 << len(bits)
    rank = lambda k: next(i for i, b in enumerate(bits) if k >> b & 1)
    return sorted(range(2, n, 2), key=lambda k: (rank(k), -k))


def attention_grads_kernel(a_ref, gm_ref, dq_ref, h_ref, dkv_ref, up_ref, after_ref, wo_ref, wq_ref, kv_ref, sum_ref,
                           send, recv, ksend, krecv, far, own, ssem, rsem, ksem, krsem, zsem, psem,
                           *, orders, line, qw):
    bits_of = [[0] + list(o)[::-1] for o in orders]
    count = len(bits_of[0])
    n = 1 << count
    half = gm_ref.shape[1] // 2
    greet(range(count), line)
    chain = Line(up_ref, sum_ref, far, zsem)
    pieces = up_ref.shape[0]
    if line:
        for i in range(pieces):
            chain.start(i)

    def own_piece(i):
        def value():
            c = pltpu.make_async_copy(up_ref.at[i], own, psem)
            c.start()
            c.wait()
            return own[...]

        return value

    ahead = [0]

    def chain_to(middles):
        while line and ahead[0] < min(middles, pieces):
            chain.middle(ahead[0], own_piece(ahead[0]))
            ahead[0] += 1
            if ahead[0] > 1:
                chain.back(ahead[0] - 2)

    kv = Scatter(bits_of[0], ksend, krecv, ksem, krsem)
    for k in list(range(1, n, 2)) + list(range(0, n, 2)):
        kv.put(k, dkv_ref[k])

    pairs = ((a_ref, gm_ref, wo_ref), (dq_ref, h_ref, wq_ref))
    work = [
        [Scatter(bits_of[p], send.at[m, p], recv.at[m, p], ssem.at[m, p], rsem.at[m, p], shared=2) for p in range(2)]
        for m in range(2)
    ]
    sequence = [scatter_order(b) for b in bits_of]

    def products(m):
        x, y, _ = pairs[m]
        for i in range(n // 2):
            for p in range(2):
                k = (sequence[p] + [0])[i]
                for j in (k + 1, k):
                    work[m][p].put(j, dot_tn(x[:, j * qw : (j + 1) * qw], y[:, p * half : (p + 1) * half]))

    def stage(m, i):
        for at in range(n // 2 - 1):
            for p in range(2):
                k = sequence[p][at]
                if work[m][p].stage(k) == i:
                    work[m][p].forward(k)

    def kv_stage(i):
        for k in scatter_order(bits_of[0]):
            if kv.stage(k) == i:
                kv.forward(k)

    def finish(m):
        for p in range(2):
            pairs[m][2][p] = work[m][p].total(0).astype(BF)

    products(0)
    stage(0, 1)
    chain_to(1)
    products(1)
    chain_to(3)
    for i in range(1, count):
        kv_stage(i)
        if i + 1 < count:
            stage(0, i + 1)
            chain_to(2 * i + 2)
        else:
            chain_to(7)
            finish(0)
            chain_to(8)
        stage(1, i)
    chain_to(10)
    kv_ref[...] = kv.total(0).astype(BF)
    chain_to(pieces)
    finish(1)
    if line:
        chain.back(pieces - 1)
        for i in range(pieces):
            chain.close(i)
    kv.drain()
    for m in range(2):
        for p in range(2):
            work[m][p].drain()


def attention_grads(a, gm, dq, h, dkv, up, early, orders):
    n, line = lax.axis_size("tensor"), lax.axis_size("dp") == 4
    tokens, d = gm.shape
    qw = a.shape[1] // n
    slot = dkv.shape[1:]
    rows, cols = up.shape
    pieces = rows // 128
    up = up.reshape(pieces, rows // pieces, cols)
    wait = up.shape if line else (1, 16, 128)
    dma = pltpu.SemaphoreType.DMA
    vmem, hbm = pl.BlockSpec(memory_space=pltpu.VMEM), pl.BlockSpec(memory_space=pl.ANY)
    wo, wq, kv, total = pl.pallas_call(
        functools.partial(attention_grads_kernel, orders=orders, line=line, qw=qw),
        in_specs=[vmem] * 5 + [hbm] * 2,
        out_specs=[vmem] * 4,
        out_shape=[
            jax.ShapeDtypeStruct((2, qw, d // 2), BF),
            jax.ShapeDtypeStruct((2, qw, d // 2), BF),
            jax.ShapeDtypeStruct(slot, BF),
            jax.ShapeDtypeStruct(wait, BF),
        ],
        scratch_shapes=[
            pltpu.VMEM((2, 2, n // 2 + 2, qw, d // 2), BF),
            pltpu.VMEM((2, 2, n - 1, qw, d // 2), BF),
            pltpu.VMEM((n,) + slot, BF),
            pltpu.VMEM((n - 1,) + slot, BF),
            pltpu.VMEM(wait, BF),
            pltpu.VMEM(up.shape[1:], BF),
            dma((2, 2, n)), dma((2, 2, n)), dma((n,)), dma((n,)), dma((2, 3, pieces)), dma,
        ],
        compiler_params=pltpu.CompilerParams(
            collective_id=1, has_side_effects=True, vmem_limit_bytes=60 * MIB
        ),
        cost_estimate=pl.CostEstimate(flops=1000, bytes_accessed=MIB, transcendentals=0),
    )(a, gm, dq, h, dkv, up, early)
    up = up.reshape(rows, cols)
    return wo, wq, kv, total.reshape(rows, cols) if line else lax.psum(up, "dp")


def last_kernel(wo_ref, wq_ref, dq_ref, kv_ref, shared_ref, h_ref, x_ref, gain_ref, mixed_ref, qb_ref, w_ref, *refs,
                order, line, eps_rows):
    count = len(order) + 1
    n = 1 << count
    (wog_ref, wqg_ref, grad_ref, late_ref, sg_ref,
     w_s, near, far, part, send, recv, dsend, drecv, piece_s, gathered, vsend, vrecv, esend, erecv,
     zsem, ssem, rsem, dsem, gsem, vsem, esem) = refs
    me, z = lax.axis_index("tensor"), lax.axis_index("dp")
    dp_bits = range(lax.axis_size("dp").bit_length() - 1)
    tokens, d = x_ref.shape
    hd = kv_ref.shape[1] // 2
    piece = d // n
    greet(range(count), line, dp_bits)

    pieces = wo_ref.shape[0]
    owns = (wo_ref, wq_ref)
    chains = []
    if line:
        for i, ref in enumerate(owns):
            chains.append(Line(ref, near.at[i], far.at[i], zsem.at[i]))
    ahead = [0, 0]

    def chain_to(middles):
        while line and ahead[1] < min(middles + 2, len(owns) * pieces):
            i, p = divmod(ahead[1], pieces)
            chains[i].start(p)
            ahead[1] += 1
        while line and ahead[0] < min(middles, len(owns) * pieces):
            i, p = divmod(ahead[0], pieces)
            chains[i].middle(p, lambda: owns[i][p])
            ahead[0] += 1
            if ahead[0] > 1:
                i, p = divmod(ahead[0] - 2, pieces)
                chains[i].back(p)

    chain_to(0)

    part[...] = dot_tn(h_ref[...], kv_ref[...])
    scatter = Scatter([0] + list(order)[::-1], send, recv, ssem, rsem)
    for k in list(range(1, n, 2)) + list(range(0, n, 2)):
        scatter.put(k, part[pl.ds(pl.multiple_of((me ^ k) * piece, piece), piece), :])
    for k in range(n):
        w_s[:, k * w_ref.shape[2] : (k + 1) * w_ref.shape[2]] = w_ref[k]
    hops = [("tensor", me, b) for b in range(count)] + [("dp", z, b) for b in dp_bits]
    pending = []

    def swap_start(buffers, sems, value, i, axis, at, bit):
        buffers[0][i] = value
        c = pltpu.make_async_remote_copy(
            src_ref=buffers[0].at[i], dst_ref=buffers[1].at[i], send_sem=sems.at[0, i], recv_sem=sems.at[1, i],
            device_id={axis: at ^ (1 << bit)}, device_id_type=MESH,
        )
        c.start()
        pending.append(c)
        return lambda value: (c.wait_recv(), value + buffers[1][i])[1]

    size = 2 * d + hd
    tail = late_ref.at[:, size:]
    front = late_ref.at[:, :size]
    early_done, last_done, piece_done = [None], [None], [None]

    def early(i):
        if early_done[0] is not None:
            tail[...] = early_done[0](tail[...])
            early_done[0] = None
        if i < len(hops):
            early_done[0] = swap_start((esend, erecv), esem, tail[...], i, *hops[i])

    def late(i):
        if last_done[0] is not None:
            front[...] = last_done[0](front[...])
            last_done[0] = None
        if i < len(hops):
            last_done[0] = swap_start((vsend, vrecv), vsem, front[...], i, *hops[i])

    def shared_sum(i):
        if piece_done[0] is not None:
            piece_s[...] = piece_done[0](piece_s[...])
            piece_done[0] = None
        if i < len(dp_bits):
            piece_done[0] = swap_start((dsend, drecv), dsem, piece_s[...], i, "dp", z, dp_bits[i])

    tail[...] = qb_ref[...]
    early(0)
    at = 1
    chain_to(at)
    for i in range(1, count):
        for k in scatter_order(scatter.bits):
            if scatter.stage(k) == i:
                scatter.forward(k)
        early(i)
        at += 1
        chain_to(at)
    piece_s[...] = scatter.total(0)
    shared_sum(0)

    gain_part, shift_part = jnp.zeros((1, d), F32), jnp.zeros((1, d), F32)
    for t in range(tokens // eps_rows):
        rows = slice(t * eps_rows, (t + 1) * eps_rows)
        grad = dot_nt(dq_ref[rows], w_s[...]) + dot_nt(kv_ref[rows], shared_ref[...])
        unit, scale = norm_parts(x_ref[rows].astype(F32))
        e = gain_ref[...] * grad
        back = e - jnp.mean(e, axis=-1, keepdims=True) - unit * jnp.mean(e * unit, axis=-1, keepdims=True)
        grad_ref[rows] = mixed_ref[rows] + scale * back
        gain_part += jnp.sum(grad * unit, axis=0, keepdims=True)
        shift_part += jnp.sum(grad, axis=0, keepdims=True)
        if t + 1 < len(dp_bits):
            shared_sum(t + 1)
        if count + t < len(hops):
            early(count + t)
        at += 1
        chain_to(at)
    late_ref[:, :d] = gain_part
    late_ref[:, d : 2 * d] = shift_part
    late_ref[:, 2 * d : size] = jnp.sum(kv_ref[:, hd:].astype(F32), axis=0, keepdims=True)
    late(0)
    for i in range(max(tokens // eps_rows + 1, 1), len(dp_bits) + 1):
        shared_sum(i)
    shared_sum(len(dp_bits))
    for i in range(count + tokens // eps_rows, len(hops) + 1):
        early(i)
    early(len(hops))
    gathered[me] = piece_s[...].astype(BF)
    sent, held, step = [], [0], 0
    for bit in list(order) + [0]:
        new = []
        for k in held:
            c = pltpu.make_async_remote_copy(
                src_ref=gathered.at[me ^ k], dst_ref=gathered.at[me ^ k], send_sem=gsem.at[0, k | (1 << bit)],
                recv_sem=gsem.at[1, k | (1 << bit)], device_id={"tensor": me ^ (1 << bit)}, device_id_type=MESH,
            )
            c.start()
            sent.append(c)
            new.append(c)
        step += 1
        late(step)
        at += 1
        chain_to(at)
        for c in new:
            c.wait_recv()
        held = held + [k | (1 << bit) for k in held]
    while step < len(hops):
        step += 1
        late(step)
        at += 1
        chain_to(at)
    chain_to(len(owns) * pieces)
    if line:
        chains[-1].back(pieces - 1)
    for k in range(n):
        sg_ref[k * piece : (k + 1) * piece] = gathered[k].astype(F32)
    if line:
        for c in chains:
            for p in range(pieces):
                c.close(p)
    half, high = d // 2, wo_ref.shape[1]
    for j in range(pieces):
        values = [near[i, j] if line else owns[i][j] for i in range(len(owns))]
        p, q = divmod(j, pieces // 2)
        for ref, value in zip((wog_ref, wqg_ref), values):
            ref[q * high : (q + 1) * high, p * half : (p + 1) * half] = value.astype(F32)
    for c in pending + sent:
        c.wait_send()
    scatter.drain()


def last(wo, wq, dq, kv, shared, h, x, gain, mixed, qb, w, order):
    n, dp = lax.axis_size("tensor"), lax.axis_size("dp")
    line = dp == 4
    tokens, d = x.shape
    qw = wo.shape[1]
    cuts = 4
    wo, wq = (v.reshape(cuts, -1, d // 2) for v in (wo, wq))
    piece, width = d // n, kv.shape[1]
    size = 2 * d + qb.shape[1] + width // 2
    bits = n.bit_length() - 1
    dbits = dp.bit_length() - 1
    dma = pltpu.SemaphoreType.DMA
    vmem = pl.BlockSpec(memory_space=pltpu.VMEM)
    item = (2,) + wo.shape
    return pl.pallas_call(
        functools.partial(last_kernel, order=order, line=line, eps_rows=tokens // 4),
        in_specs=[vmem] * 11,
        out_specs=[vmem] * 5,
        out_shape=[
            jax.ShapeDtypeStruct((qw, d), F32),
            jax.ShapeDtypeStruct((qw, d), F32),
            jax.ShapeDtypeStruct((tokens, d), F32),
            jax.ShapeDtypeStruct((1, size), F32),
            jax.ShapeDtypeStruct((d, width), F32),
        ],
        scratch_shapes=[
            pltpu.VMEM((d, n * qw), BF),
            pltpu.VMEM(item, BF),
            pltpu.VMEM(item, BF),
            pltpu.VMEM((d, width), F32),
            pltpu.VMEM((n, piece, width), BF),
            pltpu.VMEM((n - 1, piece, width), BF),
            pltpu.VMEM((dbits, piece, width), F32),
            pltpu.VMEM((dbits, piece, width), F32),
            pltpu.VMEM((piece, width), F32),
            pltpu.VMEM((n, piece, width), BF),
            pltpu.VMEM((bits + dbits, 1, size - qb.shape[1]), F32),
            pltpu.VMEM((bits + dbits, 1, size - qb.shape[1]), F32),
            pltpu.VMEM((bits + dbits,) + qb.shape, F32),
            pltpu.VMEM((bits + dbits,) + qb.shape, F32),
            dma((2, 2, 3, cuts)), dma((n,)), dma((n,)), dma((2, dbits)), dma((2, n)), dma((2, bits + dbits)), dma((2, bits + dbits)),
        ],
        compiler_params=pltpu.CompilerParams(
            collective_id=4, has_side_effects=True, vmem_limit_bytes=60 * MIB
        ),
        cost_estimate=pl.CostEstimate(flops=1000, bytes_accessed=MIB, transcendentals=0),
    )(wo, wq, dq, kv, shared, h, x, gain, mixed, qb, w)


class Gather:
    def __init__(self, orders, refs, send_sem, recv_sem):
        self.paths = [list(o) + [0] for o in orders]
        self.refs, self.send_sem, self.recv_sem = refs, send_sem, recv_sem
        self.me = lax.axis_index("tensor")
        self.n = 1 << len(self.paths[0])
        self.sent = []

    def last_bit(self, p, k):
        return max((b for b in self.paths[p] if k >> b & 1), key=self.paths[p].index)

    def copies(self, p, k, bit):
        to = k | (1 << bit)
        return [
            pltpu.make_async_remote_copy(
                src_ref=ref(p, k), dst_ref=ref(p, to), send_sem=self.send_sem.at[i, p, to],
                recv_sem=self.recv_sem.at[i, p, to], device_id={"tensor": self.me ^ (1 << bit)}, device_id_type=MESH,
            )
            for i, ref in enumerate(self.refs)
        ]

    def hop(self, p, k, bit):
        for c in self.copies(p, k, bit):
            c.start()
            self.sent.append(c)

    def arrived(self, p, k):
        bit = self.last_bit(p, k)
        for c in self.copies(p, k ^ (1 << bit), bit):
            c.wait_recv()

    def at_step(self, p, t):
        if t == 0:
            return [0]
        return sorted((k for k in range(2, self.n, 2) if self.last_bit(p, k) == self.paths[p][t - 1]), reverse=True)

    def drain(self):
        for c in self.sent:
            c.wait_send()


def first_kernel(x_ref, gain_ref, shift_ref, shared_ref, vb_ref, wq_ref, bq_ref, h_ref, k_ref, kt_ref, v_ref, vt_ref,
                 w_ref, q_ref, kv_ref, bias, send_sem, recv_sem, *, orders, factor, rows):
    n, d, qw = w_ref.shape
    seqs, span = kv_ref.shape[1:3]
    hd = vb_ref.shape[1]
    half = d // 2
    tokens = x_ref.shape[0]
    greet(range(len(orders[0]) + 1))
    weights = Gather(
        orders, [lambda p, k: w_ref.at[k, p * half : (p + 1) * half], lambda p, k: bias.at[p, k]],
        send_sem.at[0], recv_sem.at[0],
    )
    shared = Gather(orders, [lambda p, k: kv_ref.at[k, p]], send_sem.at[1], recv_sem.at[1])
    steps = len(weights.paths[0])
    w_ref[0] = wq_ref[...]
    for p in range(2):
        bias[p, 0] = bq_ref[...]
    for p in range(2):
        weights.hop(p, 0, weights.paths[p][0])
    for p in range(2):
        weights.hop(p, 0, 0)
    for t in range(tokens // rows):
        here = slice(t * rows, (t + 1) * rows)
        unit, _ = norm_parts(x_ref[here].astype(F32))
        h_ref[here] = (unit * gain_ref[...] + shift_ref[...]).astype(BF)
    kv = dot(h_ref[...], shared_ref[...])
    for r in range(seqs):
        here = slice(r * span, (r + 1) * span)
        kv_ref[0, r, :, :hd] = kv[here, :hd].astype(BF)
        kv_ref[0, r, :, hd:] = (kv[here, hd:] + vb_ref[...]).astype(BF)
    for p in range(2):
        shared.hop(p, 0, shared.paths[p][0])
    for p in range(2):
        shared.hop(p, 0, 0)

    def product(k):
        q_ref[:, k * qw : (k + 1) * qw] = ((dot(h_ref[...], w_ref[k]) + bias[0, k]) * factor).astype(BF)

    product(0)
    ready = [1]
    for t in range(1, steps):
        for g in (weights, shared):
            for p in range(2):
                for k in g.at_step(p, t):
                    g.arrived(p, k)
                    if t < steps - 1:
                        g.hop(p, k, g.paths[p][t])
                    g.hop(p, k, 0)
            if t < steps - 1:
                for p in range(2):
                    for before in range(t - 1, -1, -1):
                        for k in g.at_step(p, before):
                            g.hop(p, k, g.paths[p][t])
    for k in range(n):
        here = slice(k * span, (k + 1) * span)
        for r in range(seqs):
            if k % 2:
                shared.arrived(r, k)
            block = kv_ref[k, r]
            k_ref[r, here, :] = block[:, :hd]
            v_ref[r, here, :] = block[:, hd:]
            kt_ref[r, :, here] = block[:, :hd].T
            vt_ref[r, :, here] = block[:, hd:].T
    for k in range(1, n, 2):
        for p in range(2):
            weights.arrived(p, k)
        product(k)
        if k > 1:
            product(k - 1)
    weights.drain()
    shared.drain()


def first(x, gain, shift, shared, vb, wq, bq, seqs, factor, orders):
    n = lax.axis_size("tensor")
    tokens, d = x.shape
    qw, hd = wq.shape[1], vb.shape[1]
    span = tokens // seqs
    plain = jax.ShapeDtypeStruct((seqs, n * span, hd), BF)
    turned = jax.ShapeDtypeStruct((seqs, hd, n * span), BF)
    dma = pltpu.SemaphoreType.DMA
    vmem = pl.BlockSpec(memory_space=pltpu.VMEM)
    return pl.pallas_call(
        functools.partial(first_kernel, orders=orders, factor=factor, rows=tokens // 4),
        in_specs=[vmem] * 7,
        out_specs=[vmem] * 7,
        out_shape=[
            jax.ShapeDtypeStruct((tokens, d), BF),
            plain, turned, plain, turned,
            jax.ShapeDtypeStruct((n, d, qw), BF),
            jax.ShapeDtypeStruct((tokens, n * qw), BF),
        ],
        scratch_shapes=[
            pltpu.VMEM((n, seqs, span, 2 * hd), BF),
            pltpu.VMEM((2, n, 1, qw), F32),
            dma((2, 2, 2, n)), dma((2, 2, 2, n)),
        ],
        compiler_params=pltpu.CompilerParams(collective_id=5, has_side_effects=True, vmem_limit_bytes=48 * MIB),
        cost_estimate=pl.CostEstimate(
            flops=2 * tokens * d * n * qw, bytes_accessed=64 * MIB, transcendentals=0
        ),
    )(x, gain, shift, shared, vb, wq, bq)


def mlp_kernel(x_ref, cot_ref, up_ref, bias_ref, down_ref, gn_ref, gb_ref, xg_ref, act_ref, gr_ref, *rest, orders):
    n, seqs, span, d = cot_ref.shape
    (ff_ref, down_grad_ref, x_s, c_s, act_s, gr_s, ff_s, send, recv, a_s, acc,
     gsend, grecv, ssem, rsem, load, own, out, aload, gout) = rest
    hidden = up_ref.shape[1]
    tile, wide = min(512, hidden), 512
    me = lax.axis_index("tensor")
    paths = [list(o) + [0] for o in orders]
    bits_of = [[0] + list(o)[::-1] for o in orders]
    work = [Scatter(bits_of[p], send.at[p], recv.at[p], ssem.at[p], rsem.at[p], shared=2) for p in range(seqs)]

    def last_bit(p, k):
        return max((b for b in paths[p] if k >> b & 1), key=paths[p].index)

    def hop(p, k, bit):
        to = k | (1 << bit)
        src = x_ref.at[p] if k == 0 else xg_ref.at[me ^ k, p]
        return pltpu.make_async_remote_copy(
            src_ref=src, dst_ref=xg_ref.at[me ^ k, p], send_sem=gsend.at[p, to], recv_sem=grecv.at[p, to],
            device_id={"tensor": me ^ (1 << bit)}, device_id_type=MESH,
        )

    def arrival(p, k):
        bit = last_bit(p, k)
        return pltpu.make_async_remote_copy(
            src_ref=x_ref.at[p], dst_ref=xg_ref.at[me ^ k, p], send_sem=gsend.at[p, k], recv_sem=grecv.at[p, k],
            device_id={"tensor": me ^ (1 << bit)}, device_id_type=MESH,
        )

    def slots_at(p, t):
        if t == 0:
            return [0]
        return sorted((k for k in range(2, n, 2) if last_bit(p, k) == paths[p][t - 1]), reverse=True)

    steps = len(paths[0])
    units = [(p, k) for t in range(steps) for i in range(len(slots_at(0, t))) for p in range(seqs) for k in [slots_at(p, t)[i]]]

    def cot_loads(u):
        p, e = units[u]
        return [
            pltpu.make_async_copy(
                cot_ref.at[me ^ (e + j), p], c_s.at[u % 2, j * span : (j + 1) * span], load.at[u % 2, j]
            )
            for j in range(2)
        ]

    def x_loads(u):
        p, e = units[u]
        return [
            pltpu.make_async_copy(
                x_ref.at[p] if e + j == 0 else xg_ref.at[me ^ (e + j), p],
                x_s.at[j * span : (j + 1) * span], load.at[2, j],
            )
            for j in range(2)
        ]

    def hidden_stores(u):
        p, e = units[u]
        return [
            pltpu.make_async_copy(
                buf.at[j * span : (j + 1) * span], ref.at[me ^ (e + j), p], out.at[i, j]
            )
            for i, (buf, ref) in enumerate(((act_s, act_ref), (gr_s, gr_ref)))
            for j in range(2)
        ]

    def ff_stores(u):
        p, e = units[u]
        return [
            pltpu.make_async_copy(ff_s.at[j * span : (j + 1) * span], ff_ref.at[p, e + j], out.at[2, j])
            for j in range(2)
        ]

    waiting = []

    def run(u):
        p, e = units[u]
        for j in range(2):
            if e + j and (e + j) % 2 == 1:
                arrival(p, e + j).wait_recv()
        for c in x_loads(u):
            c.start()
        if u + 1 < len(units):
            for c in cot_loads(u + 1):
                c.start()
        if u:
            for c in hidden_stores(u - 1):
                c.wait()
        for c in x_loads(u) + cot_loads(u):
            c.wait()

        @pl.loop(0, hidden // tile)
        def _(i):
            here = pl.ds(pl.multiple_of(i * tile, tile), tile)
            raised = dot(x_s[...], up_ref[:, here]) + bias_ref[:, here]
            square = raised * raised
            th = jnp.tanh(0.7978845608028654 * raised * (1.0 + 0.044715 * square))
            act_s[:, here] = (0.5 * raised * (1.0 + th)).astype(BF)
            slope = 0.5 * (1.0 + th) + 0.5 * raised * (1.0 - th * th) * (
                0.7978845608028654 * (1.0 + 3 * 0.044715 * square)
            )
            gr = (dot_nt(c_s[u % 2], down_ref[here, :]) * slope).astype(BF)
            gr_s[:, here] = gr
            gb = jnp.sum(gr.astype(F32), axis=0, keepdims=True)
            gb_ref[:, here] = gb if u == 0 else gb_ref[:, here] + gb

        for c in hidden_stores(u):
            c.start()
        while waiting:
            q, k = waiting.pop(0)
            work[q].forward(k)
        if u:
            for c in ff_stores(u - 1):
                c.wait()
        odd, even = work[p].claim(e + 1), work[p].claim(e)

        @pl.loop(0, d // wide)
        def _(i):
            here = pl.ds(pl.multiple_of(i * wide, wide), wide)
            gn = dot_nt(gr_s[...], up_ref[here, :]).astype(BF)
            even[:, here] = gn[:span]
            odd[:, here] = gn[span:]
            ff_s[:, here] = dot(act_s[...], down_ref[:, here]).astype(BF)

        work[p].launch(e + 1)
        for c in ff_stores(u):
            c.start()

    keep = [pltpu.make_async_copy(x_ref.at[p], xg_ref.at[me, p], own.at[p]) for p in range(seqs)]
    greet(range(steps))
    for p in range(seqs):
        hop(p, 0, paths[p][0]).start()
    for p in range(seqs):
        hop(p, 0, 0).start()
        keep[p].start()
    for c in cot_loads(0):
        c.start()
    sent = [(p, 0, b) for p in range(seqs) for b in (paths[p][0], 0)]
    u = 0
    for t in range(steps):
        while u < len(units) and units[u][1] in slots_at(units[u][0], t):
            if t and units[u][0] == 0:
                for p in range(seqs):
                    k = units[u + p][1]
                    arrival(p, k).wait_recv()
                    if t < steps - 1:
                        hop(p, k, paths[p][t]).start()
                        sent.append((p, k, paths[p][t]))
                    hop(p, k, 0).start()
                    sent.append((p, k, 0))
            run(u)
            p, k = units[u]
            if work[p].stage(k) == 1:
                waiting.append((p, k))
            u += 1
        if 0 < t < steps - 1:
            for p in range(seqs):
                for before in range(t - 1, -1, -1):
                    for k in slots_at(p, before):
                        hop(p, k, paths[p][t]).start()
                        sent.append((p, k, paths[p][t]))
    for p, k in waiting:
        work[p].forward(k)
    for c in hidden_stores(len(units) - 1) + ff_stores(len(units) - 1):
        c.wait()

    strip = a_s.shape[2]
    strips = hidden // strip

    def grad_loads(q, j, slot):
        return [
            c
            for r in range(seqs)
            for c in (
                pltpu.make_async_copy(
                    act_ref.at[j, r, :, q * strip : (q + 1) * strip], a_s.at[slot, r * span : (r + 1) * span],
                    aload.at[slot, r],
                ),
                pltpu.make_async_copy(
                    cot_ref.at[j, r], c_s.at[slot, r * span : (r + 1) * span], load.at[slot, r]
                ),
            )
        ]

    def grad_store(q):
        return pltpu.make_async_copy(
            ff_s.at[:strip], down_grad_ref.at[q * strip : (q + 1) * strip], gout
        )

    def grad_strip(q):
        for c in grad_loads(q, 0, 0):
            c.start()

        @pl.loop(0, n)
        def _(j):
            slot = lax.rem(j, 2)

            @pl.when(j + 1 < n)
            def _():
                for c in grad_loads(q, j + 1, 1 - slot):
                    c.start()

            for c in grad_loads(q, j, slot):
                c.wait()
            term = dot_tn(a_s[slot], c_s[slot])

            @pl.when(j == 0)
            def _():
                acc[...] = term

            @pl.when(j > 0)
            def _():
                acc[...] += term

        if q:
            grad_store(q - 1).wait()
        ff_s[:strip] = acc[...].astype(BF)
        grad_store(q).start()

    for q in range(strips // 2):
        grad_strip(q)
    for i in range(2, steps):
        for at in range(n // 2 - 1):
            for p in range(seqs):
                k = scatter_order(bits_of[p])[at]
                if work[p].stage(k) == i:
                    work[p].forward(k)
    for q in range(strips // 2, strips):
        grad_strip(q)
    grad_store(strips - 1).wait()
    for p in range(seqs):
        gn_ref[p] = work[p].total(0)
    for c in keep:
        c.wait()
    for p, k, b in sent:
        hop(p, k, b).wait_send()
    for p in range(seqs):
        work[p].drain()


def mlp(normed, cot, up, bias, down, orders):
    n, seqs, span, d = cot.shape
    ff = up.shape[1]
    strip = min(2 * span, ff // 2, 256)
    dma = pltpu.SemaphoreType.DMA
    hbm, vmem = pl.BlockSpec(memory_space=pl.ANY), pl.BlockSpec(memory_space=pltpu.VMEM)
    return pl.pallas_call(
        functools.partial(mlp_kernel, orders=orders),
        in_specs=[hbm, hbm, vmem, vmem, vmem],
        out_specs=[vmem, vmem, hbm, hbm, hbm, hbm, hbm],
        out_shape=[
            jax.ShapeDtypeStruct((seqs, span, d), F32),
            jax.ShapeDtypeStruct((1, ff), F32),
            jax.ShapeDtypeStruct((n, seqs, span, d), BF),
            jax.ShapeDtypeStruct((n, seqs, span, ff), BF),
            jax.ShapeDtypeStruct((n, seqs, span, ff), BF),
            jax.ShapeDtypeStruct((seqs, n, span, d), BF),
            jax.ShapeDtypeStruct((ff, d), BF),
        ],
        scratch_shapes=[
            pltpu.VMEM((2 * span, d), BF),
            pltpu.VMEM((2, 2 * span, d), BF),
            pltpu.VMEM((2 * span, ff), BF),
            pltpu.VMEM((2 * span, ff), BF),
            pltpu.VMEM((2 * span, d), BF),
            pltpu.VMEM((seqs, n // 2 + 2, span, d), BF),
            pltpu.VMEM((seqs, n - 1, span, d), BF),
            pltpu.VMEM((2, seqs * span, strip), BF),
            pltpu.VMEM((strip, d), F32),
            dma((seqs, n)), dma((seqs, n)), dma((seqs, n)), dma((seqs, n)), dma((3, 2)), dma((seqs,)), dma((3, 2)),
            dma((2, seqs)), dma,
        ],
        compiler_params=pltpu.CompilerParams(collective_id=2, has_side_effects=True, vmem_limit_bytes=60 * MIB),
        cost_estimate=pl.CostEstimate(
            flops=8 * n * seqs * span * d * ff, bytes_accessed=100 * MIB, transcendentals=n * seqs * span * ff
        ),
    )(normed, cot, up, bias, down)


class ScatterParts(Scatter):
    def copy(self, k):
        if self.stage(k):
            return super().copy(k)
        return pltpu.make_async_remote_copy(
            src_ref=self.source.at[k],
            dst_ref=self.recv.at[k - 1],
            send_sem=self.send_sem.at[k],
            recv_sem=self.recv_sem.at[k],
            device_id={"tensor": self.me ^ (1 << self.bits[0])},
            device_id_type=MESH,
        )

    def place(self, k):
        return k // 2 if k % 2 == 0 else -k


def mlp_grads_kernel(gr_ref, x_ref, part_ref, mixed_ref, bias_ref, after_ref, up_ref, ff_ref,
                     a_s, b_s, acc, send, recv, ssem, rsem, load, own, *, orders):
    seqs, n = part_ref.shape[:2]
    bits_of = [[0] + list(o)[::-1] for o in orders]
    work = []
    for p in range(seqs):
        w = ScatterParts(bits_of[p], send.at[p], recv.at[p], ssem.at[p], rsem.at[p])
        w.source = part_ref.at[p]
        work.append(w)
    evens = [
        pltpu.make_async_copy(part_ref.at[p, k], send.at[p, k // 2], own.at[p, k // 2])
        for p in range(seqs) for k in range(0, n, 2)
    ]
    wide = acc.shape[0]
    tile = min(256, wide)
    steps = n

    def loads(u):
        return [
            pltpu.make_async_copy(x_ref.at[u], a_s.at[u % 2], load.at[u % 2, 0]),
            pltpu.make_async_copy(gr_ref.at[u], b_s.at[u % 2], load.at[u % 2, 1]),
        ]

    greet(range(len(bits_of[0])))
    for k in range(n - 1, 0, -2):
        for p in range(seqs):
            work[p].launch(k)
    for c in loads(0) + evens:
        c.start()

    def forwards(i):
        for at in range(n // 2 - 1):
            for p in range(seqs):
                k = scatter_order(bits_of[p])[at]
                if work[p].stage(k) == i:
                    work[p].forward(k)

    stages = len(bits_of[0])
    when = {(i - 1) * (steps // (stages - 1)) + 1: i for i in range(1, stages)} if stages > 1 else {}
    when = {min(u + 2 * (i - 1), steps - 1): i for u, i in when.items()}
    for u in range(steps):
        if u + 1 < steps:
            for c in loads(u + 1):
                c.start()
        for c in loads(u):
            c.wait()

        @pl.loop(0, wide // tile)
        def _(i, u=u):
            here = pl.ds(pl.multiple_of(i * tile, tile), tile)
            term = dot_tn(a_s[u % 2, :, here], b_s[u % 2])
            if u == 0:
                acc[here, :] = term
            elif u < n - 1:
                acc[here, :] += term
            else:
                up_ref[here, :] = (acc[here, :] + term).astype(BF)

        if u == 0:
            for c in evens:
                c.wait()
        if u in when:
            forwards(when[u])
    for p in range(seqs):
        ff_ref[p] = (mixed_ref[p] + work[p].total(0) + bias_ref[...]).astype(BF)
        work[p].drain()


def mlp_grads(gr, x, parts, mixed, bias, early, orders):
    seqs, n, span, d = parts.shape
    tokens, cols = seqs * span, gr.shape[-1]
    dma = pltpu.SemaphoreType.DMA
    hbm, vmem = pl.BlockSpec(memory_space=pl.ANY), pl.BlockSpec(memory_space=pltpu.VMEM)
    flat = lambda v: v.reshape(n, tokens, v.shape[-1])
    return pl.pallas_call(
        functools.partial(mlp_grads_kernel, orders=orders),
        in_specs=[hbm] * 3 + [vmem] * 2 + [hbm],
        out_specs=[vmem] * 2,
        out_shape=[
            jax.ShapeDtypeStruct((d, cols), BF),
            jax.ShapeDtypeStruct((seqs, span, d), BF),
        ],
        scratch_shapes=[
            pltpu.VMEM((2, tokens, d), BF),
            pltpu.VMEM((2, tokens, cols), BF),
            pltpu.VMEM((d, cols), F32),
            pltpu.VMEM((seqs, n // 2, span, d), BF),
            pltpu.VMEM((seqs, n - 1, span, d), BF),
            dma((seqs, n)), dma((seqs, n)), dma((2, 2)), dma((seqs, n // 2)),
        ],
        compiler_params=pltpu.CompilerParams(collective_id=3, has_side_effects=True, vmem_limit_bytes=60 * MIB),
        cost_estimate=pl.CostEstimate(flops=1000, bytes_accessed=MIB, transcendentals=0),
    )(flat(gr), flat(x), parts, mixed, bias, early)


def norm_parts(values):
    center = values - jnp.mean(values, axis=-1, keepdims=True)
    scale = lax.rsqrt(jnp.mean(center * center, axis=-1, keepdims=True) + EPSILON)
    return center * scale, scale


def norm_back(unit, scale, gain, grad):
    e = gain * grad
    back = scale * (e - jnp.mean(e, axis=-1, keepdims=True) - unit * jnp.mean(e * unit, axis=-1, keepdims=True))
    return back, jnp.sum(grad * unit, axis=(0, 1)), jnp.sum(grad, axis=(0, 1))


def body(
    inputs, cotangent, documents, padding, attn_gain, attn_shift, query_matrix, query_bias, shared_matrix,
    value_bias, output_matrix, output_bias, mlp_gain, mlp_shift, expansion_weights, up_bias, down_matrix, down_bias,
):
    n = lax.axis_size("tensor")
    me = lax.axis_index("tensor")
    hd = value_bias.shape[0]
    seqs, span, d = inputs.shape
    length = documents.shape[1]
    qw = query_matrix.shape[1]
    heads = qw // hd
    scale = hd**-0.5
    paths = bit_orders(n)
    tokens = seqs * span
    ff = up_bias.shape[0]

    x32 = inputs.astype(F32)
    output_every = lax.all_gather(output_matrix, "tensor")
    cot_every = lax.all_gather(cotangent, "tensor")
    h2, keys, keys_t, values, values_t, wq, query = first(
        inputs.reshape(tokens, d), attn_gain[None], attn_shift[None], shared_matrix, value_bias[None], query_matrix,
        query_bias[None], seqs, scale * LOG2E, paths,
    )
    query = query.reshape(seqs, span, n * qw)
    like = lambda t, cols: jax.ShapeDtypeStruct((tokens, cols), t)

    begin = lax.dynamic_slice_in_dim(documents, me * span, 1, 1)
    low = (jnp.sum((documents < begin).astype(jnp.int32), axis=1) // span).astype(jnp.int32)
    low = jnp.minimum(low, me)
    at = me.reshape(1).astype(jnp.int32)
    dock = jnp.where(padding == 1, documents, -1)
    dock = xor_order(dock.reshape(seqs, n, span).swapaxes(0, 1), me).swapaxes(0, 1).reshape(seqs, length, 1)
    docq = lax.dynamic_slice_in_dim(documents, me * span, span, 1)
    docq = jnp.concatenate([docq] * heads, axis=1)[:, None, :]
    attended, lse = attention_fwd(query, keys, values_t, low, at, dock, docq, heads, hd)
    a2 = attended.reshape(tokens, n * qw)
    mixed, normed = slot_product(
        o_kernel, [a2, inputs.reshape(tokens, d)], output_every, [output_bias[None], mlp_gain[None], mlp_shift[None]],
        [like(F32, d), like(BF, d)],
    )
    mixed, normed = mixed.reshape(seqs, span, d), normed.reshape(seqs, span, d)
    unit2, scale2 = norm_parts(mixed)

    grad_normed, up_bias_part, normed_every, acts, grs, ff_parts, down_part = mlp(
        normed, cot_every, expansion_weights, up_bias[None], down_matrix, paths
    )
    down_gradient = lax.psum(down_part, "dp")

    cot_wide = cotangent.astype(F32)
    back2, mlp_gain_part, mlp_shift_part = norm_back(unit2, scale2, mlp_gain, grad_normed)
    grad_mixed = cot_wide + back2
    gm2 = grad_mixed.astype(BF).reshape(tokens, d)
    (grad_attended,) = slot_product(do_kernel, [gm2], output_every, [], [like(BF, n * qw)])
    grad_attended = grad_attended.reshape(seqs, span, n * qw)
    dq, dk, dv = attention_bwd(
        query, grad_attended, attended, lse, keys, keys_t, values, low, at, dock, docq, heads, hd, scale
    )
    dq2 = dq.reshape(tokens, n * qw)
    up_part, block_out = mlp_grads(grs, normed_every, ff_parts, mixed, down_bias[None], dq2, paths)

    dkv = jnp.concatenate([dk * LN2, dv], axis=-1).astype(BF).reshape(seqs, n, span, 2 * hd).swapaxes(0, 1)
    wo_own, wq_own, dkv_own, up_gradient = attention_grads(
        a2, gm2, dq2, h2, dkv.reshape(n, tokens, 2 * hd), up_part, down_gradient, paths
    )
    query_bias_part = xor_order(jnp.sum(dq2.astype(F32), axis=0).reshape(n, qw), me).reshape(-1)
    up_bias_every = lax.dynamic_update_slice_in_dim(jnp.zeros((n * ff,), F32), up_bias_part[0], me * ff, 0)
    vector = jnp.concatenate(
        [query_bias_part, mlp_gain_part, mlp_shift_part, jnp.sum(grad_mixed, axis=(0, 1)),
         jnp.sum(cot_wide, axis=(0, 1)), up_bias_every]
    )[None]
    output_gradient, query_gradient, input_grad, late, shared_grad = last(
        wo_own, wq_own, dq2, dkv_own, shared_matrix, h2, inputs.reshape(tokens, d), attn_gain[None],
        grad_mixed.reshape(tokens, d), vector, wq, paths[0],
    )
    input_grad = input_grad.reshape(seqs, span, d)
    if lax.axis_size("dp") != 4:
        output_gradient, query_gradient = (
            g.astype(F32) for g in lax.psum((output_gradient.astype(BF), query_gradient.astype(BF)), "dp")
        )
    late = late[0]
    ends = [d, 2 * d, 2 * d + hd, 2 * d + hd + n * qw]
    ends += [ends[-1] + d * (i + 1) for i in range(4)]
    (attn_gain_grad, attn_shift_grad, value_bias_grad, query_bias_all, mlp_gain_grad, mlp_shift_grad,
     output_bias_grad, down_bias_grad, up_bias_all) = jnp.split(late, ends)
    query_bias_grad = lax.dynamic_slice_in_dim(query_bias_all, me * qw, qw, 0)
    up_bias_grad = lax.dynamic_slice_in_dim(up_bias_all, me * ff, ff, 0)
    query_gradient, up_gradient, down_gradient = query_gradient.T, up_gradient.astype(F32), down_gradient.astype(F32)
    return (
        block_out, input_grad, attn_gain_grad, attn_shift_grad, query_gradient, query_bias_grad, shared_grad,
        value_bias_grad, output_gradient, output_bias_grad, mlp_gain_grad, mlp_shift_grad, up_gradient, up_bias_grad,
        down_gradient, down_bias_grad,
    )


def solution(mesh):
    act = P("dp", "tensor", None)
    cols, rows, vec, rep = P(None, "tensor"), P("tensor", None), P("tensor"), P()
    ids = P("dp", None)
    return jax.shard_map(
        body,
        mesh=mesh,
        in_specs=(act, act, ids, ids, rep, rep, cols, vec, rep, rep, rows, rep, rep, rep, cols, vec, rows, rep),
        out_specs=(act, act, rep, rep, cols, vec, rep, rep, rows, rep, rep, rep, cols, vec, rows, rep),
        check_vma=False,
    )
```
